32 devices in a mesh: dp: 8 (over y, x, core), mp: 4 (over z).
Axes of the slice: x: 2, y: 2, z: 4, core: 2. Of those that a mesh axis runs over, the one named last changes fastest.
Arguments:
- block_input: bfloat16 [4096, 2048], P('dp'), may hold values from -6 to 6
- cotangent: bfloat16 [4096, 2048], P('dp'), may hold values from -6 to 6
- doc_lengths: int32 [1, 8], replicated, may hold values from 1 to 2048, 4096 in all within a row
- span_order: int32 [32], replicated, may hold values from 0 to 31, as said below
- weights: float32 [2048, 24576], P('dp', 'mp'), may hold values from -0.125 to 0.125
- momentum: float32 [2048, 24576], P('dp', 'mp'), may hold values from -0.001953125 to 0.001953125
- ema_weights: float32 [2048, 24576], P('dp', 'mp'), may hold values from -0.125 to 0.125
- gains: float32 [4352], replicated, may hold values from 0.7 to 7.2, as said below
- gain_momentum: float32 [4352], replicated, may hold values from -0.0078125 to 0.0078125
- gain_ema: float32 [4352], replicated, may hold values from 0.5 to 1.5
Outputs:
- block_output: bfloat16 [4096, 2048], P('dp')
- grad_input: float32 [4096, 2048], P('dp')
- grad_norm: float32 [], replicated
- new_weights: float32 [2048, 24576], P('dp', 'mp')
- new_momentum: float32 [2048, 24576], P('dp', 'mp')
- new_ema: float32 [2048, 24576], P('dp', 'mp')
- new_gains: float32 [4352], replicated
- new_gain_momentum: float32 [4352], replicated
- new_gain_ema: float32 [4352], replicated
The draws below stay inside these ranges and needn't reach their ends.
Inputs may be any that keep to these rules, and one draw needn't show every extreme that they name: `doc_lengths`: each row sums to 4096; the longest document of each row has 2048 tokens. A permutation of the 32 spans; storage span i holds span span_order[i] of the unpermuted order. Positive gains.
All inputs are finite; a program needn't handle non-finite values.
Results may differ from the reference program's by a relative error of at most 0.035.
Values may be sent and summed in bfloat16 or wider, within the bound.
No kernel may reach another device: no remote copies, remote signals or barrier semaphores. Data moves between devices by JAX's collectives and lax.ppermute only.
A program may use at most 256 MiB of HBM per device.

```python
import math
import jax
import jax.numpy as jnp
import numpy as np
from jax import lax

D = 2048
HEADS = 16
KV = 8
HD = 128
TOK_DEV = 512
SPAN = 128
NDOC = 8
TOKENS = 4096
SEQ = 4096
SEQS = 1
NSPAN = 32
Q_DEV = 512
KV_DEV = 256
FF_DEV = 1536
WALL = 24576
GAINS = 4352
N_MP = 4


def shuffle_row(subkey_row):
    return jax.random.permutation(subkey_row, NSPAN // (TOK_DEV // SPAN))


def draw_span_order(key, part):
    per_device = TOK_DEV // SPAN
    device_count = NSPAN // per_device
    per_sequence = SEQ // SPAN
    row_keys = jax.random.split(jax.random.fold_in(key, 11), per_device)
    shuffled = jax.vmap(shuffle_row)(row_keys).astype(jnp.int32)
    slots = jnp.arange(per_device, dtype=jnp.int32)[:, None] * device_count + shuffled
    ordered = jnp.transpose(slots).reshape(NSPAN)
    seq_shuffle = jax.random.permutation(jax.random.fold_in(key, 13), SEQS).astype(jnp.int32)
    return (seq_shuffle[ordered // per_sequence] * per_sequence + ordered % per_sequence).astype(jnp.int32)


def draw_gains(key, part):
    ramp_top = 3.0
    ramp = 1.0 + (ramp_top - 1.0) * jnp.arange(D, dtype=jnp.float32) / (D - 1)
    factors = jnp.exp(jax.random.uniform(jax.random.fold_in(key, 3), (2, D), minval=-0.35, maxval=0.35))
    norm_gains = (ramp[None, :] * factors).reshape(2 * D)
    head_gains = jax.random.uniform(jax.random.fold_in(key, 5), (2 * HD,), minval=0.8, maxval=1.25)
    return jnp.concatenate([norm_gains, head_gains]).astype(jnp.float32)


def level_of(own_key, shape, cuts, smallest, high):
    factor_of = 1.0
    for axis_at, blocks in cuts:
        draws = jax.random.uniform(jax.random.fold_in(jax.random.fold_in(own_key, 6), axis_at), (blocks,), jnp.float32, smallest / len(cuts), high / len(cuts))
        factor_of = factor_of * jnp.repeat(jnp.exp(draws), shape[axis_at] // blocks).reshape((-1,) + (1,) * (len(shape) - 1 - axis_at))
    return factor_of


def split_up(amount, total, reach, slope):
    loads = [(1 << 20) // math.isqrt(rank ** slope) + 1 for rank in range(2, amount + 1)]
    surplus, given = total - reach - (amount - 1), [1] * (amount - 1)
    while surplus > 0:
        candidates = [i for i in range(amount - 1) if given[i] < reach]
        mass, left = sum([loads[i] for i in candidates]), surplus
        for i in candidates:
            extra = min(reach - given[i], max(1, left * loads[i] // mass), surplus)
            given[i] = given[i] + extra
            surplus = surplus - extra
    return np.array([reach] + given)


def ragged_sizes(key, count, total, most, lean):
    if count == 2:
        one = jax.random.randint(key, (), max(1, total - most), min(most, total - 1) + 1)
        return jnp.stack([one, total - one])
    tallies = jnp.asarray(split_up(count, total, most, lean), jnp.int32)
    pairs = (count - 1) // 2
    giver, receiver = tallies[1:1 + 2 * pairs:2], tallies[2:2 + 2 * pairs:2]
    slack = jnp.minimum(giver - 1, most - receiver)
    passed = jax.random.randint(jax.random.fold_in(key, 1), (pairs,), 0, 1 << 20) % (slack + 1)
    tallies = tallies.at[1:1 + 2 * pairs:2].set(giver - passed).at[2:2 + 2 * pairs:2].set(receiver + passed)
    return tallies[jax.random.permutation(jax.random.fold_in(key, 2), count)]


def noise(own_key, shape, scale, limit, shards=(), kind=jnp.bfloat16):
    drawn = scale * jax.random.normal(own_key, shape, jnp.float32)
    if shards:
        drawn = drawn * level_of(own_key, shape, shards, -0.22, 0.18)
    return jnp.clip(drawn, -limit, limit).astype(kind)


def setup_inputs(seed: int = 0) -> dict:
    splits = jax.random.split(jax.random.key(seed), 11)
    block_input = noise(splits[0], (TOKENS, D), 1.0, 6.0, ((0, 8),))
    cotangent = noise(splits[1], (TOKENS, D), 1.0, 6.0, ((0, 8),))
    doc_lengths = jax.vmap(lambda own: ragged_sizes(own, NDOC, SEQ, SEQ // 2, 2))(jax.random.split(splits[2], SEQS)).reshape((SEQS, NDOC)).astype(jnp.int32)
    span_order = draw_span_order(jax.random.fold_in(splits[10], 71), 0)
    weights = noise(splits[4], (D, WALL), D ** -0.5, 0.125, ((0, 8), (1, 4)), jnp.float32)
    momentum = noise(splits[5], (D, WALL), ((D * WALL) ** -0.5), 0.001953125, ((0, 8), (1, 4)), jnp.float32)
    ema_weights = noise(splits[6], (D, WALL), D ** -0.5, 0.125, ((0, 8), (1, 4)), jnp.float32)
    gains = draw_gains(jax.random.fold_in(splits[10], 71), 0)
    gain_momentum = noise(splits[8], (GAINS,), (4 * (D * WALL) ** -0.5), 0.0078125, (), jnp.float32)
    gain_ema = jnp.clip(1.0 + 0.1 * jax.random.normal(splits[9], (GAINS,), jnp.float32), 0.5, 1.5)
    return {"block_input": block_input, "cotangent": cotangent, "doc_lengths": doc_lengths, "span_order": span_order, "weights": weights, "momentum": momentum, "ema_weights": ema_weights, "gains": gains, "gain_momentum": gain_momentum, "gain_ema": gain_ema}


eps_norm = 1e-06
rope_base = 1000000.0
learn_rate = 100.0
gain_rate = 4000.0
momentum_decay = 0.5
average_decay = 0.5
highest = lax.Precision.HIGHEST

@jax.custom_vjp
def low(v):
    return lax.optimization_barrier(v.astype(jnp.bfloat16)).astype(jnp.float32)

@jax.custom_vjp
def low_back(v):
    return v

def low_keep(v):
    return (low(v), None)

def low_pass(kept, grad):
    return (grad,)

def back_keep(v):
    return (v, None)

def back_low(kept, grad):
    return (low(grad),)
low.defvjp(low_keep, low_pass)
low_back.defvjp(back_keep, back_low)

def rms_scale(values, weight_gain):
    return values * lax.rsqrt(lax.optimization_barrier(jnp.mean(values * values, axis=-1, keepdims=True)) + eps_norm) * weight_gain

def rotate(values, angles):
    half_size = values.shape[-1] // 2
    cosine = jnp.cos(angles)
    sine = jnp.sin(angles)
    first_half = values[..., :half_size]
    second_half = values[..., half_size:]
    return jnp.concatenate([first_half * cosine - second_half * sine, second_half * cosine + first_half * sine], axis=-1)

def doc_places(lengths_row, seq_tokens):
    starts = jnp.cumsum(lengths_row) - lengths_row
    position = jnp.arange(seq_tokens, dtype=jnp.int32)
    started = position[:, None] >= starts[None, :]
    doc_index = lax.optimization_barrier(jnp.sum(started.astype(jnp.int32), axis=1))
    doc_start = lax.optimization_barrier(jnp.max(jnp.where(started, starts[None, :], 0), axis=1))
    return (doc_index, position - doc_start)

def layer(inputs, params, doc_index, in_doc):
    w_query, w_key, w_value, w_out, w_gate, w_up, w_down, gain_attn, gain_mlp, gain_query, gain_key = params
    seq_tokens = inputs.shape[0]
    score_scale = HD ** (-0.5)
    normed = low(rms_scale(inputs, gain_attn))
    queries = low_back(jnp.dot(normed, w_query, precision=highest, preferred_element_type=jnp.float32)).reshape(seq_tokens, HEADS, HD)
    keys_lin = low_back(jnp.dot(normed, w_key, precision=highest, preferred_element_type=jnp.float32)).reshape(seq_tokens, KV, HD)
    values = low(low_back(jnp.dot(normed, w_value, precision=highest, preferred_element_type=jnp.float32))).reshape(seq_tokens, KV, HD)
    freqs = rope_base ** (-(2.0 * jnp.arange(HD // 2, dtype=jnp.float32)) / HD)
    angles = (in_doc.astype(jnp.float32)[:, None] * freqs[None, :])[:, None, :]
    queries = low(rotate(rms_scale(queries, gain_query), angles))
    keys_rot = low(rotate(rms_scale(keys_lin, gain_key), angles))
    keys_wide = jnp.repeat(keys_rot, HEADS // KV, axis=1)
    values_wide = jnp.repeat(values, HEADS // KV, axis=1)
    block_rows = min(512, seq_tokens)
    position = jnp.arange(seq_tokens, dtype=jnp.int32)

    def attend(items):
        query_block, block_doc, block_place = items
        scores = low_back(jnp.einsum('qhd,khd->hqk', query_block, keys_wide, precision=highest) * score_scale)
        allowed = (block_doc[:, None] == doc_index[None, :]) & (position[None, :] <= block_place[:, None])
        scores = jnp.where(allowed[None], scores, -1e+30)
        probs = low(jax.nn.softmax(scores, axis=-1))
        return jnp.einsum('hqk,khd->qhd', probs, values_wide, precision=highest)
    attended = lax.map(jax.checkpoint(attend), (queries.reshape(seq_tokens // block_rows, block_rows, HEADS, HD), doc_index.reshape(-1, block_rows), position.reshape(-1, block_rows)))
    attended = low(low_back(attended.reshape(seq_tokens, HEADS * HD)))
    residual = inputs + low_back(jnp.dot(attended, w_out.T, precision=highest, preferred_element_type=jnp.float32))
    normed_mlp = low(rms_scale(residual, gain_mlp))
    gate_value = low_back(jnp.dot(normed_mlp, w_gate, precision=highest, preferred_element_type=jnp.float32))
    up_value = low_back(jnp.dot(normed_mlp, w_up, precision=highest, preferred_element_type=jnp.float32))
    hidden = low(jax.nn.silu(gate_value) * up_value)
    return residual + low_back(jnp.dot(hidden, w_down.T, precision=highest, preferred_element_type=jnp.float32))

def unpack(packed, widths):
    blocks = packed.reshape(packed.shape[0], N_MP, -1)
    pieces = []
    begin = 0
    for part_width in widths:
        pieces.append(blocks[:, :, begin:begin + part_width].reshape(packed.shape[0], N_MP * part_width))
        begin += part_width
    return pieces

def pack(pieces, widths):
    blocks = [piece.reshape(piece.shape[0], N_MP, part_width) for piece, part_width in zip(pieces, widths)]
    return jnp.concatenate(blocks, axis=2).reshape(pieces[0].shape[0], -1)

def update(value, state, average, gradient, factor, step_rate):
    clipped = gradient * factor
    state_new = momentum_decay * state + clipped
    value_new = value - step_rate * (clipped + momentum_decay * state_new)
    average_new = average_decay * average + (1.0 - average_decay) * value_new
    return (value_new, state_new, average_new)

def reference(block_input, cotangent, doc_lengths, span_order, weights, momentum, ema_weights, gains, gain_momentum, gain_ema):
    widths = [Q_DEV, KV_DEV, KV_DEV, Q_DEV, FF_DEV, FF_DEV, FF_DEV]
    inverse = jnp.zeros((NSPAN,), jnp.int32).at[span_order].set(jnp.arange(NSPAN, dtype=jnp.int32))

    def to_sequence(array):
        return array.reshape(NSPAN, SPAN, D)[inverse].reshape(SEQS, SEQ, D).astype(jnp.float32)

    def to_storage(array):
        return array.reshape(NSPAN, SPAN, D)[span_order].reshape(TOKENS, D)
    inputs = to_sequence(block_input)
    backward = to_sequence(cotangent)
    matrices = unpack(weights, widths)
    gain_parts = [gains[:D], gains[D:2 * D], gains[2 * D:2 * D + HD], gains[2 * D + HD:]]
    params = tuple(matrices) + tuple(gain_parts)

    def one_sequence(running, items):
        seq_input, seq_back, lengths_row = items
        doc_index, in_doc = doc_places(lengths_row, SEQ)

        def forward(layer_input, layer_params):
            return layer(layer_input, layer_params, doc_index, in_doc)
        outputs, pullback = jax.vjp(forward, seq_input, params)
        grad_in, grad_params = pullback(seq_back)
        return (jax.tree.map(jnp.add, running, grad_params), (outputs, grad_in))
    zeros = jax.tree.map(jnp.zeros_like, params)
    grads, (outputs, grad_inputs) = lax.scan(one_sequence, zeros, (inputs, backward, doc_lengths))
    grad_matrix = pack(list(grads[:7]), widths)
    grad_gain = jnp.concatenate(list(grads[7:]))
    grad_norm = jnp.sqrt(jnp.sum(grad_matrix * grad_matrix) + jnp.sum(grad_gain * grad_gain))
    factor = 1.0 / jnp.maximum(grad_norm, 1.0)
    new_weights, new_momentum, new_ema = update(weights, momentum, ema_weights, grad_matrix, factor, learn_rate)
    new_gains, new_gain_momentum, new_gain_ema = update(gains, gain_momentum, gain_ema, grad_gain, factor, gain_rate)
    return (to_storage(outputs).astype(jnp.bfloat16), to_storage(grad_inputs), grad_norm, new_weights, new_momentum, new_ema, new_gains, new_gain_momentum, new_gain_ema)
```

```python
import functools

import jax
import jax.numpy as jnp
from jax import lax
from jax.experimental import pallas as pl
from jax.experimental.pallas import tpu as pltpu
from jax.sharding import PartitionSpec as P

HEADS = 16
KV = 8
HD = 128
FF = 6144
SPAN = 128
CHUNK = 4
TILE = 256
VMEM_LIMIT = 60 * 1024 * 1024

eps_norm = 1e-06
rope_base = 1000000.0
learn_rate = 100.0
gain_rate = 4000.0
momentum_decay = 0.5
average_decay = 0.5
score_scale = HD ** (-0.5)
far = -1e30

bf16 = jnp.bfloat16
f32 = jnp.float32
last_dims = (((1,), (1,)), ((), ()))
first_dims = (((0,), (0,)), ((), ()))


def dot(a, b, dims=(((1,), (0,)), ((), ()))):
    return lax.dot_general(a, b, dims, preferred_element_type=f32)


def params(**more):
    return pltpu.CompilerParams(vmem_limit_bytes=VMEM_LIMIT, **more)


def swap(array, axis, distance):
    count = lax.axis_size(axis)
    return lax.ppermute(array, axis, [(i, i ^ distance) for i in range(count)])


def gather_blocks(own):
    outer = [own] + [swap(own, "dp", k) for k in (2, 4, 6)]
    inner = [swap(block, "dp", 1) for block in outer]
    return [block for pair in zip(outer, inner) for block in pair]


def scatter_blocks(even, odd):
    came = swap(odd, "dp", 1)
    half = (even.astype(f32) + came.astype(f32)).astype(bf16)
    parts = [swap(half[k], "dp", 2 * k) for k in (1, 2, 3)]
    total = half[0].astype(f32)
    for part in parts:
        total = total + part.astype(f32)
    return total


def sum_all(value):
    for axis in ("dp", "mp"):
        distance = 1
        while distance < lax.axis_size(axis):
            value = value + swap(value, axis, distance)
            distance *= 2
    return value


def project_kernel(part_count, q_heads, kv_heads, *refs):
    h_ref = refs[0]
    w_refs = refs[1 : 1 + part_count]
    cos_ref, sin_ref, gq_ref, gk_ref, q_ref, kv_ref, lin_ref = refs[1 + part_count :]
    depth = w_refs[0].shape[0]
    cosine = cos_ref[...]
    sine = sin_ref[...]

    def columns(begin):
        total = None
        for k, w_ref in enumerate(w_refs):
            term = dot(h_ref[:, k * depth : (k + 1) * depth], w_ref[:, begin : begin + TILE])
            total = term if total is None else total + term
        return total

    def turned(head, gain):
        scale = lax.rsqrt(jnp.mean(head * head, axis=1, keepdims=True) + eps_norm)
        normed = head * scale * gain
        return normed * cosine + pltpu.roll(normed, HD // 2, 1) * sine

    per_tile = TILE // HD
    for tile in range((q_heads + 2 * kv_heads) // per_tile):
        block = columns(tile * TILE)
        for part in range(per_tile):
            head = tile * per_tile + part
            values = block[:, part * HD : (part + 1) * HD]
            if head < q_heads:
                lin_ref[:, head * HD : (head + 1) * HD] = values
                q_ref[:, head * HD : (head + 1) * HD] = turned(values, gq_ref[...]).astype(bf16)
            elif head < q_heads + kv_heads:
                place = 2 * (head - q_heads) * HD
                lin_ref[:, head * HD : (head + 1) * HD] = values
                kv_ref[:, place : place + HD] = turned(values, gk_ref[...]).astype(bf16)
            else:
                place = (2 * (head - q_heads - kv_heads) + 1) * HD
                kv_ref[:, place : place + HD] = values.astype(bf16)


def span_limits(own_ref, starts_ref, i):
    span = own_ref[i]
    first = span * SPAN
    rows = first + lax.broadcasted_iota(jnp.int32, (SPAN, 1), 0)
    low = jnp.int32(0)
    begin = jnp.zeros((SPAN, 1), jnp.int32)
    for d in range(starts_ref.shape[0]):
        start = starts_ref[d]
        low = jnp.maximum(low, jnp.where(start <= first, start, 0))
        begin = jnp.maximum(begin, jnp.where(start <= rows, start, 0))
    return span, low // SPAN, rows, begin


def key_rows(inverse_ref, newest, b):
    return pl.multiple_of(inverse_ref[jnp.maximum(newest - b, 0)] * SPAN, SPAN)


def allowed_keys(newest, rows, begin):
    lane = lax.broadcasted_iota(jnp.int32, (1, CHUNK * SPAN), 1)
    place = newest * SPAN + (lane & (SPAN - 1)) - (lane & ~(SPAN - 1))
    return (place <= rows) & (place >= begin)


def stacked(ref, i, group):
    rows = pl.ds(i * SPAN, SPAN)
    return jnp.concatenate([ref[rows, h * HD : (h + 1) * HD] for h in range(group)], axis=0)


def attend_kernel(group, own_ref, inverse_ref, starts_ref, q_ref, kv_ref, o_ref, low_ref, lse_ref, s_ref):
    for i in range(own_ref.shape[0]):
        span, low, rows, begin = span_limits(own_ref, starts_ref, i)
        rows = jnp.concatenate([rows] * group, axis=0)
        begin = jnp.concatenate([begin] * group, axis=0)
        query = stacked(q_ref, i, group)
        count = (span - low) // CHUNK + 1

        def score(c, top):
            newest = span - c * CHUNK
            keys = jnp.concatenate(
                [kv_ref[pl.ds(key_rows(inverse_ref, newest, b), SPAN), :HD] for b in range(CHUNK)], axis=0
            )
            scores = dot(query, keys, last_dims) * score_scale
            scores = jnp.where(allowed_keys(newest, rows, begin), scores, far)
            s_ref[c] = scores
            for b in range(CHUNK):
                top = jnp.maximum(top, scores[:, b * SPAN : (b + 1) * SPAN])
            return top

        top = lax.fori_loop(0, count, score, jnp.full((group * SPAN, SPAN), far, f32))
        top = jnp.max(top, axis=1, keepdims=True)

        def weigh(c, carry):
            weight, total = carry
            newest = span - c * CHUNK
            values = jnp.concatenate(
                [kv_ref[pl.ds(key_rows(inverse_ref, newest, b), SPAN), HD:] for b in range(CHUNK)], axis=0
            )
            probs = jnp.exp(s_ref[c] - top)
            for b in range(CHUNK):
                weight = weight + probs[:, b * SPAN : (b + 1) * SPAN]
            return weight, total + dot(probs.astype(bf16), values)

        zeros = jnp.zeros((group * SPAN, SPAN), f32)
        weight, total = lax.fori_loop(0, count, weigh, (zeros, jnp.zeros((group * SPAN, HD), f32)))
        weight = jnp.sum(weight, axis=1, keepdims=True)
        output = total / weight
        lse = jnp.broadcast_to(top + jnp.log(weight), output.shape)
        place = pl.ds(i * SPAN, SPAN)
        for h in range(group):
            o_ref[place, h * HD : (h + 1) * HD] = output[h * SPAN : (h + 1) * SPAN]
            low_ref[place, h * HD : (h + 1) * HD] = output[h * SPAN : (h + 1) * SPAN].astype(bf16)
            lse_ref[place, h * HD : (h + 1) * HD] = lse[h * SPAN : (h + 1) * SPAN]


def attend_back_kernel(
    group, own_ref, inverse_ref, starts_ref, place_ref, q_ref, kv_ref, do_ref, o_ref, lse_ref, dq_ref, dkv_ref, acc_ref
):
    acc_ref[...] = jnp.zeros_like(acc_ref)
    for i in range(own_ref.shape[0]):
        span, low, rows, begin = span_limits(own_ref, starts_ref, i)
        rows = jnp.concatenate([rows] * group, axis=0)
        begin = jnp.concatenate([begin] * group, axis=0)
        query = stacked(q_ref, i, group)
        grad = stacked(do_ref, i, group)
        delta = jnp.sum(grad.astype(f32) * stacked(o_ref, i, group), axis=1, keepdims=True)
        lse = stacked(lse_ref, i, group)[:, :1]
        count = (span - low) // CHUNK + 1

        def step(c, grad_query):
            newest = span - c * CHUNK
            at = [key_rows(inverse_ref, newest, b) for b in range(CHUNK)]
            both = jnp.concatenate([kv_ref[pl.ds(a, SPAN), :] for a in at], axis=0)
            keys, values = both[:, :HD], both[:, HD:]
            scores = dot(query, keys, last_dims) * score_scale
            probs = jnp.exp(jnp.where(allowed_keys(newest, rows, begin), scores - lse, far))
            grad_probs = dot(grad, values, last_dims)
            grad_scores = (probs * (grad_probs - delta)).astype(bf16)
            grad_keys = dot(grad_scores, query, first_dims) * score_scale
            grad_values = dot(probs.astype(bf16), grad, first_dims)
            for b, a in enumerate(at):
                acc_ref[pl.ds(a, SPAN), :HD] += grad_keys[b * SPAN : (b + 1) * SPAN]
                acc_ref[pl.ds(a, SPAN), HD:] += grad_values[b * SPAN : (b + 1) * SPAN]
            return grad_query + dot(grad_scores, keys)

        grad_query = lax.fori_loop(0, count, step, jnp.zeros((group * SPAN, HD), f32)) * score_scale
        for h in range(group):
            dq_ref[pl.ds(i * SPAN, SPAN), h * HD : (h + 1) * HD] = grad_query[h * SPAN : (h + 1) * SPAN]

    def put(t, unused):
        source = pl.multiple_of(t * SPAN, SPAN)
        target = pl.multiple_of(place_ref[t] * SPAN, SPAN)
        dkv_ref[pl.ds(target, SPAN), :] = acc_ref[pl.ds(source, SPAN), :].astype(bf16)
        return unused

    lax.fori_loop(0, place_ref.shape[0], put, 0)


def mlp_kernel(h_ref, c_ref, wg_ref, wu_ref, wd_ref, dg_ref, du_ref, a_ref, dh_ref, acc_ref):
    step = pl.program_id(0)
    hidden = h_ref[...]
    gate = dot(hidden, wg_ref[...])
    up = dot(hidden, wu_ref[...])
    grad = dot(c_ref[...], wd_ref[...])
    sig = 1.0 / (1.0 + jnp.exp(-gate))
    silu = gate * sig
    a_ref[...] = (silu * up).astype(bf16)
    grad_gate = (grad * up * (sig + silu * (1.0 - sig))).astype(bf16)
    grad_up = (grad * silu).astype(bf16)
    dg_ref[...] = grad_gate
    du_ref[...] = grad_up
    term = dot(grad_gate, wg_ref[...], last_dims) + dot(grad_up, wu_ref[...], last_dims)

    @pl.when(step == 0)
    def _():
        acc_ref[...] = term

    @pl.when(step > 0)
    def _():
        acc_ref[...] += term

    @pl.when(step == pl.num_programs(0) - 1)
    def _():
        dh_ref[...] = acc_ref[...].astype(bf16)


def unit_scale(values):
    return lax.rsqrt(jnp.mean(values * values, axis=-1, keepdims=True) + eps_norm)


def norm_back(unit, scale, gain, gradient):
    e = gradient * gain
    return scale * (e - unit * jnp.mean(e * unit, axis=-1, keepdims=True))


def head_back(lin, gain, gradient, cosine, sine):
    tokens = lin.shape[0]
    lin = lin.reshape(tokens, -1, HD)
    gradient = gradient.reshape(tokens, -1, HD)
    turned = gradient * sine[:, None, :]
    half = HD // 2
    turned = jnp.concatenate([turned[..., half:], turned[..., :half]], axis=-1)
    grad_normed = gradient * cosine[:, None, :] + turned
    scale = unit_scale(lin)
    unit = lin * scale
    grad_gain = jnp.sum(grad_normed * unit, axis=(0, 1))
    return norm_back(unit, scale, gain, grad_normed).reshape(tokens, -1).astype(bf16), grad_gain


def update(value, state, average, gradient, factor, step_rate):
    clipped = gradient * factor
    state_new = momentum_decay * state + clipped
    value_new = value - step_rate * (clipped + momentum_decay * state_new)
    average_new = average_decay * average + (1.0 - average_decay) * value_new
    return (value_new, state_new, average_new)


def per_device(
    block_input,
    cotangent,
    doc_lengths,
    span_order,
    weights,
    momentum,
    ema_weights,
    gains,
    gain_momentum,
    gain_ema,
):
    tok_count, model_width = block_input.shape
    data_count = lax.axis_size("dp")
    model_count = lax.axis_size("mp")
    me = lax.axis_index("dp")
    row_count = weights.shape[0]
    token_total = tok_count * data_count
    span_total = token_total // SPAN
    span_own = tok_count // SPAN
    seq_len = token_total // doc_lengths.shape[0]
    doc_total = doc_lengths.shape[0] * doc_lengths.shape[1]
    q_heads = HEADS // model_count
    kv_heads = KV // model_count
    group = q_heads // kv_heads
    query_width = q_heads * HD
    kv_width = kv_heads * HD
    ff_width = FF // model_count
    qkv_cols = query_width + 2 * kv_width
    out_end = qkv_cols + query_width
    in_pairs = data_count == 8
    gain_attn = gains[:model_width]
    gain_mlp = gains[model_width : 2 * model_width]
    gain_query = gains[2 * model_width : 2 * model_width + HD]
    gain_key = gains[2 * model_width + HD :]

    doc_ids = jnp.arange(doc_lengths.shape[1], dtype=jnp.int32)
    earlier = doc_ids[None, :] < doc_ids[:, None]
    starts = jnp.sum(jnp.where(earlier[None], doc_lengths[:, None, :], 0), axis=2)
    starts = starts + seq_len * jnp.arange(doc_lengths.shape[0], dtype=jnp.int32)[:, None]
    starts = starts.reshape(doc_total)
    span_ids = jnp.arange(span_total, dtype=jnp.int32)
    inverse = jnp.sum(jnp.where(span_order[None, :] == span_ids[:, None], span_ids[None, :], 0), axis=1)
    own_spans = lax.dynamic_slice(span_order, (me * span_own,), (span_own,))
    home = (own_spans[:, None] * SPAN + jnp.arange(SPAN, dtype=jnp.int32)[None, :]).reshape(tok_count)
    doc_start = jnp.max(jnp.where(starts[None, :] <= home[:, None], starts[None, :], 0), axis=1)
    freqs = rope_base ** (-(2.0 * jnp.arange(HD // 2, dtype=f32)) / HD)
    angles = (home - doc_start).astype(f32)[:, None] * freqs[None, :]
    cosine = jnp.tile(jnp.cos(angles), (1, 2))
    sine_half = jnp.sin(angles)
    sine = jnp.concatenate([-sine_half, sine_half], axis=1)

    qkv_own = weights[:, :qkv_cols].astype(bf16)
    out_own = weights[:, qkv_cols:out_end].astype(bf16)
    mlp_own = weights[:, out_end:].astype(bf16)
    inputs = block_input.astype(f32)
    scale_in = unit_scale(inputs)
    unit_in = inputs * scale_in
    normed_low = (unit_in * gain_attn).astype(bf16)

    if in_pairs:
        order = [me ^ k for k in range(data_count)]

        def reordered(array):
            return jnp.concatenate(
                [lax.dynamic_slice(array, (0, b * row_count), (array.shape[0], row_count)) for b in order], axis=1
            )

        qkv_parts = gather_blocks(qkv_own)
        normed_low = reordered(normed_low)
        out_parts = gather_blocks(out_own)
        mlp_own, qkv_parts = lax.optimization_barrier((mlp_own, qkv_parts))
    else:

        def reordered(array):
            return array

        qkv_parts = [lax.all_gather(qkv_own, "dp", axis=0, tiled=True)]
        out_parts = [lax.all_gather(out_own, "dp", axis=0, tiled=True)]
    mlp_weights = lax.all_gather(mlp_own, "dp", axis=0, tiled=True)
    qkv_weights = jnp.concatenate(qkv_parts, axis=0)
    out_weights = jnp.concatenate(out_parts, axis=0)

    queries, keys_values, lin = pl.pallas_call(
        functools.partial(project_kernel, len(qkv_parts), q_heads, kv_heads),
        out_shape=(
            jax.ShapeDtypeStruct((tok_count, query_width), bf16),
            jax.ShapeDtypeStruct((tok_count, 2 * kv_width), bf16),
            jax.ShapeDtypeStruct((tok_count, query_width + kv_width), f32),
        ),
        compiler_params=params(),
        name="project",
    )(normed_low, *qkv_parts, cosine, sine, gain_query[None], gain_key[None])

    if in_pairs:
        kv_parts = gather_blocks(keys_values)
        kv_all = jnp.concatenate(kv_parts, axis=0)
        kv_inverse = ((inverse // span_own) ^ me) * span_own + inverse % span_own
        kv_place = ((span_ids // span_own) >> 1) * span_own + span_ids % span_own
        kv_place = kv_place + jnp.where(((span_ids // span_own) & 1) == 1, span_total // 2, 0)
    else:
        kv_all = lax.all_gather(keys_values, "dp", axis=0, tiled=True)
        kv_inverse = inverse
        kv_place = span_ids

    wide = group * HD
    q_spec = pl.BlockSpec((tok_count, wide), lambda g, *_: (0, g))
    kv_spec = pl.BlockSpec((token_total, 2 * HD), lambda g, *_: (0, g))
    attended, attended_low, lse = pl.pallas_call(
        functools.partial(attend_kernel, group),
        grid_spec=pltpu.PrefetchScalarGridSpec(
            num_scalar_prefetch=3,
            grid=(kv_heads,),
            in_specs=[q_spec, kv_spec],
            out_specs=[q_spec, q_spec, q_spec],
            scratch_shapes=[pltpu.VMEM((seq_len // (CHUNK * SPAN) + 1, group * SPAN, CHUNK * SPAN), f32)],
        ),
        out_shape=(
            jax.ShapeDtypeStruct((tok_count, query_width), f32),
            jax.ShapeDtypeStruct((tok_count, query_width), bf16),
            jax.ShapeDtypeStruct((tok_count, query_width), f32),
        ),
        compiler_params=params(),
        name="attend",
    )(own_spans, kv_inverse, starts, queries, kv_all)

    attn_part = dot(attended_low, out_weights, last_dims).astype(bf16)
    attn_sum = lax.psum(attn_part, "mp").astype(f32)
    inputs_there = reordered(block_input).astype(f32)
    residual = inputs_there + attn_sum
    gain_mlp_there = reordered(gain_mlp[None])[0]
    scale_mlp = unit_scale(residual)
    unit_mlp = residual * scale_mlp
    mlp_low_there = (unit_mlp * gain_mlp_there).astype(bf16)

    def restored(array):
        return reordered(array)

    mlp_low = restored(mlp_low_there)

    tiles = ff_width // TILE
    rows_spec = pl.BlockSpec((tok_count, model_width), lambda n: (0, 0))
    tile_spec = pl.BlockSpec((tok_count, TILE), lambda n: (0, n))
    hidden_shape = jax.ShapeDtypeStruct((tok_count, ff_width), bf16)
    grad_gate, grad_up, hidden_low, grad_mlp_part = pl.pallas_call(
        mlp_kernel,
        grid=(tiles,),
        in_specs=[
            rows_spec,
            rows_spec,
            pl.BlockSpec((model_width, TILE), lambda n: (0, n)),
            pl.BlockSpec((model_width, TILE), lambda n: (0, n + tiles)),
            pl.BlockSpec((model_width, TILE), lambda n: (0, n + 2 * tiles)),
        ],
        out_specs=[tile_spec, tile_spec, tile_spec, rows_spec],
        out_shape=(hidden_shape, hidden_shape, hidden_shape, jax.ShapeDtypeStruct((tok_count, model_width), bf16)),
        scratch_shapes=[pltpu.VMEM((tok_count, model_width), f32)],
        compiler_params=params(),
        name="mlp",
    )(mlp_low, cotangent, mlp_weights, mlp_weights, mlp_weights)

    grad_mlp_full = lax.psum(grad_mlp_part, "mp").astype(f32)
    mlp_part = dot(hidden_low, mlp_weights[:, 2 * ff_width :], last_dims).astype(bf16)
    mlp_part, grad_mlp_full = lax.optimization_barrier((mlp_part, grad_mlp_full))
    mlp_sum = lax.psum(mlp_part, "mp").astype(f32)
    block_output = (restored(residual) + mlp_sum).astype(bf16)

    unit_mlp_here = restored(unit_mlp)
    mlp_gain_grad = jnp.sum(grad_mlp_part.astype(f32) * unit_mlp_here, axis=0)
    grad_residual = cotangent.astype(f32) + norm_back(unit_mlp_here, scale_mlp, gain_mlp, grad_mlp_full)
    grad_res_low = grad_residual.astype(bf16)
    grad_res_there = reordered(grad_res_low)
    grad_att_low = dot(grad_res_there, out_weights).astype(bf16)

    grad_queries, grad_kv = pl.pallas_call(
        functools.partial(attend_back_kernel, group),
        grid_spec=pltpu.PrefetchScalarGridSpec(
            num_scalar_prefetch=4,
            grid=(kv_heads,),
            in_specs=[q_spec, kv_spec, q_spec, q_spec, q_spec],
            out_specs=[q_spec, kv_spec],
            scratch_shapes=[pltpu.VMEM((token_total, 2 * HD), f32)],
        ),
        out_shape=(
            jax.ShapeDtypeStruct((tok_count, query_width), f32),
            jax.ShapeDtypeStruct((token_total, 2 * kv_width), bf16),
        ),
        compiler_params=params(),
        name="attend_back",
    )(own_spans, kv_inverse, starts, kv_place, queries, kv_all, grad_att_low, attended, lse)

    if in_pairs:
        halves = grad_kv.reshape(2, data_count // 2, tok_count, 2 * kv_width)
        grad_kv_mine = scatter_blocks(halves[0], halves[1])
    else:
        grad_kv_mine = lax.psum_scatter(grad_kv, "dp", scatter_dimension=0, tiled=True).astype(f32)
    grad_kv_mine = grad_kv_mine.reshape(tok_count, kv_heads, 2, HD)
    grad_query_low, grad_gain_query = head_back(lin[:, :query_width], gain_query, grad_queries, cosine, sine)
    grad_key_low, grad_gain_key = head_back(lin[:, query_width:], gain_key, grad_kv_mine[:, :, 0], cosine, sine)
    grad_qkv_low = jnp.concatenate(
        [grad_query_low, grad_key_low, grad_kv_mine[:, :, 1].reshape(tok_count, kv_width).astype(bf16)], axis=1
    )

    grad_norm_part = dot(grad_qkv_low, qkv_weights, last_dims).astype(bf16)
    unit_there = reordered(unit_in)
    gain_attn_there = reordered(gain_attn[None])[0]
    attn_gain_grad = restored(jnp.sum(grad_norm_part.astype(f32) * unit_there, axis=0, keepdims=True))[0]
    grad_norm_full = lax.psum(grad_norm_part, "mp").astype(f32)
    grad_input = grad_residual + restored(norm_back(unit_there, scale_in, gain_attn_there, grad_norm_full))

    grad_gate_up = jnp.concatenate([grad_gate, grad_up], axis=1)
    dw_down = dot(cotangent, hidden_low, first_dims).astype(bf16)
    dw_gate_up = dot(mlp_low, grad_gate_up, first_dims).astype(bf16)
    dw_qkv = dot(normed_low, grad_qkv_low, first_dims).astype(bf16)
    dw_out = dot(grad_res_there, attended_low, first_dims).astype(bf16)

    def scattered(array):
        return lax.psum_scatter(array, "dp", scatter_dimension=0, tiled=True).astype(f32)

    if in_pairs:

        def scattered_there(array):
            blocks = array.reshape(data_count, row_count, -1)
            return scatter_blocks(blocks[0::2], blocks[1::2])
    else:
        scattered_there = scattered
    weight_grads = [
        scattered_there(dw_qkv),
        scattered_there(dw_out),
        scattered(dw_gate_up),
        scattered(dw_down),
    ]
    square = sum(jnp.sum(grad * grad) for grad in weight_grads)
    gain_grads = sum_all(jnp.concatenate([attn_gain_grad, mlp_gain_grad, grad_gain_query, grad_gain_key]))
    square_total = sum_all(square.reshape(1, 1))[0, 0]
    grad_norm = jnp.sqrt(square_total + jnp.sum(gain_grads * gain_grads))
    factor = 1.0 / jnp.maximum(grad_norm, 1.0)
    weight_grad = jnp.concatenate(weight_grads, axis=1)
    new_weights, new_momentum, new_ema = update(weights, momentum, ema_weights, weight_grad, factor, learn_rate)
    new_gains, new_gain_momentum, new_gain_ema = update(gains, gain_momentum, gain_ema, gain_grads, factor, gain_rate)
    return (
        block_output,
        grad_input,
        grad_norm,
        new_weights,
        new_momentum,
        new_ema,
        new_gains,
        new_gain_momentum,
        new_gain_ema,
    )


def solution(mesh):
    return jax.shard_map(
        per_device,
        mesh=mesh,
        in_specs=(
            P("dp", None),
            P("dp", None),
            P(),
            P(),
            P("dp", "mp"),
            P("dp", "mp"),
            P("dp", "mp"),
            P(),
            P(),
            P(),
        ),
        out_specs=(
            P("dp", None),
            P("dp", None),
            P(),
            P("dp", "mp"),
            P("dp", "mp"),
            P("dp", "mp"),
            P(),
            P(),
            P(),
        ),
        check_vma=False,
    )
```

```python
import functools

import jax
import jax.numpy as jnp
from jax import lax
from jax.experimental import pallas as pl
from jax.experimental.pallas import tpu as pltpu
from jax.sharding import PartitionSpec as P

HEADS = 16
KV = 8
HD = 128
FF = 6144
SPAN = 128
CHUNK = 4
TILE = 256
WIDE = 512
VMEM_LIMIT = 60 * 1024 * 1024

eps_norm = 1e-06
rope_base = 1000000.0
learn_rate = 100.0
gain_rate = 4000.0
momentum_decay = 0.5
average_decay = 0.5
score_scale = HD ** (-0.5)
far = -1e30

bf16 = jnp.bfloat16
f32 = jnp.float32
plain_dims = (((1,), (0,)), ((), ()))
last_dims = (((1,), (1,)), ((), ()))
first_dims = (((0,), (0,)), ((), ()))


def dot(a, b, dims=plain_dims):
    return lax.dot_general(a, b, dims, preferred_element_type=f32)


def cost(micros):
    return pl.CostEstimate(flops=int(micros * 1.0e9), bytes_accessed=int(micros * 3.4e6), transcendentals=0)


def params(**more):
    return pltpu.CompilerParams(vmem_limit_bytes=VMEM_LIMIT, **more)


def swap(array, axis, distance):
    count = lax.axis_size(axis)
    return lax.ppermute(array, axis, [(i, i ^ distance) for i in range(count)])


def gather_chips(own):
    return [own] + [swap(own, "dp", k) for k in (2, 4, 6)]


def gather_cores(outer):
    inner = [swap(block, "dp", 1) for block in outer]
    return [block for pair in zip(outer, inner) for block in pair]


def scatter_small(even, odd):
    came = swap(odd, "dp", 1)
    half = (even.astype(f32) + came.astype(f32)).astype(bf16)
    return [half[0]] + [swap(half[k], "dp", 2 * k) for k in (1, 2, 3)]


def add_pair(a, b):
    return (a.astype(f32) + b.astype(f32)).astype(bf16)


def sum_all(value):
    for axis in ("dp", "mp"):
        distance = 1
        while distance < lax.axis_size(axis):
            value = value + swap(value, axis, distance)
            distance *= 2
    return value


def place_of(me_ref, k, parts):
    return me_ref[0] ^ k if parts > 1 else 0


def columns_at(ref, block, width):
    return ref[:, pl.ds(pl.multiple_of(block * width, width), width)]


def turned(normed, cosine, sine):
    return normed * cosine + pltpu.roll(normed, HD // 2, 1) * sine


def turned_back(gradient, cosine, sine):
    return gradient * cosine + pltpu.roll(gradient * sine, HD // 2, 1)


def unit_scale(values):
    return lax.rsqrt(jnp.mean(values * values, axis=-1, keepdims=True) + eps_norm)


def norm_back(unit, scale, gain, gradient):
    e = gradient * gain
    return scale * (e - unit * jnp.mean(e * unit, axis=-1, keepdims=True))


def project_kernel(parts, q_tiles, me_ref, h_ref, *refs):
    w_refs = refs[:parts]
    cos_ref, sin_ref, gain_ref, q_ref, kv_ref, lin_ref = refs[parts:]
    tile = pl.program_id(0)
    depth = w_refs[0].shape[0]
    total = None
    for k, w_ref in enumerate(w_refs):
        term = dot(columns_at(h_ref, place_of(me_ref, k, parts), depth), w_ref[...])
        total = term if total is None else total + term
    per_tile = TILE // HD

    def normed_to(out_ref, gain):
        for part in range(per_tile):
            at = slice(part * HD, (part + 1) * HD)
            values = total[:, at]
            lin_ref[:, at] = values
            normed = values * unit_scale(values) * gain
            out_ref[:, at] = turned(normed, cos_ref[...], sin_ref[...]).astype(bf16)

    @pl.when(tile < q_tiles)
    def _():
        normed_to(q_ref, gain_ref[0:1])

    @pl.when(tile == q_tiles)
    def _():
        normed_to(kv_ref, gain_ref[1:2])

    @pl.when(tile > q_tiles)
    def _():
        kv_ref[...] = total.astype(bf16)


def span_limits(own_ref, starts_ref, i, group):
    span = own_ref[i]
    first = span * SPAN
    lane = lax.broadcasted_iota(jnp.int32, (1, group * SPAN), 1)
    places = first + (lane & (SPAN - 1))
    low = jnp.int32(0)
    begin = jnp.zeros((1, group * SPAN), jnp.int32)
    for d in range(starts_ref.shape[0]):
        start = starts_ref[d]
        low = jnp.maximum(low, jnp.where(start <= first, start, 0))
        begin = jnp.maximum(begin, jnp.where(start <= places, start, 0))
    return span, low // SPAN, places, begin


def key_rows(inverse_ref, newest, b):
    return pl.multiple_of(inverse_ref[jnp.maximum(newest - b, 0)] * SPAN, SPAN)


def allowed_keys(newest, places, begin):
    row = lax.broadcasted_iota(jnp.int32, (CHUNK * SPAN, 1), 0)
    key = newest * SPAN + (row & (SPAN - 1)) - (row & ~(SPAN - 1))
    return (key <= places) & (key >= begin)


def stacked(ref, i, head, group):
    rows = pl.ds(i * SPAN, SPAN)
    return jnp.concatenate([ref[rows, h * HD : (h + 1) * HD] for h in range(head * group, (head + 1) * group)], axis=0)


def head_columns(first, heads, kv_heads):
    keys = [pl.ds(pl.multiple_of((first + h) * HD, HD), HD) for h in range(heads)]
    values = [pl.ds(pl.multiple_of((first + h + kv_heads) * HD, HD), HD) for h in range(heads)]
    return keys, values


def load_parts(part_refs, target_ref, sem_ref, first):
    rows = part_refs[0].shape[0]
    return [
        pltpu.make_async_copy(ref, target_ref.at[pl.ds(k * rows, rows)], sem_ref.at[first + k])
        for k, ref in enumerate(part_refs)
    ]


def attend_kernel(group, heads, parts, own_ref, inverse_ref, starts_ref, q_ref, *refs):
    kv_parts = refs[:parts]
    turned_ref, low_ref, lse_ref, kv_ref, sem_ref = refs[parts:]
    g = pl.program_id(0)
    kv_heads = pl.num_programs(0) * heads
    kv_copies = load_parts(kv_parts, kv_ref, sem_ref, 0)

    @pl.when(g == 0)
    def _():
        for copy in kv_copies:
            copy.start()
        for copy in kv_copies:
            copy.wait()

    key_at, value_at = head_columns(g * heads, heads, kv_heads)
    wide = group * SPAN
    for i in range(own_ref.shape[0]):
        span, low, places, begin = span_limits(own_ref, starts_ref, i, group)
        queries = [stacked(q_ref, i, h, group) for h in range(heads)]
        count = (span - low) // CHUNK + 1

        def step(c, carry):
            newest = span - c * CHUNK
            at = [key_rows(inverse_ref, newest, b) for b in range(CHUNK)]
            allowed = allowed_keys(newest, places, begin)
            made = []
            for h, (top, weight, total) in enumerate(carry):
                keys = jnp.concatenate([kv_ref[pl.ds(a, SPAN), key_at[h]] for a in at], axis=0)
                values = jnp.concatenate([kv_ref[pl.ds(a, SPAN), value_at[h]] for a in at], axis=0)
                scores = jnp.where(allowed, dot(keys, queries[h], last_dims), far)
                new_top = jnp.maximum(top, jnp.max(scores, axis=0, keepdims=True))
                probs = jnp.exp((scores - new_top) * score_scale)
                shrink = jnp.exp((top - new_top) * score_scale)
                weight = weight * shrink + jnp.sum(probs, axis=0, keepdims=True)
                total = total * shrink + dot(values, probs.astype(bf16), first_dims)
                made.append((new_top, weight, total))
            return tuple(made)

        start = (jnp.full((1, wide), far, f32), jnp.zeros((1, wide), f32), jnp.zeros((HD, wide), f32))
        made = lax.fori_loop(0, count, step, (start,) * heads)
        for h, (top, weight, total) in enumerate(made):
            output = total / weight
            place = i * heads + h
            turned_ref[place] = output
            lse_ref[place] = jnp.broadcast_to(top * score_scale + jnp.log(weight), (8, wide))
            back = output.T.astype(bf16)
            for k in range(group):
                column = pl.multiple_of(((g * heads + h) * group + k) * HD, HD)
                low_ref[pl.ds(i * SPAN, SPAN), pl.ds(column, HD)] = back[k * SPAN : (k + 1) * SPAN]


def project_out_kernel(parts, me_ref, low_ref, *refs):
    out_parts = refs[:parts]
    o_ref = refs[parts]
    width = out_parts[0].shape[0]
    block = min(width, TILE)
    for k, w_ref in enumerate(out_parts):
        first = place_of(me_ref, k, parts) * width
        for b in range(width // block):
            at = pl.multiple_of(first + b * block, block)
            term = dot(low_ref[...], w_ref[b * block : (b + 1) * block], last_dims)
            o_ref[:, pl.ds(at, block)] = term.astype(bf16)


def mlp_kernel(x_ref, s_ref, gain_ref, c_ref, wg_ref, wu_ref, wd_ref, y_ref, h_ref, dg_ref, du_ref, a_ref):
    @pl.when(pl.program_id(0) == 0)
    def _():
        def rows_of(r, unused):
            at = pl.ds(pl.multiple_of(r * 64, 64), 64)
            y = x_ref[at, :].astype(f32) + s_ref[at, :].astype(f32)
            y_ref[at, :] = y
            h_ref[at, :] = (y * unit_scale(y) * gain_ref[...]).astype(bf16)
            return unused

        lax.fori_loop(0, x_ref.shape[0] // 64, rows_of, 0, unroll=2)

    hidden = h_ref[...]
    gate = dot(hidden, wg_ref[...])
    up = dot(hidden, wu_ref[...])
    grad = dot(c_ref[...], wd_ref[...])
    sig = 1.0 / (1.0 + jnp.exp(-gate))
    silu = gate * sig
    a_ref[...] = (silu * up).astype(bf16)
    dg_ref[...] = (grad * up * (sig + silu * (1.0 - sig))).astype(bf16)
    du_ref[...] = (grad * silu).astype(bf16)


def mlp_back_kernel(dg_ref, du_ref, wg_ref, wu_ref, dh_ref):
    dh_ref[...] = (dot(dg_ref[...], wg_ref[...], last_dims) + dot(du_ref[...], wu_ref[...], last_dims)).astype(bf16)


def rows_by_rows_kernel(a_ref, w_ref, o_ref):
    o_ref[...] = dot(a_ref[...], w_ref[...], last_dims).astype(bf16)


def residual_back_kernel(parts, share, me_ref, y_ref, c_ref, s_ref, gain_ref, *refs):
    out_parts = refs[:parts]
    dy_ref, low_ref, do_ref, dgain_ref = refs[parts:]

    @pl.when(pl.program_id(0) == 0)
    def _():
        dgain_ref[...] = jnp.zeros_like(dgain_ref)

    def rows_of(r, dgain):
        at = pl.ds(pl.multiple_of(r * 32, 32), 32)
        y = y_ref[at, :]
        scale = unit_scale(y)
        unit = y * scale
        grad = s_ref[at, :].astype(f32)
        dy = c_ref[at, :].astype(f32) + norm_back(unit, scale, gain_ref[...], grad)
        dy_ref[at, :] = dy
        low_ref[at, :] = dy.astype(bf16)
        return dgain + jnp.sum(grad * unit, axis=0, keepdims=True)

    zeros = jnp.zeros(dgain_ref.shape, f32)
    dgain_ref[...] += share * lax.fori_loop(0, y_ref.shape[0] // 32, rows_of, zeros, unroll=2)
    total = None
    depth = out_parts[0].shape[0]
    for k, w_ref in enumerate(out_parts):
        term = dot(columns_at(low_ref, place_of(me_ref, k, parts), depth), w_ref[...])
        total = term if total is None else total + term
    do_ref[...] = total.astype(bf16)


def attend_back_kernel(group, heads, parts, outs, own_ref, inverse_ref, starts_ref, q_ref, *refs):
    kv_parts = refs[:parts]
    do_ref, turned_ref, lse_ref, lin_ref, cos_ref, sin_ref, gain_ref = refs[parts : parts + 7]
    dq_ref, dgain_ref = refs[parts + 7 : parts + 9]
    dkv_refs = refs[parts + 9 : parts + 9 + outs]
    kv_ref, acc_ref, sem_ref = refs[parts + 9 + outs :]
    g = pl.program_id(0)
    kv_heads = pl.num_programs(0) * heads
    copies = load_parts(kv_parts, kv_ref, sem_ref, 0)

    @pl.when(g == 0)
    def _():
        for copy in copies:
            copy.start()

    acc_ref[...] = jnp.zeros_like(acc_ref)

    @pl.when(g == 0)
    def _():
        for copy in copies:
            copy.wait()

    key_at, value_at = head_columns(g * heads, heads, kv_heads)
    wide = group * SPAN
    dgain = jnp.zeros((1, HD), f32)
    for i in range(own_ref.shape[0]):
        span, low, places, begin = span_limits(own_ref, starts_ref, i, group)
        queries = [stacked(q_ref, i, h, group) for h in range(heads)]
        grads = [stacked(do_ref, i, h, group) for h in range(heads)]
        deltas = [
            jnp.sum(grads[h].astype(f32).T * turned_ref[i * heads + h], axis=0, keepdims=True) for h in range(heads)
        ]
        lses = [lse_ref[i * heads + h, :1] for h in range(heads)]
        count = (span - low) // CHUNK + 1

        def step(c, carry):
            newest = span - c * CHUNK
            at = [key_rows(inverse_ref, newest, b) for b in range(CHUNK)]
            allowed = allowed_keys(newest, places, begin)
            made = []
            for h, grad_query in enumerate(carry):
                keys = jnp.concatenate([kv_ref[pl.ds(a, SPAN), key_at[h]] for a in at], axis=0)
                values = jnp.concatenate([kv_ref[pl.ds(a, SPAN), value_at[h]] for a in at], axis=0)
                scores = dot(keys, queries[h], last_dims) * score_scale
                probs = jnp.exp(jnp.where(allowed, scores - lses[h], far))
                grad_probs = dot(values, grads[h], last_dims)
                grad_scores = (probs * (grad_probs - deltas[h])).astype(bf16)
                grad_values = dot(probs.astype(bf16), grads[h])
                grad_keys = dot(grad_scores, queries[h]) * score_scale
                left = 2 * h * HD
                for b, a in enumerate(at):
                    rows = slice(b * SPAN, (b + 1) * SPAN)
                    acc_ref[pl.ds(a, SPAN), left : left + HD] += grad_keys[rows]
                    acc_ref[pl.ds(a, SPAN), left + HD : left + 2 * HD] += grad_values[rows]
                made.append(grad_query + dot(keys, grad_scores, first_dims))
            return tuple(made)

        made = lax.fori_loop(0, count, step, (jnp.zeros((HD, wide), f32),) * heads)
        place = pl.ds(i * SPAN, SPAN)
        for h, grad_query in enumerate(made):
            grad_query = (grad_query * score_scale).T
            for k in range(group):
                at = slice((h * group + k) * HD, (h * group + k + 1) * HD)
                back = turned_back(grad_query[k * SPAN : (k + 1) * SPAN], cos_ref[place, :], sin_ref[place, :])
                lin = lin_ref[place, at]
                scale = unit_scale(lin)
                unit = lin * scale
                dgain = dgain + jnp.sum(back * unit, axis=0, keepdims=True)
                dq_ref[place, at] = norm_back(unit, scale, gain_ref[...], back).astype(bf16)
    dgain_ref[...] = jnp.broadcast_to(dgain, dgain_ref.shape)

    rows = acc_ref.shape[0] // parts
    for k in range(parts):
        dkv_refs[k % outs][pl.ds((k // outs) * rows, rows), :] = acc_ref[pl.ds(k * rows, rows), :].astype(bf16)


def key_back_kernel(parts, terms, kv_heads, me_ref, *refs):
    term_refs = refs[:terms]
    lin_ref, cos_ref, sin_ref, gain_ref, dq_ref, x_ref = refs[terms : terms + 6]
    w_refs = refs[terms + 6 : terms + 6 + parts]
    dkv_ref, dgain_k_ref, dgain_ref, dh_ref, unit_ref = refs[terms + 6 + parts :]
    dgain = jnp.zeros((1, HD), f32)

    def total(begin):
        value = None
        for ref in term_refs:
            term = ref[:, begin : begin + HD].astype(f32)
            value = term if value is None else value + term
        return value

    for g in range(kv_heads):
        at = slice(g * HD, (g + 1) * HD)
        back = turned_back(total(2 * g * HD), cos_ref[...], sin_ref[...])
        lin = lin_ref[:, at]
        scale = unit_scale(lin)
        unit = lin * scale
        dgain = dgain + jnp.sum(back * unit, axis=0, keepdims=True)
        dkv_ref[:, at] = norm_back(unit, scale, gain_ref[...], back).astype(bf16)
        dkv_ref[:, (kv_heads + g) * HD : (kv_heads + g + 1) * HD] = total((2 * g + 1) * HD).astype(bf16)
    dgain_k_ref[...] = jnp.broadcast_to(dgain, dgain_k_ref.shape)

    def rows_of(r, unused):
        at = pl.ds(pl.multiple_of(r * 64, 64), 64)
        x = x_ref[at, :].astype(f32)
        unit_ref[at, :] = x * unit_scale(x)
        return unused

    lax.fori_loop(0, x_ref.shape[0] // 64, rows_of, 0, unroll=2)
    width = w_refs[0].shape[0]
    block = min(width, TILE)
    q_width = dq_ref.shape[1]
    for k, w_ref in enumerate(w_refs):
        first = place_of(me_ref, k, parts) * width
        for b in range(width // block):
            here = pl.ds(pl.multiple_of(first + b * block, block), block)
            rows = slice(b * block, (b + 1) * block)
            term = dot(dq_ref[...], w_ref[rows, :q_width], last_dims)
            term = term + dot(dkv_ref[...], w_ref[rows, q_width:], last_dims)
            dh_ref[:, here] = term.astype(bf16)
            dgain_ref[:, here] = jnp.sum(term * unit_ref[:, here], axis=0, keepdims=True)


def input_back_kernel(dy_ref, x_ref, s_ref, gain_ref, o_ref):
    def rows_of(r, unused):
        at = pl.ds(pl.multiple_of(r * 32, 32), 32)
        x = x_ref[at, :].astype(f32)
        scale = unit_scale(x)
        back = norm_back(x * scale, scale, gain_ref[...], s_ref[at, :].astype(f32))
        o_ref[at, :] = dy_ref[at, :] + back
        return unused

    lax.fori_loop(0, x_ref.shape[0] // 32, rows_of, 0, unroll=2)


def transpose_kernel(me_ref, x_ref, o_ref):
    o_ref[...] = x_ref[...].T


def transposed(me, lhs, parts, rows):
    tokens, depth = lhs.shape
    rows = rows if parts > 1 else TILE
    return pl.pallas_call(
        transpose_kernel,
        grid_spec=pltpu.PrefetchScalarGridSpec(
            num_scalar_prefetch=1,
            grid=(depth // rows,),
            in_specs=[pl.BlockSpec((tokens, rows), weight_source(parts, depth // rows))],
            out_specs=pl.BlockSpec((rows, tokens), lambda p, _: (p, 0)),
        ),
        out_shape=jax.ShapeDtypeStruct((depth, tokens), bf16),
        compiler_params=params(),
        cost_estimate=cost(5),
        name="transposed",
    )(me, lhs)


def weight_source(parts, steps):
    half = steps // 2

    def source(p, me_ref):
        return (0, me_ref[0] ^ (2 * (p % half) + p // half)) if parts > 1 else (0, p)

    return source


def weight_grad_kernel(outs, count, me_ref, lhs_ref, *refs):
    rhs_refs = refs[:count]
    out_refs = refs[count:]
    step = pl.program_id(0)
    half = pl.num_programs(0) // outs
    for o in range(outs):

        @pl.when((step >= o * half) & (step < (o + 1) * half))
        def _():
            for rhs_ref, out_ref in zip(rhs_refs, out_refs[o * count : (o + 1) * count]):
                out_ref[0] = dot(lhs_ref[...], rhs_ref[...], first_dims).astype(bf16)


def mlp_weight_grad_kernel(h_ref, c_ref, dg_ref, du_ref, a_ref, dgu_ref, down_ref):
    width = a_ref.shape[1]
    dgu_ref[:, :width] = dot(h_ref[...], dg_ref[...], first_dims).astype(bf16)
    dgu_ref[:, width:] = dot(h_ref[...], du_ref[...], first_dims).astype(bf16)
    down_ref[...] = dot(c_ref[...], a_ref[...], first_dims).astype(bf16)


def weight_grad_turned_kernel(outs, lhs_ref, rhs_ref, *out_refs):
    for o, out_ref in enumerate(out_refs):

        @pl.when(pl.program_id(0) == o)
        def _():
            out_ref[...] = dot(lhs_ref[...], rhs_ref[...]).astype(bf16)


def weight_grad(me, lhs, rhs, parts, rows, is_transposed=False):
    tokens = rhs[0].shape[0]
    depth = lhs.size // tokens
    outs = 2 if parts > 1 else 1
    rows = rows if parts > 1 else TILE
    columns = sum(r.shape[1] for r in rhs)
    if is_transposed:
        half = depth // rows // outs
        made = pl.pallas_call(
            functools.partial(weight_grad_turned_kernel, outs),
            grid=(outs,),
            in_specs=[pl.BlockSpec((depth // outs, tokens), lambda p: (p, 0)), pl.BlockSpec(rhs[0].shape, lambda p: (0, 0))],
            out_specs=[pl.BlockSpec((depth // outs, columns), lambda p: (0, 0))] * outs,
            out_shape=[jax.ShapeDtypeStruct((depth // outs, columns), bf16)] * outs,
            compiler_params=params(),
            cost_estimate=cost(1),
            name="weight_grad_turned",
        )(lhs, rhs[0])
        return [[m.reshape(half, rows, columns) for m in made]]
    steps = depth // rows
    half = steps // outs

    def out_spec(o, width):
        return pl.BlockSpec((1, rows, width), lambda p, _: (jnp.clip(p - o * half, 0, half - 1), 0, 0))

    made = pl.pallas_call(
        functools.partial(weight_grad_kernel, outs, len(rhs)),
        grid_spec=pltpu.PrefetchScalarGridSpec(
            num_scalar_prefetch=1,
            grid=(steps,),
            in_specs=[pl.BlockSpec((tokens, rows), weight_source(parts, steps))]
            + [pl.BlockSpec(r.shape, lambda p, _: (0, 0)) for r in rhs],
            out_specs=[out_spec(o, r.shape[1]) for o in range(outs) for r in rhs],
        ),
        out_shape=[jax.ShapeDtypeStruct((half, rows, r.shape[1]), bf16) for o in range(outs) for r in rhs],
        compiler_params=params(),
        cost_estimate=cost(1),
        name="weight_grad",
    )(me, lhs, *rhs)
    return [made[k :: len(rhs)] for k in range(len(rhs))]


def update_kernel(factor_ref, w_ref, m_ref, e_ref, *refs):
    new_w_ref, new_m_ref, new_e_ref = refs[-3:]
    begin = 0
    for g_ref in refs[:-3]:
        at = slice(begin, begin + g_ref.shape[1])
        made = update(w_ref[:, at], m_ref[:, at], e_ref[:, at], g_ref[...].astype(f32), factor_ref[0], learn_rate)
        new_w_ref[:, at], new_m_ref[:, at], new_e_ref[:, at] = made
        begin += g_ref.shape[1]


def update_weights(factor, weights, momentum, average, pieces):
    rows, columns = weights.shape
    step = 32
    spec = pl.BlockSpec((step, columns), lambda n, _: (n, 0))
    shape = jax.ShapeDtypeStruct(weights.shape, f32)
    return pl.pallas_call(
        update_kernel,
        grid_spec=pltpu.PrefetchScalarGridSpec(
            num_scalar_prefetch=1,
            grid=(rows // step,),
            in_specs=[spec, spec, spec]
            + [pl.BlockSpec((step, piece.shape[1]), lambda n, _: (n, 0)) for piece in pieces],
            out_specs=[spec, spec, spec],
        ),
        out_shape=(shape, shape, shape),
        compiler_params=params(),
        cost_estimate=cost(1),
        name="update",
    )(factor, weights, momentum, average, *pieces)


def update(value, state, average, gradient, factor, step_rate):
    clipped = gradient * factor
    state_new = momentum_decay * state + clipped
    value_new = value - step_rate * (clipped + momentum_decay * state_new)
    average_new = average_decay * average + (1.0 - average_decay) * value_new
    return (value_new, state_new, average_new)


def per_device(
    block_input,
    cotangent,
    doc_lengths,
    span_order,
    weights,
    momentum,
    ema_weights,
    gains,
    gain_momentum,
    gain_ema,
):
    tok_count, model_width = block_input.shape
    data_count = lax.axis_size("dp")
    model_count = lax.axis_size("mp")
    me = lax.axis_index("dp").astype(jnp.int32)
    me_array = me[None]
    row_count = weights.shape[0]
    token_total = tok_count * data_count
    span_total = token_total // SPAN
    span_own = tok_count // SPAN
    seq_len = token_total // doc_lengths.shape[0]
    doc_total = doc_lengths.shape[0] * doc_lengths.shape[1]
    q_heads = HEADS // model_count
    kv_heads = KV // model_count
    group = q_heads // kv_heads
    query_width = q_heads * HD
    kv_width = kv_heads * HD
    ff_width = FF // model_count
    qkv_cols = query_width + 2 * kv_width
    out_end = qkv_cols + query_width
    in_pairs = data_count == 8
    parts = data_count if in_pairs else 1
    outs = 2 if in_pairs else 1
    gain_attn = gains[:model_width]
    gain_mlp = gains[model_width : 2 * model_width]
    head_gains = gains[2 * model_width :].reshape(2, HD)

    qkv_own = weights[:, :qkv_cols].astype(bf16)
    if in_pairs:
        qkv_outer = gather_chips(qkv_own)
        later, qkv_own = lax.optimization_barrier((weights, qkv_own))
        out_outer = gather_chips(later[:, qkv_cols:out_end].astype(bf16))
    else:
        later = weights
        qkv_parts = [lax.all_gather(qkv_own, "dp", axis=0, tiled=True)]
        out_own = weights[:, qkv_cols:out_end].astype(bf16)
        out_parts = [lax.all_gather(out_own, "dp", axis=0, tiled=True)]

    doc_ids = jnp.arange(doc_lengths.shape[1], dtype=jnp.int32)
    earlier = doc_ids[None, :] < doc_ids[:, None]
    starts = jnp.sum(jnp.where(earlier[None], doc_lengths[:, None, :], 0), axis=2)
    starts = starts + seq_len * jnp.arange(doc_lengths.shape[0], dtype=jnp.int32)[:, None]
    starts = starts.reshape(doc_total)
    span_ids = jnp.arange(span_total, dtype=jnp.int32)
    inverse = jnp.sum(jnp.where(span_order[None, :] == span_ids[:, None], span_ids[None, :], 0), axis=1)
    if in_pairs:
        inverse = ((inverse // span_own) ^ me) * span_own + inverse % span_own
    own_spans = lax.dynamic_slice(span_order, (me * span_own,), (span_own,))
    home = (own_spans[:, None] * SPAN + jnp.arange(SPAN, dtype=jnp.int32)[None, :]).reshape(tok_count)
    doc_start = jnp.max(jnp.where(starts[None, :] <= home[:, None], starts[None, :], 0), axis=1)
    freqs = rope_base ** (-(2.0 * (jnp.arange(HD, dtype=jnp.int32) % (HD // 2)).astype(f32)) / HD)
    angles = (home - doc_start).astype(f32)[:, None] * freqs[None, :]
    cosine = jnp.cos(angles)
    sine = jnp.sin(angles) * jnp.where(jnp.arange(HD) < HD // 2, -1.0, 1.0)[None, :]

    inputs = block_input.astype(f32)
    normed_low = (inputs * unit_scale(inputs) * gain_attn).astype(bf16)

    normed_turned = transposed(me_array, normed_low, parts, row_count)
    if in_pairs:
        normed_turned, qkv_outer[1] = lax.optimization_barrier((normed_turned, qkv_outer[1]))
        qkv_parts = gather_cores(qkv_outer)

    q_tiles = query_width // TILE
    rows_all = pl.BlockSpec((tok_count, model_width), lambda *_: (0, 0))
    angle_spec = pl.BlockSpec((tok_count, HD), lambda *_: (0, 0))
    part_tile = pl.BlockSpec((model_width // parts, TILE), lambda n, *_: (0, n))
    queries, keys_values, lin = pl.pallas_call(
        functools.partial(project_kernel, parts, q_tiles),
        grid_spec=pltpu.PrefetchScalarGridSpec(
            num_scalar_prefetch=1,
            grid=(qkv_cols // TILE,),
            in_specs=[rows_all]
            + [part_tile] * parts
            + [angle_spec, angle_spec, pl.BlockSpec((2, HD), lambda *_: (0, 0))],
            out_specs=[
                pl.BlockSpec((tok_count, TILE), lambda n, *_: (0, jnp.minimum(n, q_tiles - 1))),
                pl.BlockSpec((tok_count, TILE), lambda n, *_: (0, jnp.maximum(n - q_tiles, 0))),
                pl.BlockSpec((tok_count, TILE), lambda n, *_: (0, jnp.minimum(n, q_tiles))),
            ],
        ),
        out_shape=(
            jax.ShapeDtypeStruct((tok_count, query_width), bf16),
            jax.ShapeDtypeStruct((tok_count, 2 * kv_width), bf16),
            jax.ShapeDtypeStruct((tok_count, query_width + kv_width), f32),
        ),
        compiler_params=params(),
        cost_estimate=cost(6),
        name="project",
    )(me_array, normed_low, *qkv_parts, cosine, sine, head_gains)

    mlp_own = later[:, out_end:].astype(bf16)
    if in_pairs:
        keys_values, out_outer = lax.optimization_barrier((keys_values, out_outer))
        kv_parts = gather_cores(gather_chips(keys_values))
        out_parts = gather_cores(out_outer)
        mlp_own, out_parts, kv_parts = lax.optimization_barrier((mlp_own, out_parts, kv_parts))
    else:
        kv_parts = [lax.all_gather(keys_values, "dp", axis=0, tiled=True)]
    mlp_weights = lax.all_gather(mlp_own, "dp", axis=0, tiled=True)

    heads = kv_heads if in_pairs else 1
    head_steps = kv_heads // heads
    wide = group * SPAN
    anywhere = pl.BlockSpec(memory_space=pl.ANY)
    head_spec = pl.BlockSpec((tok_count, heads * group * HD), lambda g, *_: (0, g))
    q_all = pl.BlockSpec((tok_count, query_width), lambda *_: (0, 0))
    turned_spec = pl.BlockSpec((span_own * heads, HD, wide), lambda g, *_: (g, 0, 0))
    lse_spec = pl.BlockSpec((span_own * heads, 8, wide), lambda g, *_: (g, 0, 0))
    attended, attended_low, lse = pl.pallas_call(
        functools.partial(attend_kernel, group, heads, parts),
        grid_spec=pltpu.PrefetchScalarGridSpec(
            num_scalar_prefetch=3,
            grid=(head_steps,),
            in_specs=[head_spec] + [anywhere] * parts,
            out_specs=[turned_spec, q_all, lse_spec],
            scratch_shapes=[
                pltpu.VMEM((token_total, 2 * kv_width), bf16),
                pltpu.SemaphoreType.DMA((parts,)),
            ],
        ),
        out_shape=(
            jax.ShapeDtypeStruct((span_own * kv_heads, HD, wide), f32),
            jax.ShapeDtypeStruct((tok_count, query_width), bf16),
            jax.ShapeDtypeStruct((span_own * kv_heads, 8, wide), f32),
        ),
        compiler_params=params(),
        cost_estimate=cost(16),
        name="attend",
    )(own_spans, inverse, starts, queries, *kv_parts)
    part_all = pl.BlockSpec((model_width // parts, query_width), lambda *_: (0, 0))
    attn_part = pl.pallas_call(
        functools.partial(project_out_kernel, parts),
        grid_spec=pltpu.PrefetchScalarGridSpec(
            num_scalar_prefetch=1,
            grid=(1,),
            in_specs=[q_all] + [part_all] * parts,
            out_specs=rows_all,
        ),
        out_shape=jax.ShapeDtypeStruct((tok_count, model_width), bf16),
        compiler_params=params(),
        cost_estimate=cost(4),
        name="project_out",
    )(me_array, attended_low, *out_parts)

    attn_sum = lax.psum(attn_part, "mp")

    tiles = ff_width // TILE
    gain_spec = pl.BlockSpec((1, model_width), lambda *_: (0, 0))
    tile_spec = pl.BlockSpec((tok_count, TILE), lambda n: (0, n))
    hidden_shape = jax.ShapeDtypeStruct((tok_count, ff_width), bf16)
    low_shape = jax.ShapeDtypeStruct((tok_count, model_width), bf16)
    wide_shape = jax.ShapeDtypeStruct((tok_count, model_width), f32)
    residual, mlp_low, grad_gate, grad_up, hidden_low = pl.pallas_call(
        mlp_kernel,
        grid=(tiles,),
        in_specs=[
            rows_all,
            rows_all,
            gain_spec,
            rows_all,
            pl.BlockSpec((model_width, TILE), lambda n: (0, n)),
            pl.BlockSpec((model_width, TILE), lambda n: (0, n + tiles)),
            pl.BlockSpec((model_width, TILE), lambda n: (0, n + 2 * tiles)),
        ],
        out_specs=[rows_all, rows_all, tile_spec, tile_spec, tile_spec],
        out_shape=(wide_shape, low_shape, hidden_shape, hidden_shape, hidden_shape),
        compiler_params=params(),
        cost_estimate=cost(18),
        name="mlp",
    )(block_input, attn_sum, gain_mlp[None], cotangent, mlp_weights, mlp_weights, mlp_weights)

    hidden_all = pl.BlockSpec((tok_count, ff_width), lambda n: (0, 0))
    out_tile = pl.BlockSpec((tok_count, 512), lambda n: (0, n))
    grad_mlp_part = pl.pallas_call(
        mlp_back_kernel,
        grid=(model_width // WIDE,),
        in_specs=[
            hidden_all,
            hidden_all,
            pl.BlockSpec((WIDE, ff_width), lambda n: (n, 0)),
            pl.BlockSpec((WIDE, ff_width), lambda n: (n, 1)),
        ],
        out_specs=out_tile,
        out_shape=low_shape,
        compiler_params=params(),
        cost_estimate=cost(11),
        name="mlp_back",
    )(grad_gate, grad_up, mlp_weights, mlp_weights)
    grad_mlp_part, mlp_low, hidden_low = lax.optimization_barrier((grad_mlp_part, mlp_low, hidden_low))
    grad_mlp_sum = lax.psum(grad_mlp_part, "mp")

    row_tile = pl.BlockSpec((tok_count, TILE), lambda n: (0, n))
    dw_gate_up, dw_down = pl.pallas_call(
        mlp_weight_grad_kernel,
        grid=(model_width // TILE,),
        in_specs=[row_tile, row_tile, hidden_all, hidden_all, hidden_all],
        out_specs=[pl.BlockSpec((TILE, k * ff_width), lambda n: (n, 0)) for k in (2, 1)],
        out_shape=[jax.ShapeDtypeStruct((model_width, k * ff_width), bf16) for k in (2, 1)],
        compiler_params=params(),
        cost_estimate=cost(1),
        name="mlp_weight_grad",
    )(mlp_low, cotangent, grad_gate, grad_up, hidden_low)
    mlp_part = pl.pallas_call(
        rows_by_rows_kernel,
        grid=(model_width // 512,),
        in_specs=[hidden_all, pl.BlockSpec((512, ff_width), lambda n: (n, 2))],
        out_specs=out_tile,
        out_shape=low_shape,
        compiler_params=params(),
        cost_estimate=cost(1),
        name="mlp_out",
    )(hidden_low, mlp_weights)
    gate_up_grads = lax.psum_scatter(dw_gate_up, "dp", scatter_dimension=0, tiled=True)
    down_grads = lax.psum_scatter(dw_down, "dp", scatter_dimension=0, tiled=True)
    grad_mlp_sum, mlp_part, dw_gate_up = lax.optimization_barrier((grad_mlp_sum, mlp_part, dw_gate_up))
    mlp_sum = lax.psum(mlp_part, "mp")

    half_rows = tok_count // 2
    half_spec = pl.BlockSpec((half_rows, model_width), lambda n, *_: (n, 0))
    grad_residual, grad_res_low, grad_att_low, mlp_gain_grad = pl.pallas_call(
        functools.partial(residual_back_kernel, parts, 1.0 / model_count),
        grid_spec=pltpu.PrefetchScalarGridSpec(
            num_scalar_prefetch=1,
            grid=(2,),
            in_specs=[half_spec, half_spec, half_spec, gain_spec]
            + [pl.BlockSpec((model_width // parts, query_width), lambda *_: (0, 0))] * parts,
            out_specs=[half_spec, half_spec, pl.BlockSpec((half_rows, query_width), lambda n, *_: (n, 0)), gain_spec],
        ),
        out_shape=(
            wide_shape,
            low_shape,
            jax.ShapeDtypeStruct((tok_count, query_width), bf16),
            jax.ShapeDtypeStruct((1, model_width), f32),
        ),
        compiler_params=params(),
        cost_estimate=cost(1),
        name="residual_back",
    )(me_array, residual, cotangent, grad_mlp_sum, gain_mlp[None], *out_parts)
    out_rows = token_total // parts
    dkv_spec = pl.BlockSpec((out_rows, 2 * heads * HD), lambda g, *_: (0, g))
    back = pl.pallas_call(
        functools.partial(attend_back_kernel, group, heads, parts, parts),
        grid_spec=pltpu.PrefetchScalarGridSpec(
            num_scalar_prefetch=3,
            grid=(head_steps,),
            in_specs=[head_spec]
            + [anywhere] * parts
            + [head_spec, turned_spec, lse_spec, head_spec]
            + [angle_spec, angle_spec, pl.BlockSpec((1, HD), lambda *_: (0, 0))],
            out_specs=[head_spec, pl.BlockSpec((8, HD), lambda g, *_: (g, 0))] + [dkv_spec] * parts,
            scratch_shapes=[
                pltpu.VMEM((token_total, 2 * kv_width), bf16),
                pltpu.VMEM((token_total, 2 * heads * HD), f32),
                pltpu.SemaphoreType.DMA((parts,)),
            ],
        ),
        out_shape=[
            jax.ShapeDtypeStruct((tok_count, query_width), bf16),
            jax.ShapeDtypeStruct((8 * head_steps, HD), f32),
        ]
        + [jax.ShapeDtypeStruct((out_rows, 2 * kv_width), bf16)] * parts,
        compiler_params=params(),
        cost_estimate=cost(1),
        name="attend_back",
    )(
        own_spans,
        inverse,
        starts,
        queries,
        *kv_parts,
        grad_att_low,
        attended,
        lse,
        lin,
        cosine,
        sine,
        head_gains[:1],
    )
    back, gate_up_grads = lax.optimization_barrier((back, gate_up_grads))
    grad_query_low, query_gain_grad = back[:2]
    query_gain_grad = jnp.sum(query_gain_grad, axis=0) / 8.0
    if in_pairs:
        came = [swap(back[2 + k], "dp", 1) for k in range(1, parts, 2)]
        halves = [add_pair(back[2 + 2 * k], came[k]) for k in range(parts // 2)]
        terms = [halves[0]] + [swap(halves[k], "dp", 2 * k) for k in range(1, parts // 2)]
    else:
        terms = [lax.psum_scatter(back[2], "dp", scatter_dimension=0, tiled=True)]

    [dw_query] = weight_grad(me_array, normed_turned, [grad_query_low], parts, row_count, True)
    [dw_out] = weight_grad(me_array, grad_res_low, [attended_low], parts, row_count)

    terms, dw_query, dw_out, mlp_sum = lax.optimization_barrier((terms, dw_query, dw_out, mlp_sum))
    grad_kv_low, key_gain_grad, attn_gain_grad, grad_norm_part = pl.pallas_call(
        functools.partial(key_back_kernel, parts, len(terms), kv_heads),
        grid_spec=pltpu.PrefetchScalarGridSpec(
            num_scalar_prefetch=1,
            grid=(1,),
            in_specs=[pl.BlockSpec((tok_count, 2 * kv_width), lambda *_: (0, 0))] * len(terms)
            + [pl.BlockSpec((tok_count, kv_width), lambda *_: (0, query_width // kv_width))]
            + [angle_spec, angle_spec, pl.BlockSpec((1, HD), lambda *_: (0, 0))]
            + [q_all, rows_all]
            + [pl.BlockSpec((model_width // parts, qkv_cols), lambda *_: (0, 0))] * parts,
            out_specs=[
                pl.BlockSpec((tok_count, 2 * kv_width), lambda *_: (0, 0)),
                pl.BlockSpec((8, HD), lambda *_: (0, 0)),
                gain_spec,
                rows_all,
            ],
            scratch_shapes=[pltpu.VMEM((tok_count, model_width), f32)],
        ),
        out_shape=[
            jax.ShapeDtypeStruct((tok_count, 2 * kv_width), bf16),
            jax.ShapeDtypeStruct((8, HD), f32),
            jax.ShapeDtypeStruct((1, model_width), f32),
            low_shape,
        ],
        compiler_params=params(),
        cost_estimate=cost(1),
        name="key_back",
    )(me_array, *terms, lin, cosine, sine, head_gains[1:], grad_query_low, block_input, *qkv_parts)
    [dw_kv] = weight_grad(me_array, normed_turned, [grad_kv_low], parts, row_count, True)

    grad_norm_sum = lax.psum(grad_norm_part, "mp")
    if in_pairs:
        small = [scatter_small(*dw) for dw in (dw_query, dw_kv, dw_out)]
        small = [sum(term.astype(f32) for term in piece).astype(bf16) for piece in small]
    else:

        def scattered(made):
            whole = made[0].reshape(model_width, -1)
            return lax.psum_scatter(whole, "dp", scatter_dimension=0, tiled=True)

        small = [scattered(dw) for dw in (dw_query, dw_kv, dw_out)]
    gain_grads = sum_all(
        jnp.concatenate([attn_gain_grad[0], mlp_gain_grad[0], query_gain_grad, key_gain_grad[0]])
    )
    square = sum(jnp.sum(jnp.square(grad.astype(f32))) for grad in small + [gate_up_grads, down_grads])
    square_total = sum_all(square.reshape(1, 1))[0, 0]
    grad_norm = jnp.sqrt(square_total + jnp.sum(gain_grads * gain_grads))
    factor = 1.0 / jnp.maximum(grad_norm, 1.0)
    new_weights, new_momentum, new_ema = update_weights(factor[None], weights, momentum, ema_weights, small + [gate_up_grads, down_grads])
    gain_grads, mlp_sum = lax.optimization_barrier((gain_grads, mlp_sum))
    block_output = (residual + mlp_sum.astype(f32)).astype(bf16)
    eighth = tok_count // 8
    eighth_spec = pl.BlockSpec((eighth, model_width), lambda n: (n, 0))
    grad_input = pl.pallas_call(
        input_back_kernel,
        grid=(8,),
        in_specs=[eighth_spec, eighth_spec, eighth_spec, gain_spec],
        out_specs=eighth_spec,
        out_shape=wide_shape,
        compiler_params=params(),
        cost_estimate=cost(300),
        name="input_back",
    )(grad_residual, block_input, grad_norm_sum, gain_attn[None])
    new_gains, new_gain_momentum, new_gain_ema = update(gains, gain_momentum, gain_ema, gain_grads, factor, gain_rate)
    return (
        block_output,
        grad_input,
        grad_norm,
        new_weights,
        new_momentum,
        new_ema,
        new_gains,
        new_gain_momentum,
        new_gain_ema,
    )


def solution(mesh):
    return jax.shard_map(
        per_device,
        mesh=mesh,
        in_specs=(
            P("dp", None),
            P("dp", None),
            P(),
            P(),
            P("dp", "mp"),
            P("dp", "mp"),
            P("dp", "mp"),
            P(),
            P(),
            P(),
        ),
        out_specs=(
            P("dp", None),
            P("dp", None),
            P(),
            P("dp", "mp"),
            P("dp", "mp"),
            P("dp", "mp"),
            P(),
            P(),
            P(),
        ),
        check_vma=False,
    )
```

```python
import functools

import jax
import jax.numpy as jnp
from jax import lax
from jax.experimental import pallas as pl
from jax.experimental.pallas import tpu as pltpu
from jax.sharding import PartitionSpec as P

HEADS = 16
KV = 8
HD = 128
FF = 6144
SPAN = 128
CHUNK = 4
TILE = 256
WIDE = 512
VMEM_LIMIT = 60 * 1024 * 1024

eps_norm = 1e-06
rope_base = 1000000.0
learn_rate = 100.0
gain_rate = 4000.0
momentum_decay = 0.5
average_decay = 0.5
score_scale = HD ** (-0.5)
far = -1e30

bf16 = jnp.bfloat16
f32 = jnp.float32
plain_dims = (((1,), (0,)), ((), ()))
last_dims = (((1,), (1,)), ((), ()))
first_dims = (((0,), (0,)), ((), ()))


def dot(a, b, dims=plain_dims):
    return lax.dot_general(a, b, dims, preferred_element_type=f32)


def cost(micros):
    return pl.CostEstimate(flops=int(micros * 1.0e9), bytes_accessed=int(micros * 3.4e6), transcendentals=0)


def params(**more):
    return pltpu.CompilerParams(vmem_limit_bytes=VMEM_LIMIT, **more)


def swap(array, axis, distance):
    count = lax.axis_size(axis)
    return lax.ppermute(array, axis, [(i, i ^ distance) for i in range(count)])


def gather_chips(own):
    return [own] + [swap(own, "dp", k) for k in (2, 4, 6)]


def gather_cores(outer):
    inner = [swap(block, "dp", 1) for block in outer]
    return [block for pair in zip(outer, inner) for block in pair]


def scatter_small(even, odd):
    came = swap(odd, "dp", 1)
    half = (even.astype(f32) + came.astype(f32)).astype(bf16)
    return [half[0]] + [swap(half[k], "dp", 2 * k) for k in (1, 2, 3)]


def add_pair(a, b):
    return (a.astype(f32) + b.astype(f32)).astype(bf16)


def sum_all(value):
    for axis in ("dp", "mp"):
        distance = 1
        while distance < lax.axis_size(axis):
            value = value + swap(value, axis, distance)
            distance *= 2
    return value


def place_of(me_ref, k, parts):
    return me_ref[0] ^ k if parts > 1 else 0


def in_order(me_ref, part_refs, whole_ref):
    parts = len(part_refs)
    rows = part_refs[0].shape[0]
    for k, ref in enumerate(part_refs):
        at = pl.multiple_of(place_of(me_ref, k, parts) * rows, rows)
        whole_ref[pl.ds(at, rows), :] = ref[...]


def turned(normed, cosine, sine):
    return normed * cosine + pltpu.roll(normed, HD // 2, 1) * sine


def turned_back(gradient, cosine, sine):
    return gradient * cosine + pltpu.roll(gradient * sine, HD // 2, 1)


def unit_scale(values):
    return lax.rsqrt(jnp.mean(values * values, axis=-1, keepdims=True) + eps_norm)


def norm_back(unit, scale, gain, gradient):
    e = gradient * gain
    return scale * (e - unit * jnp.mean(e * unit, axis=-1, keepdims=True))


def project_kernel(parts, q_tiles, me_ref, h_ref, *refs):
    cos_ref, sin_ref, gain_ref, q_ref, kv_ref, lin_ref, w_ref = refs[parts:]
    tile = pl.program_id(0)
    in_order(me_ref, refs[:parts], w_ref)
    total = dot(h_ref[...], w_ref[...])
    per_tile = TILE // HD

    def normed_to(out_ref, gain):
        for part in range(per_tile):
            at = slice(part * HD, (part + 1) * HD)
            values = total[:, at]
            lin_ref[:, at] = values
            normed = values * unit_scale(values) * gain
            out_ref[:, at] = turned(normed, cos_ref[...], sin_ref[...]).astype(bf16)

    @pl.when(tile < q_tiles)
    def _():
        normed_to(q_ref, gain_ref[0:1])

    @pl.when(tile == q_tiles)
    def _():
        normed_to(kv_ref, gain_ref[1:2])

    @pl.when(tile > q_tiles)
    def _():
        kv_ref[...] = total.astype(bf16)


def span_limits(own_ref, starts_ref, i, group):
    span = own_ref[i]
    first = span * SPAN
    lane = lax.broadcasted_iota(jnp.int32, (1, group * SPAN), 1)
    places = first + (lane & (SPAN - 1))
    low = jnp.int32(0)
    begin = jnp.zeros((1, group * SPAN), jnp.int32)
    for d in range(starts_ref.shape[0]):
        start = starts_ref[d]
        low = jnp.maximum(low, jnp.where(start <= first, start, 0))
        begin = jnp.maximum(begin, jnp.where(start <= places, start, 0))
    return span, low // SPAN, places, begin


def key_rows(inverse_ref, newest, b):
    return pl.multiple_of(inverse_ref[jnp.maximum(newest - b, 0)] * SPAN, SPAN)


def allowed_keys(newest, places, begin):
    row = lax.broadcasted_iota(jnp.int32, (CHUNK * SPAN, 1), 0)
    key = newest * SPAN + (row & (SPAN - 1)) - (row & ~(SPAN - 1))
    return (key <= places) & (key >= begin)


def stacked(ref, i, head, group):
    rows = pl.ds(i * SPAN, SPAN)
    return jnp.concatenate([ref[rows, h * HD : (h + 1) * HD] for h in range(head * group, (head + 1) * group)], axis=0)


def head_columns(first, heads, kv_heads):
    keys = [pl.ds(pl.multiple_of((first + h) * HD, HD), HD) for h in range(heads)]
    values = [pl.ds(pl.multiple_of((first + h + kv_heads) * HD, HD), HD) for h in range(heads)]
    return keys, values


def load_parts(part_refs, target_ref, sem_ref, first):
    rows = part_refs[0].shape[0]
    return [
        pltpu.make_async_copy(ref, target_ref.at[pl.ds(k * rows, rows)], sem_ref.at[first + k])
        for k, ref in enumerate(part_refs)
    ]


def attend_kernel(group, heads, parts, own_ref, inverse_ref, starts_ref, q_ref, *refs):
    kv_parts = refs[:parts]
    turned_ref, low_ref, lse_ref, kv_ref, sem_ref = refs[parts:]
    g = pl.program_id(0)
    kv_heads = pl.num_programs(0) * heads
    kv_copies = load_parts(kv_parts, kv_ref, sem_ref, 0)

    @pl.when(g == 0)
    def _():
        for copy in kv_copies:
            copy.start()
        for copy in kv_copies:
            copy.wait()

    key_at, value_at = head_columns(g * heads, heads, kv_heads)
    wide = group * SPAN
    for i in range(own_ref.shape[0]):
        span, low, places, begin = span_limits(own_ref, starts_ref, i, group)
        queries = [stacked(q_ref, i, h, group) for h in range(heads)]
        count = (span - low) // CHUNK + 1

        def step(c, carry):
            newest = span - c * CHUNK
            at = [key_rows(inverse_ref, newest, b) for b in range(CHUNK)]
            allowed = allowed_keys(newest, places, begin)
            made = []
            for h, (top, weight, total) in enumerate(carry):
                keys = jnp.concatenate([kv_ref[pl.ds(a, SPAN), key_at[h]] for a in at], axis=0)
                values = jnp.concatenate([kv_ref[pl.ds(a, SPAN), value_at[h]] for a in at], axis=0)
                scores = jnp.where(allowed, dot(keys, queries[h], last_dims), far)
                new_top = jnp.maximum(top, jnp.max(scores, axis=0, keepdims=True))
                probs = jnp.exp((scores - new_top) * score_scale)
                shrink = jnp.exp((top - new_top) * score_scale)
                weight = weight * shrink + jnp.sum(probs, axis=0, keepdims=True)
                total = total * shrink + dot(values, probs.astype(bf16), first_dims)
                made.append((new_top, weight, total))
            return tuple(made)

        start = (jnp.full((1, wide), far, f32), jnp.zeros((1, wide), f32), jnp.zeros((HD, wide), f32))
        made = lax.fori_loop(0, count, step, (start,) * heads)
        for h, (top, weight, total) in enumerate(made):
            output = total / weight
            place = i * heads + h
            turned_ref[place] = output
            lse_ref[place] = jnp.broadcast_to(top * score_scale + jnp.log(weight), (8, wide))
            back = output.T.astype(bf16)
            for k in range(group):
                column = pl.multiple_of(((g * heads + h) * group + k) * HD, HD)
                low_ref[pl.ds(i * SPAN, SPAN), pl.ds(column, HD)] = back[k * SPAN : (k + 1) * SPAN]


def project_out_kernel(parts, me_ref, low_ref, *refs):
    out_parts = refs[:parts]
    o_ref = refs[parts]
    width = out_parts[0].shape[0]
    block = min(width, TILE)
    for k, w_ref in enumerate(out_parts):
        first = place_of(me_ref, k, parts) * width
        for b in range(width // block):
            at = pl.multiple_of(first + b * block, block)
            term = dot(low_ref[...], w_ref[b * block : (b + 1) * block], last_dims)
            o_ref[:, pl.ds(at, block)] = term.astype(bf16)


def plain_kernel(a_ref, w_ref, o_ref):
    o_ref[...] = dot(a_ref[...], w_ref[...]).astype(bf16)


def mlp_kernel(x_ref, s_ref, gain_ref, wg_ref, wu_ref, da_ref, y_ref, h_ref, scale_ref, dg_ref, du_ref, a_ref):
    @pl.when(pl.program_id(0) == 0)
    def _():
        def rows_of(r, unused):
            at = pl.ds(pl.multiple_of(r * 64, 64), 64)
            y = x_ref[at, :].astype(f32) + s_ref[at, :].astype(f32)
            y_ref[at, :] = y
            scale = unit_scale(y)
            scale_ref[at, :] = scale
            h_ref[at, :] = (y * scale * gain_ref[...]).astype(bf16)
            return unused

        lax.fori_loop(0, x_ref.shape[0] // 64, rows_of, 0, unroll=2)

    hidden = h_ref[...]
    gate = dot(hidden, wg_ref[...])
    up = dot(hidden, wu_ref[...])
    grad = da_ref[...].astype(f32)
    sig = 1.0 / (1.0 + jnp.exp(-gate))
    silu = gate * sig
    a_ref[...] = (silu * up).astype(bf16)
    dg_ref[...] = (grad * up * (sig + silu * (1.0 - sig))).astype(bf16)
    du_ref[...] = (grad * silu).astype(bf16)


def mlp_back_kernel(dg_ref, du_ref, wg_ref, wu_ref, dh_ref):
    dh_ref[...] = (dot(dg_ref[...], wg_ref[...], last_dims) + dot(du_ref[...], wu_ref[...], last_dims)).astype(bf16)


def rows_by_rows_kernel(a_ref, w_ref, o_ref):
    o_ref[...] = dot(a_ref[...], w_ref[...], last_dims).astype(bf16)


def residual_back_kernel(parts, share, me_ref, y_ref, scale_ref, c_ref, s_ref, gain_ref, *refs):
    dy_ref, low_ref, do_ref, dgain_ref, w_ref = refs[parts:]

    @pl.when(pl.program_id(0) == 0)
    def _():
        dgain_ref[...] = jnp.zeros_like(dgain_ref)
        in_order(me_ref, refs[:parts], w_ref)

    def rows_of(r, dgain):
        at = pl.ds(pl.multiple_of(r * 32, 32), 32)
        scale = scale_ref[at, :]
        unit = y_ref[at, :] * scale
        grad = s_ref[at, :].astype(f32)
        dy = c_ref[at, :].astype(f32) + norm_back(unit, scale, gain_ref[...], grad)
        dy_ref[at, :] = dy
        low_ref[at, :] = dy.astype(bf16)
        return dgain + jnp.sum(grad * unit, axis=0, keepdims=True)

    zeros = jnp.zeros(dgain_ref.shape, f32)
    dgain_ref[...] += share * lax.fori_loop(0, y_ref.shape[0] // 32, rows_of, zeros, unroll=2)
    do_ref[...] = dot(low_ref[...], w_ref[...]).astype(bf16)


def attend_back_kernel(group, heads, parts, outs, own_ref, inverse_ref, starts_ref, q_ref, *refs):
    kv_parts = refs[:parts]
    do_ref, turned_ref, lse_ref, lin_ref, cos_ref, sin_ref, gain_ref = refs[parts : parts + 7]
    dq_ref, dgain_ref = refs[parts + 7 : parts + 9]
    dkv_refs = refs[parts + 9 : parts + 9 + outs]
    kv_ref, acc_ref, sem_ref = refs[parts + 9 + outs :]
    g = pl.program_id(0)
    kv_heads = pl.num_programs(0) * heads
    copies = load_parts(kv_parts, kv_ref, sem_ref, 0)

    @pl.when(g == 0)
    def _():
        for copy in copies:
            copy.start()

    acc_ref[...] = jnp.zeros_like(acc_ref)

    @pl.when(g == 0)
    def _():
        for copy in copies:
            copy.wait()

    key_at, value_at = head_columns(g * heads, heads, kv_heads)
    wide = group * SPAN
    dgain = jnp.zeros((1, HD), f32)
    for i in range(own_ref.shape[0]):
        span, low, places, begin = span_limits(own_ref, starts_ref, i, group)
        queries = [stacked(q_ref, i, h, group) for h in range(heads)]
        grads = [stacked(do_ref, i, h, group) for h in range(heads)]
        deltas = [
            jnp.sum(grads[h].astype(f32).T * turned_ref[i * heads + h], axis=0, keepdims=True) for h in range(heads)
        ]
        lses = [lse_ref[i * heads + h, :1] for h in range(heads)]
        count = (span - low) // CHUNK + 1

        def step(c, carry):
            newest = span - c * CHUNK
            at = [key_rows(inverse_ref, newest, b) for b in range(CHUNK)]
            allowed = allowed_keys(newest, places, begin)
            made = []
            for h, grad_query in enumerate(carry):
                keys = jnp.concatenate([kv_ref[pl.ds(a, SPAN), key_at[h]] for a in at], axis=0)
                values = jnp.concatenate([kv_ref[pl.ds(a, SPAN), value_at[h]] for a in at], axis=0)
                scores = dot(keys, queries[h], last_dims) * score_scale
                probs = jnp.exp(jnp.where(allowed, scores - lses[h], far))
                grad_probs = dot(values, grads[h], last_dims)
                grad_scores = (probs * (grad_probs - deltas[h])).astype(bf16)
                grad_values = dot(probs.astype(bf16), grads[h])
                grad_keys = dot(grad_scores, queries[h]) * score_scale
                left = 2 * h * HD
                for b, a in enumerate(at):
                    rows = slice(b * SPAN, (b + 1) * SPAN)
                    acc_ref[pl.ds(a, SPAN), left : left + HD] += grad_keys[rows]
                    acc_ref[pl.ds(a, SPAN), left + HD : left + 2 * HD] += grad_values[rows]
                made.append(grad_query + dot(keys, grad_scores, first_dims))
            return tuple(made)

        made = lax.fori_loop(0, count, step, (jnp.zeros((HD, wide), f32),) * heads)
        place = pl.ds(i * SPAN, SPAN)
        for h, grad_query in enumerate(made):
            grad_query = (grad_query * score_scale).T
            for k in range(group):
                at = slice((h * group + k) * HD, (h * group + k + 1) * HD)
                back = turned_back(grad_query[k * SPAN : (k + 1) * SPAN], cos_ref[place, :], sin_ref[place, :])
                lin = lin_ref[place, at]
                scale = unit_scale(lin)
                unit = lin * scale
                dgain = dgain + jnp.sum(back * unit, axis=0, keepdims=True)
                dq_ref[place, at] = norm_back(unit, scale, gain_ref[...], back).astype(bf16)
    dgain_ref[...] = jnp.broadcast_to(dgain, dgain_ref.shape)

    rows = acc_ref.shape[0] // parts
    for k in range(parts):
        dkv_refs[k % outs][pl.ds((k // outs) * rows, rows), :] = acc_ref[pl.ds(k * rows, rows), :].astype(bf16)


def key_back_kernel(parts, terms, kv_heads, me_ref, *refs):
    term_refs = refs[:terms]
    lin_ref, cos_ref, sin_ref, gain_ref, dq_ref, x_ref, scale_ref = refs[terms : terms + 7]
    w_refs = refs[terms + 7 : terms + 7 + parts]
    dkv_ref, dgain_k_ref, dgain_ref, dh_ref = refs[terms + 7 + parts :]
    dgain = jnp.zeros((1, HD), f32)

    def total(begin):
        value = None
        for ref in term_refs:
            term = ref[:, begin : begin + HD].astype(f32)
            value = term if value is None else value + term
        return value

    for g in range(kv_heads):
        at = slice(g * HD, (g + 1) * HD)
        back = turned_back(total(2 * g * HD), cos_ref[...], sin_ref[...])
        lin = lin_ref[:, at]
        scale = unit_scale(lin)
        unit = lin * scale
        dgain = dgain + jnp.sum(back * unit, axis=0, keepdims=True)
        dkv_ref[:, at] = norm_back(unit, scale, gain_ref[...], back).astype(bf16)
        dkv_ref[:, (kv_heads + g) * HD : (kv_heads + g + 1) * HD] = total((2 * g + 1) * HD).astype(bf16)
    dgain_k_ref[...] = jnp.broadcast_to(dgain, dgain_k_ref.shape)

    scale = scale_ref[...]
    width = w_refs[0].shape[0]
    block = min(width, TILE)
    q_width = dq_ref.shape[1]
    for k, w_ref in enumerate(w_refs):
        first = place_of(me_ref, k, parts) * width
        for b in range(width // block):
            here = pl.ds(pl.multiple_of(first + b * block, block), block)
            rows = slice(b * block, (b + 1) * block)
            term = dot(dq_ref[...], w_ref[rows, :q_width], last_dims)
            term = term + dot(dkv_ref[...], w_ref[rows, q_width:], last_dims)
            dh_ref[:, here] = term.astype(bf16)
            unit = x_ref[:, here].astype(f32) * scale
            dgain_ref[:, here] = jnp.sum(term * unit, axis=0, keepdims=True)


def input_back_kernel(dy_ref, x_ref, scale_ref, s_ref, gain_ref, o_ref):
    def rows_of(r, unused):
        at = pl.ds(pl.multiple_of(r * 32, 32), 32)
        scale = scale_ref[at, :]
        back = norm_back(x_ref[at, :].astype(f32) * scale, scale, gain_ref[...], s_ref[at, :].astype(f32))
        o_ref[at, :] = dy_ref[at, :] + back
        return unused

    lax.fori_loop(0, x_ref.shape[0] // 32, rows_of, 0, unroll=2)


def transpose_kernel(me_ref, x_ref, o_ref):
    o_ref[...] = x_ref[...].T


def transposed(me, lhs, parts, rows):
    tokens, depth = lhs.shape
    rows = rows if parts > 1 else TILE
    return pl.pallas_call(
        transpose_kernel,
        grid_spec=pltpu.PrefetchScalarGridSpec(
            num_scalar_prefetch=1,
            grid=(depth // rows,),
            in_specs=[pl.BlockSpec((tokens, rows), weight_source(parts, depth // rows))],
            out_specs=pl.BlockSpec((rows, tokens), lambda p, _: (p, 0)),
        ),
        out_shape=jax.ShapeDtypeStruct((depth, tokens), bf16),
        compiler_params=params(),
        cost_estimate=cost(5),
        name="transposed",
    )(me, lhs)


def weight_source(parts, steps):
    half = steps // 2

    def source(p, me_ref):
        return (0, me_ref[0] ^ (2 * (p % half) + p // half)) if parts > 1 else (0, p)

    return source


def weight_grad_kernel(outs, count, me_ref, lhs_ref, *refs):
    rhs_refs = refs[:count]
    out_refs = refs[count:]
    step = pl.program_id(0)
    half = pl.num_programs(0) // outs
    for o in range(outs):

        @pl.when((step >= o * half) & (step < (o + 1) * half))
        def _():
            for rhs_ref, out_ref in zip(rhs_refs, out_refs[o * count : (o + 1) * count]):
                out_ref[0] = dot(lhs_ref[...], rhs_ref[...], first_dims).astype(bf16)


def mlp_weight_grad_kernel(h_ref, c_ref, dg_ref, du_ref, a_ref, o_ref):
    width = a_ref.shape[1]
    for k, (lhs_ref, rhs_ref) in enumerate(((h_ref, dg_ref), (h_ref, du_ref), (c_ref, a_ref))):
        o_ref[:, k * width : (k + 1) * width] = dot(lhs_ref[...], rhs_ref[...], first_dims).astype(bf16)


def weight_grad_turned_kernel(outs, lhs_ref, rhs_ref, *out_refs):
    for o, out_ref in enumerate(out_refs):

        @pl.when(pl.program_id(0) == o)
        def _():
            out_ref[...] = dot(lhs_ref[...], rhs_ref[...]).astype(bf16)


def weight_grad(me, lhs, rhs, parts, rows, is_transposed=False):
    tokens = rhs[0].shape[0]
    depth = lhs.size // tokens
    outs = 2 if parts > 1 else 1
    rows = rows if parts > 1 else TILE
    columns = sum(r.shape[1] for r in rhs)
    if is_transposed:
        half = depth // rows // outs
        made = pl.pallas_call(
            functools.partial(weight_grad_turned_kernel, outs),
            grid=(outs,),
            in_specs=[pl.BlockSpec((depth // outs, tokens), lambda p: (p, 0)), pl.BlockSpec(rhs[0].shape, lambda p: (0, 0))],
            out_specs=[pl.BlockSpec((depth // outs, columns), lambda p: (0, 0))] * outs,
            out_shape=[jax.ShapeDtypeStruct((depth // outs, columns), bf16)] * outs,
            compiler_params=params(),
            cost_estimate=cost(1),
            name="weight_grad_turned",
        )(lhs, rhs[0])
        return [[m.reshape(half, rows, columns) for m in made]]
    steps = depth // rows
    half = steps // outs

    def out_spec(o, width):
        return pl.BlockSpec((1, rows, width), lambda p, _: (jnp.clip(p - o * half, 0, half - 1), 0, 0))

    made = pl.pallas_call(
        functools.partial(weight_grad_kernel, outs, len(rhs)),
        grid_spec=pltpu.PrefetchScalarGridSpec(
            num_scalar_prefetch=1,
            grid=(steps,),
            in_specs=[pl.BlockSpec((tokens, rows), weight_source(parts, steps))]
            + [pl.BlockSpec(r.shape, lambda p, _: (0, 0)) for r in rhs],
            out_specs=[out_spec(o, r.shape[1]) for o in range(outs) for r in rhs],
        ),
        out_shape=[jax.ShapeDtypeStruct((half, rows, r.shape[1]), bf16) for o in range(outs) for r in rhs],
        compiler_params=params(),
        cost_estimate=cost(1),
        name="weight_grad",
    )(me, lhs, *rhs)
    return [made[k :: len(rhs)] for k in range(len(rhs))]


def update_kernel(factor_ref, w_ref, m_ref, e_ref, *refs):
    new_w_ref, new_m_ref, new_e_ref = refs[-3:]
    begin = 0
    for g_ref in refs[:-3]:
        at = slice(begin, begin + g_ref.shape[1])
        made = update(w_ref[:, at], m_ref[:, at], e_ref[:, at], g_ref[...].astype(f32), factor_ref[0], learn_rate)
        new_w_ref[:, at], new_m_ref[:, at], new_e_ref[:, at] = made
        begin += g_ref.shape[1]


def update_weights(factor, weights, momentum, average, pieces):
    rows, columns = weights.shape
    step = 32
    spec = pl.BlockSpec((step, columns), lambda n, _: (n, 0))
    shape = jax.ShapeDtypeStruct(weights.shape, f32)
    return pl.pallas_call(
        update_kernel,
        grid_spec=pltpu.PrefetchScalarGridSpec(
            num_scalar_prefetch=1,
            grid=(rows // step,),
            in_specs=[spec, spec, spec]
            + [pl.BlockSpec((step, piece.shape[1]), lambda n, _: (n, 0)) for piece in pieces],
            out_specs=[spec, spec, spec],
        ),
        out_shape=(shape, shape, shape),
        compiler_params=params(),
        cost_estimate=cost(1),
        name="update",
    )(factor, weights, momentum, average, *pieces)


def update(value, state, average, gradient, factor, step_rate):
    clipped = gradient * factor
    state_new = momentum_decay * state + clipped
    value_new = value - step_rate * (clipped + momentum_decay * state_new)
    average_new = average_decay * average + (1.0 - average_decay) * value_new
    return (value_new, state_new, average_new)


def per_device(
    block_input,
    cotangent,
    doc_lengths,
    span_order,
    weights,
    momentum,
    ema_weights,
    gains,
    gain_momentum,
    gain_ema,
):
    tok_count, model_width = block_input.shape
    data_count = lax.axis_size("dp")
    model_count = lax.axis_size("mp")
    me = lax.axis_index("dp").astype(jnp.int32)
    me_array = me[None]
    row_count = weights.shape[0]
    token_total = tok_count * data_count
    span_total = token_total // SPAN
    span_own = tok_count // SPAN
    seq_len = token_total // doc_lengths.shape[0]
    doc_total = doc_lengths.shape[0] * doc_lengths.shape[1]
    q_heads = HEADS // model_count
    kv_heads = KV // model_count
    group = q_heads // kv_heads
    query_width = q_heads * HD
    kv_width = kv_heads * HD
    ff_width = FF // model_count
    qkv_cols = query_width + 2 * kv_width
    out_end = qkv_cols + query_width
    in_pairs = data_count == 8
    parts = data_count if in_pairs else 1
    outs = 2 if in_pairs else 1
    gain_attn = gains[:model_width]
    gain_mlp = gains[model_width : 2 * model_width]
    head_gains = gains[2 * model_width :].reshape(2, HD)

    qkv_own = weights[:, :qkv_cols].astype(bf16)
    if in_pairs:
        qkv_outer = gather_chips(qkv_own)
        later, qkv_own = lax.optimization_barrier((weights, qkv_own))
        out_outer = gather_chips(later[:, qkv_cols:out_end].astype(bf16))
    else:
        later = weights
        qkv_parts = [lax.all_gather(qkv_own, "dp", axis=0, tiled=True)]
        out_own = weights[:, qkv_cols:out_end].astype(bf16)
        out_parts = [lax.all_gather(out_own, "dp", axis=0, tiled=True)]

    doc_ids = jnp.arange(doc_lengths.shape[1], dtype=jnp.int32)
    earlier = doc_ids[None, :] < doc_ids[:, None]
    starts = jnp.sum(jnp.where(earlier[None], doc_lengths[:, None, :], 0), axis=2)
    starts = starts + seq_len * jnp.arange(doc_lengths.shape[0], dtype=jnp.int32)[:, None]
    starts = starts.reshape(doc_total)
    span_ids = jnp.arange(span_total, dtype=jnp.int32)
    inverse = jnp.sum(jnp.where(span_order[None, :] == span_ids[:, None], span_ids[None, :], 0), axis=1)
    if in_pairs:
        inverse = ((inverse // span_own) ^ me) * span_own + inverse % span_own
    own_spans = lax.dynamic_slice(span_order, (me * span_own,), (span_own,))
    home = (own_spans[:, None] * SPAN + jnp.arange(SPAN, dtype=jnp.int32)[None, :]).reshape(tok_count)
    doc_start = jnp.max(jnp.where(starts[None, :] <= home[:, None], starts[None, :], 0), axis=1)
    freqs = rope_base ** (-(2.0 * (jnp.arange(HD, dtype=jnp.int32) % (HD // 2)).astype(f32)) / HD)
    angles = (home - doc_start).astype(f32)[:, None] * freqs[None, :]
    cosine = jnp.cos(angles)
    sine = jnp.sin(angles) * jnp.where(jnp.arange(HD) < HD // 2, -1.0, 1.0)[None, :]

    inputs = block_input.astype(f32)
    scale_in = unit_scale(inputs)
    normed_low = (inputs * scale_in * gain_attn).astype(bf16)

    normed_turned = transposed(me_array, normed_low, parts, row_count)
    if in_pairs:
        normed_turned, qkv_outer[1] = lax.optimization_barrier((normed_turned, qkv_outer[1]))
        qkv_parts = gather_cores(qkv_outer)

    q_tiles = query_width // TILE
    rows_all = pl.BlockSpec((tok_count, model_width), lambda *_: (0, 0))
    angle_spec = pl.BlockSpec((tok_count, HD), lambda *_: (0, 0))
    part_tile = pl.BlockSpec((model_width // parts, TILE), lambda n, *_: (0, n))
    queries, keys_values, lin = pl.pallas_call(
        functools.partial(project_kernel, parts, q_tiles),
        grid_spec=pltpu.PrefetchScalarGridSpec(
            num_scalar_prefetch=1,
            grid=(qkv_cols // TILE,),
            in_specs=[rows_all]
            + [part_tile] * parts
            + [angle_spec, angle_spec, pl.BlockSpec((2, HD), lambda *_: (0, 0))],
            out_specs=[
                pl.BlockSpec((tok_count, TILE), lambda n, *_: (0, jnp.minimum(n, q_tiles - 1))),
                pl.BlockSpec((tok_count, TILE), lambda n, *_: (0, jnp.maximum(n - q_tiles, 0))),
                pl.BlockSpec((tok_count, TILE), lambda n, *_: (0, jnp.minimum(n, q_tiles))),
            ],
            scratch_shapes=[pltpu.VMEM((model_width, TILE), bf16)],
        ),
        out_shape=(
            jax.ShapeDtypeStruct((tok_count, query_width), bf16),
            jax.ShapeDtypeStruct((tok_count, 2 * kv_width), bf16),
            jax.ShapeDtypeStruct((tok_count, query_width + kv_width), f32),
        ),
        compiler_params=params(),
        cost_estimate=cost(6),
        name="project",
    )(me_array, normed_low, *qkv_parts, cosine, sine, head_gains)

    mlp_own = later[:, out_end:].astype(bf16)
    if in_pairs:
        keys_values, out_outer = lax.optimization_barrier((keys_values, out_outer))
        kv_parts = gather_cores(gather_chips(keys_values))
        out_parts = gather_cores(out_outer)
        mlp_own, out_parts, kv_parts = lax.optimization_barrier((mlp_own, out_parts, kv_parts))
    else:
        kv_parts = [lax.all_gather(keys_values, "dp", axis=0, tiled=True)]
    mlp_weights = lax.all_gather(mlp_own, "dp", axis=0, tiled=True)

    heads = kv_heads if in_pairs else 1
    head_steps = kv_heads // heads
    wide = group * SPAN
    anywhere = pl.BlockSpec(memory_space=pl.ANY)
    head_spec = pl.BlockSpec((tok_count, heads * group * HD), lambda g, *_: (0, g))
    q_all = pl.BlockSpec((tok_count, query_width), lambda *_: (0, 0))
    turned_spec = pl.BlockSpec((span_own * heads, HD, wide), lambda g, *_: (g, 0, 0))
    lse_spec = pl.BlockSpec((span_own * heads, 8, wide), lambda g, *_: (g, 0, 0))
    attended, attended_low, lse = pl.pallas_call(
        functools.partial(attend_kernel, group, heads, parts),
        grid_spec=pltpu.PrefetchScalarGridSpec(
            num_scalar_prefetch=3,
            grid=(head_steps,),
            in_specs=[head_spec] + [anywhere] * parts,
            out_specs=[turned_spec, q_all, lse_spec],
            scratch_shapes=[
                pltpu.VMEM((token_total, 2 * kv_width), bf16),
                pltpu.SemaphoreType.DMA((parts,)),
            ],
        ),
        out_shape=(
            jax.ShapeDtypeStruct((span_own * kv_heads, HD, wide), f32),
            jax.ShapeDtypeStruct((tok_count, query_width), bf16),
            jax.ShapeDtypeStruct((span_own * kv_heads, 8, wide), f32),
        ),
        compiler_params=params(),
        cost_estimate=cost(16),
        name="attend",
    )(own_spans, inverse, starts, queries, *kv_parts)
    part_all = pl.BlockSpec((model_width // parts, query_width), lambda *_: (0, 0))
    attn_part = pl.pallas_call(
        functools.partial(project_out_kernel, parts),
        grid_spec=pltpu.PrefetchScalarGridSpec(
            num_scalar_prefetch=1,
            grid=(1,),
            in_specs=[q_all] + [part_all] * parts,
            out_specs=rows_all,
        ),
        out_shape=jax.ShapeDtypeStruct((tok_count, model_width), bf16),
        compiler_params=params(),
        cost_estimate=cost(4),
        name="project_out",
    )(me_array, attended_low, *out_parts)

    attn_sum = lax.psum(attn_part, "mp")

    tiles = ff_width // TILE
    gain_spec = pl.BlockSpec((1, model_width), lambda *_: (0, 0))
    tile_spec = pl.BlockSpec((tok_count, TILE), lambda n: (0, n))
    hidden_shape = jax.ShapeDtypeStruct((tok_count, ff_width), bf16)
    low_shape = jax.ShapeDtypeStruct((tok_count, model_width), bf16)
    wide_shape = jax.ShapeDtypeStruct((tok_count, model_width), f32)
    scale_spec = pl.BlockSpec((tok_count, 1), lambda *_: (0, 0))
    scale_shape = jax.ShapeDtypeStruct((tok_count, 1), f32)
    grad_hidden = pl.pallas_call(
        plain_kernel,
        grid=(tiles,),
        in_specs=[rows_all, pl.BlockSpec((model_width, TILE), lambda n: (0, n + 2 * tiles))],
        out_specs=tile_spec,
        out_shape=hidden_shape,
        compiler_params=params(),
        cost_estimate=cost(30),
        name="grad_hidden",
    )(cotangent, mlp_weights)
    residual, mlp_low, scale_mlp, grad_gate, grad_up, hidden_low = pl.pallas_call(
        mlp_kernel,
        grid=(tiles,),
        in_specs=[
            rows_all,
            rows_all,
            gain_spec,
            pl.BlockSpec((model_width, TILE), lambda n: (0, n)),
            pl.BlockSpec((model_width, TILE), lambda n: (0, n + tiles)),
            tile_spec,
        ],
        out_specs=[rows_all, rows_all, scale_spec, tile_spec, tile_spec, tile_spec],
        out_shape=(wide_shape, low_shape, scale_shape, hidden_shape, hidden_shape, hidden_shape),
        compiler_params=params(),
        cost_estimate=cost(18),
        name="mlp",
    )(block_input, attn_sum, gain_mlp[None], mlp_weights, mlp_weights, grad_hidden)

    hidden_all = pl.BlockSpec((tok_count, ff_width), lambda n: (0, 0))
    out_tile = pl.BlockSpec((tok_count, 512), lambda n: (0, n))
    grad_mlp_part = pl.pallas_call(
        mlp_back_kernel,
        grid=(model_width // WIDE,),
        in_specs=[
            hidden_all,
            hidden_all,
            pl.BlockSpec((WIDE, ff_width), lambda n: (n, 0)),
            pl.BlockSpec((WIDE, ff_width), lambda n: (n, 1)),
        ],
        out_specs=out_tile,
        out_shape=low_shape,
        compiler_params=params(),
        cost_estimate=cost(11),
        name="mlp_back",
    )(grad_gate, grad_up, mlp_weights, mlp_weights)
    grad_mlp_part, mlp_low, hidden_low = lax.optimization_barrier((grad_mlp_part, mlp_low, hidden_low))
    grad_mlp_sum = lax.psum(grad_mlp_part, "mp")

    row_tile = pl.BlockSpec((tok_count, TILE), lambda n: (0, n))
    dw_mlp = pl.pallas_call(
        mlp_weight_grad_kernel,
        grid=(model_width // TILE,),
        in_specs=[row_tile, row_tile, hidden_all, hidden_all, hidden_all],
        out_specs=pl.BlockSpec((TILE, 3 * ff_width), lambda n: (n, 0)),
        out_shape=jax.ShapeDtypeStruct((model_width, 3 * ff_width), bf16),
        compiler_params=params(),
        cost_estimate=cost(1),
        name="mlp_weight_grad",
    )(mlp_low, cotangent, grad_gate, grad_up, hidden_low)
    mlp_part = pl.pallas_call(
        rows_by_rows_kernel,
        grid=(model_width // 512,),
        in_specs=[hidden_all, pl.BlockSpec((512, ff_width), lambda n: (n, 2))],
        out_specs=out_tile,
        out_shape=low_shape,
        compiler_params=params(),
        cost_estimate=cost(1),
        name="mlp_out",
    )(hidden_low, mlp_weights)
    mlp_grads = lax.psum_scatter(dw_mlp, "dp", scatter_dimension=0, tiled=True)
    grad_mlp_sum, mlp_part, dw_mlp = lax.optimization_barrier((grad_mlp_sum, mlp_part, dw_mlp))
    mlp_sum = lax.psum(mlp_part, "mp")

    half_rows = tok_count // 2
    half_spec = pl.BlockSpec((half_rows, model_width), lambda n, *_: (n, 0))
    grad_residual, grad_res_low, grad_att_low, mlp_gain_grad = pl.pallas_call(
        functools.partial(residual_back_kernel, parts, 1.0 / model_count),
        grid_spec=pltpu.PrefetchScalarGridSpec(
            num_scalar_prefetch=1,
            grid=(2,),
            in_specs=[
                half_spec,
                pl.BlockSpec((half_rows, 1), lambda n, *_: (n, 0)),
                half_spec,
                half_spec,
                gain_spec,
            ]
            + [pl.BlockSpec((model_width // parts, query_width), lambda *_: (0, 0))] * parts,
            out_specs=[half_spec, half_spec, pl.BlockSpec((half_rows, query_width), lambda n, *_: (n, 0)), gain_spec],
            scratch_shapes=[pltpu.VMEM((model_width, query_width), bf16)],
        ),
        out_shape=(
            wide_shape,
            low_shape,
            jax.ShapeDtypeStruct((tok_count, query_width), bf16),
            jax.ShapeDtypeStruct((1, model_width), f32),
        ),
        compiler_params=params(),
        cost_estimate=cost(1),
        name="residual_back",
    )(me_array, residual, scale_mlp, cotangent, grad_mlp_sum, gain_mlp[None], *out_parts)
    out_rows = token_total // parts
    dkv_spec = pl.BlockSpec((out_rows, 2 * heads * HD), lambda g, *_: (0, g))
    back = pl.pallas_call(
        functools.partial(attend_back_kernel, group, heads, parts, parts),
        grid_spec=pltpu.PrefetchScalarGridSpec(
            num_scalar_prefetch=3,
            grid=(head_steps,),
            in_specs=[head_spec]
            + [anywhere] * parts
            + [head_spec, turned_spec, lse_spec, head_spec]
            + [angle_spec, angle_spec, pl.BlockSpec((1, HD), lambda *_: (0, 0))],
            out_specs=[head_spec, pl.BlockSpec((8, HD), lambda g, *_: (g, 0))] + [dkv_spec] * parts,
            scratch_shapes=[
                pltpu.VMEM((token_total, 2 * kv_width), bf16),
                pltpu.VMEM((token_total, 2 * heads * HD), f32),
                pltpu.SemaphoreType.DMA((parts,)),
            ],
        ),
        out_shape=[
            jax.ShapeDtypeStruct((tok_count, query_width), bf16),
            jax.ShapeDtypeStruct((8 * head_steps, HD), f32),
        ]
        + [jax.ShapeDtypeStruct((out_rows, 2 * kv_width), bf16)] * parts,
        compiler_params=params(),
        cost_estimate=cost(1),
        name="attend_back",
    )(
        own_spans,
        inverse,
        starts,
        queries,
        *kv_parts,
        grad_att_low,
        attended,
        lse,
        lin,
        cosine,
        sine,
        head_gains[:1],
    )
    grad_query_low, query_gain_grad = back[:2]
    query_gain_grad = jnp.sum(query_gain_grad, axis=0) / 8.0
    if in_pairs:
        came = [swap(back[2 + k], "dp", 1) for k in range(1, parts, 2)]
        halves = [add_pair(back[2 + 2 * k], came[k]) for k in range(parts // 2)]
        halves, mlp_grads = lax.optimization_barrier((halves, mlp_grads))
        terms = [halves[0]] + [swap(halves[k], "dp", 2 * k) for k in range(1, parts // 2)]
    else:
        terms = [lax.psum_scatter(back[2], "dp", scatter_dimension=0, tiled=True)]

    [dw_query] = weight_grad(me_array, normed_turned, [grad_query_low], parts, row_count, True)
    [dw_out] = weight_grad(me_array, grad_res_low, [attended_low], parts, row_count)

    def scattered(made):
        if in_pairs:
            return sum(term.astype(f32) for term in scatter_small(*made)).astype(bf16)
        whole = made[0].reshape(model_width, -1)
        return lax.psum_scatter(whole, "dp", scatter_dimension=0, tiled=True)

    block_output = (residual + mlp_sum.astype(f32)).astype(bf16)
    terms, block_output, dw_query, dw_out = lax.optimization_barrier((terms, block_output, dw_query, dw_out))
    query_grads, out_grads = scattered(dw_query), scattered(dw_out)
    grad_kv_low, key_gain_grad, attn_gain_grad, grad_norm_part = pl.pallas_call(
        functools.partial(key_back_kernel, parts, len(terms), kv_heads),
        grid_spec=pltpu.PrefetchScalarGridSpec(
            num_scalar_prefetch=1,
            grid=(1,),
            in_specs=[pl.BlockSpec((tok_count, 2 * kv_width), lambda *_: (0, 0))] * len(terms)
            + [pl.BlockSpec((tok_count, kv_width), lambda *_: (0, query_width // kv_width))]
            + [angle_spec, angle_spec, pl.BlockSpec((1, HD), lambda *_: (0, 0))]
            + [q_all, rows_all, scale_spec]
            + [pl.BlockSpec((model_width // parts, qkv_cols), lambda *_: (0, 0))] * parts,
            out_specs=[
                pl.BlockSpec((tok_count, 2 * kv_width), lambda *_: (0, 0)),
                pl.BlockSpec((8, HD), lambda *_: (0, 0)),
                gain_spec,
                rows_all,
            ],
        ),
        out_shape=[
            jax.ShapeDtypeStruct((tok_count, 2 * kv_width), bf16),
            jax.ShapeDtypeStruct((8, HD), f32),
            jax.ShapeDtypeStruct((1, model_width), f32),
            low_shape,
        ],
        compiler_params=params(),
        cost_estimate=cost(1),
        name="key_back",
    )(me_array, *terms, lin, cosine, sine, head_gains[1:], grad_query_low, block_input, scale_in, *qkv_parts)
    [dw_kv] = weight_grad(me_array, normed_turned, [grad_kv_low], parts, row_count, True)

    grad_norm_share = lax.psum_scatter(grad_norm_part, "mp", scatter_dimension=0, tiled=True)
    weight_grads = [query_grads, scattered(dw_kv), out_grads, mlp_grads]
    square = sum(jnp.sum(jnp.square(grad.astype(f32))) for grad in weight_grads)
    square, grad_norm_share = lax.optimization_barrier((square, grad_norm_share))
    grad_norm_sum = lax.all_gather(grad_norm_share, "mp", axis=0, tiled=True)
    local = [attn_gain_grad[0], mlp_gain_grad[0], query_gain_grad, key_gain_grad[0]]
    totals = sum_all(jnp.concatenate([jnp.broadcast_to(square, (HD,))] + local))
    square_total, gain_grads = totals[0], totals[HD:]
    grad_norm = jnp.sqrt(square_total + jnp.sum(gain_grads * gain_grads))
    factor = 1.0 / jnp.maximum(grad_norm, 1.0)
    new_weights, new_momentum, new_ema = update_weights(factor[None], weights, momentum, ema_weights, weight_grads)
    eighth = tok_count // 8
    eighth_spec = pl.BlockSpec((eighth, model_width), lambda n: (n, 0))
    grad_input = pl.pallas_call(
        input_back_kernel,
        grid=(8,),
        in_specs=[
            eighth_spec,
            eighth_spec,
            pl.BlockSpec((eighth, 1), lambda n: (n, 0)),
            eighth_spec,
            gain_spec,
        ],
        out_specs=eighth_spec,
        out_shape=wide_shape,
        compiler_params=params(),
        cost_estimate=cost(8),
        name="input_back",
    )(grad_residual, block_input, scale_in, grad_norm_sum, gain_attn[None])
    new_gains, new_gain_momentum, new_gain_ema = update(gains, gain_momentum, gain_ema, gain_grads, factor, gain_rate)
    return (
        block_output,
        grad_input,
        grad_norm,
        new_weights,
        new_momentum,
        new_ema,
        new_gains,
        new_gain_momentum,
        new_gain_ema,
    )


def solution(mesh):
    return jax.shard_map(
        per_device,
        mesh=mesh,
        in_specs=(
            P("dp", None),
            P("dp", None),
            P(),
            P(),
            P("dp", "mp"),
            P("dp", "mp"),
            P("dp", "mp"),
            P(),
            P(),
            P(),
        ),
        out_specs=(
            P("dp", None),
            P("dp", None),
            P(),
            P("dp", "mp"),
            P("dp", "mp"),
            P("dp", "mp"),
            P(),
            P(),
            P(),
        ),
        check_vma=False,
    )
```

```python
import functools

import jax
import jax.numpy as jnp
from jax import lax
from jax.experimental import pallas as pl
from jax.experimental.pallas import tpu as pltpu
from jax.sharding import PartitionSpec as P

HEADS = 16
KV = 8
HD = 128
FF = 6144
SPAN = 128
CHUNK = 4
TILE = 256
WIDE = 512
VMEM_LIMIT = 60 * 1024 * 1024

eps_norm = 1e-06
rope_base = 1000000.0
learn_rate = 100.0
gain_rate = 4000.0
momentum_decay = 0.5
average_decay = 0.5
score_scale = HD ** (-0.5)
far = -1e30

bf16 = jnp.bfloat16
f32 = jnp.float32
plain_dims = (((1,), (0,)), ((), ()))
last_dims = (((1,), (1,)), ((), ()))
first_dims = (((0,), (0,)), ((), ()))


def dot(a, b, dims=plain_dims):
    return lax.dot_general(a, b, dims, preferred_element_type=f32)


def cost(micros):
    return pl.CostEstimate(flops=int(micros * 1.0e9), bytes_accessed=int(micros * 3.4e6), transcendentals=0)


def params(**more):
    return pltpu.CompilerParams(vmem_limit_bytes=VMEM_LIMIT, **more)


def swap(array, axis, distance):
    count = lax.axis_size(axis)
    return lax.ppermute(array, axis, [(i, i ^ distance) for i in range(count)])


def gather_chips(own):
    return [own] + [swap(own, "dp", k) for k in (2, 4, 6)]


def gather_cores(outer):
    inner = [swap(block, "dp", 1) for block in outer]
    return [block for pair in zip(outer, inner) for block in pair]


def scatter_small(even, odd):
    came = swap(odd, "dp", 1)
    half = (even.astype(f32) + came.astype(f32)).astype(bf16)
    return [half[0]] + [swap(half[k], "dp", 2 * k) for k in (1, 2, 3)]


def add_pair(a, b):
    return (a.astype(f32) + b.astype(f32)).astype(bf16)


def sum_all(value):
    for axis in ("dp", "mp"):
        distance = 1
        while distance < lax.axis_size(axis):
            value = value + swap(value, axis, distance)
            distance *= 2
    return value


def place_of(me_ref, k, parts):
    return me_ref[0] ^ k if parts > 1 else 0


def in_order(me_ref, part_refs, whole_ref):
    parts = len(part_refs)
    rows = part_refs[0].shape[0]
    for k, ref in enumerate(part_refs):
        at = pl.multiple_of(place_of(me_ref, k, parts) * rows, rows)
        whole_ref[pl.ds(at, rows), :] = ref[...]


def turned(normed, cosine, sine):
    return normed * cosine + pltpu.roll(normed, HD // 2, 1) * sine


def turned_back(gradient, cosine, sine):
    return gradient * cosine + pltpu.roll(gradient * sine, HD // 2, 1)


def unit_scale(values):
    return lax.rsqrt(jnp.mean(values * values, axis=-1, keepdims=True) + eps_norm)


def norm_back(unit, scale, gain, gradient):
    e = gradient * gain
    return scale * (e - unit * jnp.mean(e * unit, axis=-1, keepdims=True))


def project_kernel(parts, heads, me_ref, h_ref, *refs):
    cos_ref, sin_ref, gain_ref, o_ref, lin_ref, w_ref = refs[parts:]
    in_order(me_ref, refs[:parts], w_ref)
    total = dot(h_ref[...], w_ref[...])
    for head in range(heads):
        at = slice(head * HD, (head + 1) * HD)
        values = total[:, at]
        lin_ref[:, at] = values
        normed = values * unit_scale(values) * gain_ref[...]
        o_ref[:, at] = turned(normed, cos_ref[...], sin_ref[...]).astype(bf16)
    if heads * HD < o_ref.shape[1]:
        o_ref[:, heads * HD :] = total[:, heads * HD :].astype(bf16)


def span_limits(own_ref, starts_ref, i, group):
    span = own_ref[i]
    first = span * SPAN
    lane = lax.broadcasted_iota(jnp.int32, (1, group * SPAN), 1)
    places = first + (lane & (SPAN - 1))
    low = jnp.int32(0)
    begin = jnp.zeros((1, group * SPAN), jnp.int32)
    for d in range(starts_ref.shape[0]):
        start = starts_ref[d]
        low = jnp.maximum(low, jnp.where(start <= first, start, 0))
        begin = jnp.maximum(begin, jnp.where(start <= places, start, 0))
    return span, low // SPAN, places, begin


def key_rows(inverse_ref, newest, b):
    return pl.multiple_of(inverse_ref[jnp.maximum(newest - b, 0)] * SPAN, SPAN)


def allowed_keys(newest, places, begin):
    row = lax.broadcasted_iota(jnp.int32, (CHUNK * SPAN, 1), 0)
    key = newest * SPAN + (row & (SPAN - 1)) - (row & ~(SPAN - 1))
    return (key <= places) & (key >= begin)


def stacked(ref, i, head, group):
    rows = pl.ds(i * SPAN, SPAN)
    return jnp.concatenate([ref[rows, h * HD : (h + 1) * HD] for h in range(head * group, (head + 1) * group)], axis=0)


def head_columns(first, heads, kv_heads):
    keys = [pl.ds(pl.multiple_of((first + h) * HD, HD), HD) for h in range(heads)]
    values = [pl.ds(pl.multiple_of((first + h + kv_heads) * HD, HD), HD) for h in range(heads)]
    return keys, values


def load_parts(part_refs, target_ref, sem_ref, first):
    rows = part_refs[0].shape[0]
    return [
        pltpu.make_async_copy(ref, target_ref.at[pl.ds(k * rows, rows)], sem_ref.at[first + k])
        for k, ref in enumerate(part_refs)
    ]


def attend_kernel(group, heads, parts, own_ref, inverse_ref, starts_ref, q_ref, *refs):
    kv_parts = refs[:parts]
    turned_ref, low_ref, lse_ref, kv_ref, sem_ref = refs[parts:]
    g = pl.program_id(0)
    kv_heads = pl.num_programs(0) * heads
    kv_copies = load_parts(kv_parts, kv_ref, sem_ref, 0)

    @pl.when(g == 0)
    def _():
        for copy in kv_copies:
            copy.start()
        for copy in kv_copies:
            copy.wait()

    key_at, value_at = head_columns(g * heads, heads, kv_heads)
    wide = group * SPAN
    for i in range(own_ref.shape[0]):
        span, low, places, begin = span_limits(own_ref, starts_ref, i, group)
        queries = [stacked(q_ref, i, h, group) for h in range(heads)]
        count = (span - low) // CHUNK + 1

        def step(c, carry):
            newest = span - c * CHUNK
            at = [key_rows(inverse_ref, newest, b) for b in range(CHUNK)]
            allowed = allowed_keys(newest, places, begin)
            made = []
            for h, (top, weight, total) in enumerate(carry):
                keys = jnp.concatenate([kv_ref[pl.ds(a, SPAN), key_at[h]] for a in at], axis=0)
                values = jnp.concatenate([kv_ref[pl.ds(a, SPAN), value_at[h]] for a in at], axis=0)
                scores = jnp.where(allowed, dot(keys, queries[h], last_dims), far)
                new_top = jnp.maximum(top, jnp.max(scores, axis=0, keepdims=True))
                probs = jnp.exp((scores - new_top) * score_scale)
                shrink = jnp.exp((top - new_top) * score_scale)
                weight = weight * shrink + jnp.sum(probs, axis=0, keepdims=True)
                total = total * shrink + dot(values, probs.astype(bf16), first_dims)
                made.append((new_top, weight, total))
            return tuple(made)

        start = (jnp.full((1, wide), far, f32), jnp.zeros((1, wide), f32), jnp.zeros((HD, wide), f32))
        made = lax.fori_loop(0, count, step, (start,) * heads)
        for h, (top, weight, total) in enumerate(made):
            output = total / weight
            place = i * heads + h
            turned_ref[place] = output
            lse_ref[place] = jnp.broadcast_to(top * score_scale + jnp.log(weight), (8, wide))
            back = output.T.astype(bf16)
            for k in range(group):
                column = pl.multiple_of(((g * heads + h) * group + k) * HD, HD)
                low_ref[pl.ds(i * SPAN, SPAN), pl.ds(column, HD)] = back[k * SPAN : (k + 1) * SPAN]


def project_out_kernel(parts, me_ref, low_ref, *refs):
    out_parts = refs[:parts]
    o_ref = refs[parts]
    width = out_parts[0].shape[0]
    block = min(width, TILE)
    for k, w_ref in enumerate(out_parts):
        first = place_of(me_ref, k, parts) * width
        for b in range(width // block):
            at = pl.multiple_of(first + b * block, block)
            term = dot(low_ref[...], w_ref[b * block : (b + 1) * block], last_dims)
            o_ref[:, pl.ds(at, block)] = term.astype(bf16)


def output_first_kernel(y_ref, s_ref, o_ref):
    o_ref[...] = (y_ref[...] + s_ref[...].astype(f32)).astype(bf16)


def output_rest_kernel(y_ref, s_ref, made_ref, o_ref):
    o_ref[...] = (y_ref[...] + s_ref[...].astype(f32)).astype(bf16)


def plain_kernel(a_ref, w_ref, o_ref):
    o_ref[...] = dot(a_ref[...], w_ref[...]).astype(bf16)


def mlp_kernel(x_ref, s_ref, gain_ref, wg_ref, wu_ref, da_ref, y_ref, h_ref, scale_ref, dg_ref, du_ref, a_ref):
    @pl.when(pl.program_id(0) == 0)
    def _():
        def rows_of(r, unused):
            at = pl.ds(pl.multiple_of(r * 64, 64), 64)
            y = x_ref[at, :].astype(f32) + s_ref[at, :].astype(f32)
            y_ref[at, :] = y
            scale = unit_scale(y)
            scale_ref[at, :] = scale
            h_ref[at, :] = (y * scale * gain_ref[...]).astype(bf16)
            return unused

        lax.fori_loop(0, x_ref.shape[0] // 64, rows_of, 0, unroll=2)

    hidden = h_ref[...]
    gate = dot(hidden, wg_ref[...])
    up = dot(hidden, wu_ref[...])
    grad = da_ref[...].astype(f32)
    sig = 1.0 / (1.0 + jnp.exp(-gate))
    silu = gate * sig
    a_ref[...] = (silu * up).astype(bf16)
    dg_ref[...] = (grad * up * (sig + silu * (1.0 - sig))).astype(bf16)
    du_ref[...] = (grad * silu).astype(bf16)


def mlp_back_kernel(dg_ref, du_ref, wg_ref, wu_ref, dh_ref):
    dh_ref[...] = (dot(dg_ref[...], wg_ref[...], last_dims) + dot(du_ref[...], wu_ref[...], last_dims)).astype(bf16)


def rows_by_rows_kernel(a_ref, w_ref, o_ref):
    o_ref[...] = dot(a_ref[...], w_ref[...], last_dims).astype(bf16)


def residual_back_kernel(parts, share, me_ref, y_ref, scale_ref, c_ref, s_ref, gain_ref, *refs):
    dy_ref, low_ref, do_ref, dgain_ref, w_ref = refs[parts:]

    @pl.when(pl.program_id(0) == 0)
    def _():
        dgain_ref[...] = jnp.zeros_like(dgain_ref)
        in_order(me_ref, refs[:parts], w_ref)

    def rows_of(r, dgain):
        at = pl.ds(pl.multiple_of(r * 32, 32), 32)
        scale = scale_ref[at, :]
        unit = y_ref[at, :] * scale
        grad = s_ref[at, :].astype(f32)
        dy = c_ref[at, :].astype(f32) + norm_back(unit, scale, gain_ref[...], grad)
        dy_ref[at, :] = dy
        low_ref[at, :] = dy.astype(bf16)
        return dgain + jnp.sum(grad * unit, axis=0, keepdims=True)

    zeros = jnp.zeros(dgain_ref.shape, f32)
    dgain_ref[...] += share * lax.fori_loop(0, y_ref.shape[0] // 32, rows_of, zeros, unroll=2)
    do_ref[...] = dot(low_ref[...], w_ref[...]).astype(bf16)


def attend_back_kernel(group, heads, parts, outs, own_ref, inverse_ref, starts_ref, q_ref, *refs):
    kv_parts = refs[:parts]
    do_ref, turned_ref, lse_ref, lin_ref, cos_ref, sin_ref, gain_ref = refs[parts : parts + 7]
    dq_ref, dgain_ref = refs[parts + 7 : parts + 9]
    dkv_refs = refs[parts + 9 : parts + 9 + outs]
    kv_ref, acc_ref, sem_ref = refs[parts + 9 + outs :]
    g = pl.program_id(0)
    kv_heads = pl.num_programs(0) * heads
    copies = load_parts(kv_parts, kv_ref, sem_ref, 0)

    @pl.when(g == 0)
    def _():
        for copy in copies:
            copy.start()

    acc_ref[...] = jnp.zeros_like(acc_ref)

    @pl.when(g == 0)
    def _():
        for copy in copies:
            copy.wait()

    key_at, value_at = head_columns(g * heads, heads, kv_heads)
    wide = group * SPAN
    dgain = jnp.zeros((1, HD), f32)
    for i in range(own_ref.shape[0]):
        span, low, places, begin = span_limits(own_ref, starts_ref, i, group)
        queries = [stacked(q_ref, i, h, group) for h in range(heads)]
        grads = [stacked(do_ref, i, h, group) for h in range(heads)]
        deltas = [
            jnp.sum(grads[h].astype(f32).T * turned_ref[i * heads + h], axis=0, keepdims=True) for h in range(heads)
        ]
        lses = [lse_ref[i * heads + h, :1] for h in range(heads)]
        count = (span - low) // CHUNK + 1

        def step(c, carry):
            newest = span - c * CHUNK
            at = [key_rows(inverse_ref, newest, b) for b in range(CHUNK)]
            allowed = allowed_keys(newest, places, begin)
            made = []
            for h, grad_query in enumerate(carry):
                keys = jnp.concatenate([kv_ref[pl.ds(a, SPAN), key_at[h]] for a in at], axis=0)
                values = jnp.concatenate([kv_ref[pl.ds(a, SPAN), value_at[h]] for a in at], axis=0)
                scores = dot(keys, queries[h], last_dims) * score_scale
                probs = jnp.exp(jnp.where(allowed, scores - lses[h], far))
                grad_probs = dot(values, grads[h], last_dims)
                grad_scores = (probs * (grad_probs - deltas[h])).astype(bf16)
                grad_values = dot(probs.astype(bf16), grads[h])
                grad_keys = dot(grad_scores, queries[h]) * score_scale
                left = 2 * h * HD
                for b, a in enumerate(at):
                    rows = slice(b * SPAN, (b + 1) * SPAN)
                    acc_ref[pl.ds(a, SPAN), left : left + HD] += grad_keys[rows]
                    acc_ref[pl.ds(a, SPAN), left + HD : left + 2 * HD] += grad_values[rows]
                made.append(grad_query + dot(keys, grad_scores, first_dims))
            return tuple(made)

        made = lax.fori_loop(0, count, step, (jnp.zeros((HD, wide), f32),) * heads)
        place = pl.ds(i * SPAN, SPAN)
        for h, grad_query in enumerate(made):
            grad_query = (grad_query * score_scale).T
            for k in range(group):
                at = slice((h * group + k) * HD, (h * group + k + 1) * HD)
                back = turned_back(grad_query[k * SPAN : (k + 1) * SPAN], cos_ref[place, :], sin_ref[place, :])
                lin = lin_ref[place, at]
                scale = unit_scale(lin)
                unit = lin * scale
                dgain = dgain + jnp.sum(back * unit, axis=0, keepdims=True)
                dq_ref[place, at] = norm_back(unit, scale, gain_ref[...], back).astype(bf16)
    dgain_ref[...] = jnp.broadcast_to(dgain, dgain_ref.shape)

    rows = acc_ref.shape[0] // parts
    for k in range(parts):
        dkv_refs[k % outs][pl.ds((k // outs) * rows, rows), :] = acc_ref[pl.ds(k * rows, rows), :].astype(bf16)


def key_back_kernel(parts, terms, kv_heads, me_ref, *refs):
    term_refs = refs[:terms]
    lin_ref, cos_ref, sin_ref, gain_ref, dq_ref, x_ref, scale_ref = refs[terms : terms + 7]
    wq_refs = refs[terms + 7 : terms + 7 + parts]
    wkv_refs = refs[terms + 7 + parts : terms + 7 + 2 * parts]
    dkv_ref, dgain_k_ref, dgain_ref, dh_ref = refs[terms + 7 + 2 * parts :]
    dgain = jnp.zeros((1, HD), f32)

    def total(begin):
        value = None
        for ref in term_refs:
            term = ref[:, begin : begin + HD].astype(f32)
            value = term if value is None else value + term
        return value

    for g in range(kv_heads):
        at = slice(g * HD, (g + 1) * HD)
        back = turned_back(total(2 * g * HD), cos_ref[...], sin_ref[...])
        lin = lin_ref[:, at]
        scale = unit_scale(lin)
        unit = lin * scale
        dgain = dgain + jnp.sum(back * unit, axis=0, keepdims=True)
        dkv_ref[:, at] = norm_back(unit, scale, gain_ref[...], back).astype(bf16)
        dkv_ref[:, (kv_heads + g) * HD : (kv_heads + g + 1) * HD] = total((2 * g + 1) * HD).astype(bf16)
    dgain_k_ref[...] = jnp.broadcast_to(dgain, dgain_k_ref.shape)

    scale = scale_ref[...]
    width = wq_refs[0].shape[0]
    block = min(width, TILE)
    for k in range(parts):
        first = place_of(me_ref, k, parts) * width
        for b in range(width // block):
            here = pl.ds(pl.multiple_of(first + b * block, block), block)
            rows = slice(b * block, (b + 1) * block)
            term = dot(dq_ref[...], wq_refs[k][rows, :], last_dims)
            term = term + dot(dkv_ref[...], wkv_refs[k][rows, :], last_dims)
            dh_ref[:, here] = term.astype(bf16)
            unit = x_ref[:, here].astype(f32) * scale
            dgain_ref[:, here] = jnp.sum(term * unit, axis=0, keepdims=True)


def input_back_kernel(dy_ref, x_ref, scale_ref, s_ref, gain_ref, o_ref):
    def rows_of(r, unused):
        at = pl.ds(pl.multiple_of(r * 16, 16), 16)
        scale = scale_ref[at, :]
        back = norm_back(x_ref[at, :].astype(f32) * scale, scale, gain_ref[...], s_ref[at, :].astype(f32))
        o_ref[at, :] = dy_ref[at, :] + back
        return unused

    lax.fori_loop(0, x_ref.shape[0] // 16, rows_of, 0, unroll=4)


def transpose_kernel(me_ref, x_ref, o_ref):
    o_ref[...] = x_ref[...].T


def transposed(me, lhs, parts, rows):
    tokens, depth = lhs.shape
    rows = rows if parts > 1 else TILE
    return pl.pallas_call(
        transpose_kernel,
        grid_spec=pltpu.PrefetchScalarGridSpec(
            num_scalar_prefetch=1,
            grid=(depth // rows,),
            in_specs=[pl.BlockSpec((tokens, rows), weight_source(parts, depth // rows))],
            out_specs=pl.BlockSpec((rows, tokens), lambda p, _: (p, 0)),
        ),
        out_shape=jax.ShapeDtypeStruct((depth, tokens), bf16),
        compiler_params=params(),
        cost_estimate=cost(5),
        name="transposed",
    )(me, lhs)


def weight_source(parts, steps):
    half = steps // 2

    def source(p, me_ref):
        return (0, me_ref[0] ^ (2 * (p % half) + p // half)) if parts > 1 else (0, p)

    return source


def weight_grad_kernel(outs, count, me_ref, lhs_ref, *refs):
    rhs_refs = refs[:count]
    out_refs = refs[count:]
    step = pl.program_id(0)
    half = pl.num_programs(0) // outs
    for o in range(outs):

        @pl.when((step >= o * half) & (step < (o + 1) * half))
        def _():
            for rhs_ref, out_ref in zip(rhs_refs, out_refs[o * count : (o + 1) * count]):
                out_ref[0] = dot(lhs_ref[...], rhs_ref[...], first_dims).astype(bf16)


def mlp_weight_grad_kernel(h_ref, c_ref, dg_ref, du_ref, a_ref, o_ref):
    width = a_ref.shape[1]
    for k, (lhs_ref, rhs_ref) in enumerate(((h_ref, dg_ref), (h_ref, du_ref), (c_ref, a_ref))):
        o_ref[:, k * width : (k + 1) * width] = dot(lhs_ref[...], rhs_ref[...], first_dims).astype(bf16)


def weight_grad_turned_kernel(outs, lhs_ref, rhs_ref, *out_refs):
    for o, out_ref in enumerate(out_refs):

        @pl.when(pl.program_id(0) == o)
        def _():
            out_ref[...] = dot(lhs_ref[...], rhs_ref[...]).astype(bf16)


def weight_grad(me, lhs, rhs, parts, rows, is_transposed=False):
    tokens = rhs[0].shape[0]
    depth = lhs.size // tokens
    outs = 2 if parts > 1 else 1
    rows = rows if parts > 1 else TILE
    columns = sum(r.shape[1] for r in rhs)
    if is_transposed:
        half = depth // rows // outs
        made = pl.pallas_call(
            functools.partial(weight_grad_turned_kernel, outs),
            grid=(outs,),
            in_specs=[pl.BlockSpec((depth // outs, tokens), lambda p: (p, 0)), pl.BlockSpec(rhs[0].shape, lambda p: (0, 0))],
            out_specs=[pl.BlockSpec((depth // outs, columns), lambda p: (0, 0))] * outs,
            out_shape=[jax.ShapeDtypeStruct((depth // outs, columns), bf16)] * outs,
            compiler_params=params(),
            cost_estimate=cost(1),
            name="weight_grad_turned",
        )(lhs, rhs[0])
        return [[m.reshape(half, rows, columns) for m in made]]
    steps = depth // rows
    half = steps // outs

    def out_spec(o, width):
        return pl.BlockSpec((1, rows, width), lambda p, _: (jnp.clip(p - o * half, 0, half - 1), 0, 0))

    made = pl.pallas_call(
        functools.partial(weight_grad_kernel, outs, len(rhs)),
        grid_spec=pltpu.PrefetchScalarGridSpec(
            num_scalar_prefetch=1,
            grid=(steps,),
            in_specs=[pl.BlockSpec((tokens, rows), weight_source(parts, steps))]
            + [pl.BlockSpec(r.shape, lambda p, _: (0, 0)) for r in rhs],
            out_specs=[out_spec(o, r.shape[1]) for o in range(outs) for r in rhs],
        ),
        out_shape=[jax.ShapeDtypeStruct((half, rows, r.shape[1]), bf16) for o in range(outs) for r in rhs],
        compiler_params=params(),
        cost_estimate=cost(1),
        name="weight_grad",
    )(me, lhs, *rhs)
    return [made[k :: len(rhs)] for k in range(len(rhs))]


def update_kernel(factor_ref, w_ref, m_ref, e_ref, *refs):
    new_w_ref, new_m_ref, new_e_ref = refs[-3:]
    begin = 0
    for g_ref in refs[:-3]:
        at = slice(begin, begin + g_ref.shape[1])
        made = update(w_ref[:, at], m_ref[:, at], e_ref[:, at], g_ref[...].astype(f32), factor_ref[0], learn_rate)
        new_w_ref[:, at], new_m_ref[:, at], new_e_ref[:, at] = made
        begin += g_ref.shape[1]


def update_weights(factor, weights, momentum, average, pieces):
    rows, columns = weights.shape
    step = 64
    spec = pl.BlockSpec((step, columns), lambda n, _: (n, 0))
    shape = jax.ShapeDtypeStruct(weights.shape, f32)
    return pl.pallas_call(
        update_kernel,
        grid_spec=pltpu.PrefetchScalarGridSpec(
            num_scalar_prefetch=1,
            grid=(rows // step,),
            in_specs=[spec, spec, spec]
            + [pl.BlockSpec((step, piece.shape[1]), lambda n, _: (n, 0)) for piece in pieces],
            out_specs=[spec, spec, spec],
        ),
        out_shape=(shape, shape, shape),
        compiler_params=params(),
        cost_estimate=cost(1),
        name="update",
    )(factor, weights, momentum, average, *pieces)


def update(value, state, average, gradient, factor, step_rate):
    clipped = gradient * factor
    state_new = momentum_decay * state + clipped
    value_new = value - step_rate * (clipped + momentum_decay * state_new)
    average_new = average_decay * average + (1.0 - average_decay) * value_new
    return (value_new, state_new, average_new)


def per_device(
    block_input,
    cotangent,
    doc_lengths,
    span_order,
    weights,
    momentum,
    ema_weights,
    gains,
    gain_momentum,
    gain_ema,
):
    tok_count, model_width = block_input.shape
    data_count = lax.axis_size("dp")
    model_count = lax.axis_size("mp")
    me = lax.axis_index("dp").astype(jnp.int32)
    me_array = me[None]
    row_count = weights.shape[0]
    token_total = tok_count * data_count
    span_total = token_total // SPAN
    span_own = tok_count // SPAN
    seq_len = token_total // doc_lengths.shape[0]
    doc_total = doc_lengths.shape[0] * doc_lengths.shape[1]
    q_heads = HEADS // model_count
    kv_heads = KV // model_count
    group = q_heads // kv_heads
    query_width = q_heads * HD
    kv_width = kv_heads * HD
    ff_width = FF // model_count
    qkv_cols = query_width + 2 * kv_width
    out_end = qkv_cols + query_width
    in_pairs = data_count == 8
    parts = data_count if in_pairs else 1
    outs = 2 if in_pairs else 1
    gain_attn = gains[:model_width]
    gain_mlp = gains[model_width : 2 * model_width]
    head_gains = gains[2 * model_width :].reshape(2, HD)

    kv_own = weights[:, query_width:qkv_cols].astype(bf16)
    if in_pairs:
        kv_outer = gather_chips(kv_own)
        later, kv_own = lax.optimization_barrier((weights, kv_own))
        qo_own = jnp.concatenate([later[:, :query_width], later[:, qkv_cols:out_end]], axis=1).astype(bf16)
        qo_outer = gather_chips(qo_own)
        later, qo_own = lax.optimization_barrier((later, qo_own))
        mlp_own = later[:, out_end:].astype(bf16)
        kv_outer[1], qo_own = lax.optimization_barrier((kv_outer[1], qo_own))
    else:
        mlp_own = weights[:, out_end:].astype(bf16)
        qo_own = jnp.concatenate([weights[:, :query_width], weights[:, qkv_cols:out_end]], axis=1).astype(bf16)
        qo_weights = [lax.all_gather(qo_own, "dp", axis=0, tiled=True)]
        kv_weights = [lax.all_gather(kv_own, "dp", axis=0, tiled=True)]

    doc_ids = jnp.arange(doc_lengths.shape[1], dtype=jnp.int32)
    earlier = doc_ids[None, :] < doc_ids[:, None]
    starts = jnp.sum(jnp.where(earlier[None], doc_lengths[:, None, :], 0), axis=2)
    starts = starts + seq_len * jnp.arange(doc_lengths.shape[0], dtype=jnp.int32)[:, None]
    starts = starts.reshape(doc_total)
    span_ids = jnp.arange(span_total, dtype=jnp.int32)
    inverse = jnp.sum(jnp.where(span_order[None, :] == span_ids[:, None], span_ids[None, :], 0), axis=1)
    if in_pairs:
        inverse = ((inverse // span_own) ^ me) * span_own + inverse % span_own
    own_spans = lax.dynamic_slice(span_order, (me * span_own,), (span_own,))
    home = (own_spans[:, None] * SPAN + jnp.arange(SPAN, dtype=jnp.int32)[None, :]).reshape(tok_count)
    doc_start = jnp.max(jnp.where(starts[None, :] <= home[:, None], starts[None, :], 0), axis=1)
    freqs = rope_base ** (-(2.0 * (jnp.arange(HD, dtype=jnp.int32) % (HD // 2)).astype(f32)) / HD)
    angles = (home - doc_start).astype(f32)[:, None] * freqs[None, :]
    cosine = jnp.cos(angles)
    sine = jnp.sin(angles) * jnp.where(jnp.arange(HD) < HD // 2, -1.0, 1.0)[None, :]

    inputs = block_input.astype(f32)
    scale_in = unit_scale(inputs)
    normed_low = (inputs * scale_in * gain_attn).astype(bf16)

    if in_pairs:
        kv_weights = gather_cores(kv_outer)

    rows_all = pl.BlockSpec((tok_count, model_width), lambda *_: (0, 0))
    angle_spec = pl.BlockSpec((tok_count, HD), lambda *_: (0, 0))
    gain_head_spec = pl.BlockSpec((1, HD), lambda *_: (0, 0))

    def project(weight_parts, width, head_count, gain):
        lin_width = head_count * HD
        return pl.pallas_call(
            functools.partial(project_kernel, parts, head_count),
            grid_spec=pltpu.PrefetchScalarGridSpec(
                num_scalar_prefetch=1,
                grid=(1,),
                in_specs=[rows_all]
                + [pl.BlockSpec((model_width // parts, width), lambda *_: (0, 0))] * parts
                + [angle_spec, angle_spec, gain_head_spec],
                out_specs=[
                    pl.BlockSpec((tok_count, width), lambda *_: (0, 0)),
                    pl.BlockSpec((tok_count, lin_width), lambda *_: (0, 0)),
                ],
                scratch_shapes=[pltpu.VMEM((model_width, width), bf16)],
            ),
            out_shape=(
                jax.ShapeDtypeStruct((tok_count, width), bf16),
                jax.ShapeDtypeStruct((tok_count, lin_width), f32),
            ),
            compiler_params=params(),
            cost_estimate=cost(5),
            name="project",
        )(me_array, normed_low, *weight_parts, cosine, sine, gain)

    keys_values, lin_k = project(kv_weights, 2 * kv_width, kv_heads, head_gains[1:])
    if in_pairs:
        keys_values, qo_outer = lax.optimization_barrier((keys_values, qo_outer))
        qo_weights = gather_cores(qo_outer)
        normed_there, qo_outer = lax.optimization_barrier((normed_low, qo_outer))
        normed_turned = transposed(me_array, normed_there, parts, row_count)
        mlp_own, normed_turned, qo_weights = lax.optimization_barrier((mlp_own, normed_turned, qo_weights))
    else:
        normed_turned = transposed(me_array, normed_low, parts, row_count)
    queries, lin_q = project(qo_weights, query_width, q_heads, head_gains[:1])

    if in_pairs:
        kv_chips, queries, normed_turned, mlp_own = lax.optimization_barrier(
            (gather_chips(keys_values), queries, normed_turned, mlp_own)
        )
        kv_parts = gather_cores(kv_chips)
        mlp_own, kv_parts = lax.optimization_barrier((mlp_own, kv_parts))
    else:
        kv_parts = [lax.all_gather(keys_values, "dp", axis=0, tiled=True)]
    mlp_weights = lax.all_gather(mlp_own, "dp", axis=0, tiled=True)

    heads = kv_heads if in_pairs else 1
    head_steps = kv_heads // heads
    wide = group * SPAN
    anywhere = pl.BlockSpec(memory_space=pl.ANY)
    head_spec = pl.BlockSpec((tok_count, heads * group * HD), lambda g, *_: (0, g))
    q_all = pl.BlockSpec((tok_count, query_width), lambda *_: (0, 0))
    turned_spec = pl.BlockSpec((span_own * heads, HD, wide), lambda g, *_: (g, 0, 0))
    lse_spec = pl.BlockSpec((span_own * heads, 8, wide), lambda g, *_: (g, 0, 0))
    attended, attended_low, lse = pl.pallas_call(
        functools.partial(attend_kernel, group, heads, parts),
        grid_spec=pltpu.PrefetchScalarGridSpec(
            num_scalar_prefetch=3,
            grid=(head_steps,),
            in_specs=[head_spec] + [anywhere] * parts,
            out_specs=[turned_spec, q_all, lse_spec],
            scratch_shapes=[
                pltpu.VMEM((token_total, 2 * kv_width), bf16),
                pltpu.SemaphoreType.DMA((parts,)),
            ],
        ),
        out_shape=(
            jax.ShapeDtypeStruct((span_own * kv_heads, HD, wide), f32),
            jax.ShapeDtypeStruct((tok_count, query_width), bf16),
            jax.ShapeDtypeStruct((span_own * kv_heads, 8, wide), f32),
        ),
        compiler_params=params(),
        cost_estimate=cost(16),
        name="attend",
    )(own_spans, inverse, starts, queries, *kv_parts)
    q_part = pl.BlockSpec((model_width // parts, query_width), lambda *_: (0, 0))
    out_part = pl.BlockSpec((model_width // parts, query_width), lambda *_: (0, 1))
    attn_part = pl.pallas_call(
        functools.partial(project_out_kernel, parts),
        grid_spec=pltpu.PrefetchScalarGridSpec(
            num_scalar_prefetch=1,
            grid=(1,),
            in_specs=[q_all] + [out_part] * parts,
            out_specs=rows_all,
        ),
        out_shape=jax.ShapeDtypeStruct((tok_count, model_width), bf16),
        compiler_params=params(),
        cost_estimate=cost(4),
        name="project_out",
    )(me_array, attended_low, *qo_weights)

    attn_sum = lax.psum(attn_part, "mp")

    tiles = ff_width // TILE
    gain_spec = pl.BlockSpec((1, model_width), lambda *_: (0, 0))
    tile_spec = pl.BlockSpec((tok_count, TILE), lambda n: (0, n))
    hidden_shape = jax.ShapeDtypeStruct((tok_count, ff_width), bf16)
    low_shape = jax.ShapeDtypeStruct((tok_count, model_width), bf16)
    wide_shape = jax.ShapeDtypeStruct((tok_count, model_width), f32)
    scale_spec = pl.BlockSpec((tok_count, 1), lambda *_: (0, 0))
    scale_shape = jax.ShapeDtypeStruct((tok_count, 1), f32)
    grad_hidden = pl.pallas_call(
        plain_kernel,
        grid=(tiles,),
        in_specs=[rows_all, pl.BlockSpec((model_width, TILE), lambda n: (0, n + 2 * tiles))],
        out_specs=tile_spec,
        out_shape=hidden_shape,
        compiler_params=params(),
        cost_estimate=cost(30),
        name="grad_hidden",
    )(cotangent, mlp_weights)
    residual, mlp_low, scale_mlp, grad_gate, grad_up, hidden_low = pl.pallas_call(
        mlp_kernel,
        grid=(tiles,),
        in_specs=[
            rows_all,
            rows_all,
            gain_spec,
            pl.BlockSpec((model_width, TILE), lambda n: (0, n)),
            pl.BlockSpec((model_width, TILE), lambda n: (0, n + tiles)),
            tile_spec,
        ],
        out_specs=[rows_all, rows_all, scale_spec, tile_spec, tile_spec, tile_spec],
        out_shape=(wide_shape, low_shape, scale_shape, hidden_shape, hidden_shape, hidden_shape),
        compiler_params=params(),
        cost_estimate=cost(18),
        name="mlp",
    )(block_input, attn_sum, gain_mlp[None], mlp_weights, mlp_weights, grad_hidden)

    hidden_all = pl.BlockSpec((tok_count, ff_width), lambda n: (0, 0))
    out_tile = pl.BlockSpec((tok_count, 512), lambda n: (0, n))
    grad_mlp_part = pl.pallas_call(
        mlp_back_kernel,
        grid=(model_width // WIDE,),
        in_specs=[
            hidden_all,
            hidden_all,
            pl.BlockSpec((WIDE, ff_width), lambda n: (n, 0)),
            pl.BlockSpec((WIDE, ff_width), lambda n: (n, 1)),
        ],
        out_specs=out_tile,
        out_shape=low_shape,
        compiler_params=params(),
        cost_estimate=cost(11),
        name="mlp_back",
    )(grad_gate, grad_up, mlp_weights, mlp_weights)
    grad_mlp_part, mlp_low, hidden_low = lax.optimization_barrier((grad_mlp_part, mlp_low, hidden_low))
    grad_mlp_sum = lax.psum(grad_mlp_part, "mp")

    row_tile = pl.BlockSpec((tok_count, TILE), lambda n: (0, n))
    dw_mlp = pl.pallas_call(
        mlp_weight_grad_kernel,
        grid=(model_width // TILE,),
        in_specs=[row_tile, row_tile, hidden_all, hidden_all, hidden_all],
        out_specs=pl.BlockSpec((TILE, 3 * ff_width), lambda n: (n, 0)),
        out_shape=jax.ShapeDtypeStruct((model_width, 3 * ff_width), bf16),
        compiler_params=params(),
        cost_estimate=cost(1),
        name="mlp_weight_grad",
    )(mlp_low, cotangent, grad_gate, grad_up, hidden_low)
    mlp_part = pl.pallas_call(
        rows_by_rows_kernel,
        grid=(model_width // 512,),
        in_specs=[hidden_all, pl.BlockSpec((512, ff_width), lambda n: (n, 2))],
        out_specs=out_tile,
        out_shape=low_shape,
        compiler_params=params(),
        cost_estimate=cost(1),
        name="mlp_out",
    )(hidden_low, mlp_weights)
    mlp_grads = lax.psum_scatter(dw_mlp, "dp", scatter_dimension=0, tiled=True)
    grad_mlp_sum, mlp_part, dw_mlp = lax.optimization_barrier((grad_mlp_sum, mlp_part, dw_mlp))
    mlp_sum = lax.psum(mlp_part, "mp")

    half_rows = tok_count // 2
    half_spec = pl.BlockSpec((half_rows, model_width), lambda n, *_: (n, 0))
    grad_residual, grad_res_low, grad_att_low, mlp_gain_grad = pl.pallas_call(
        functools.partial(residual_back_kernel, parts, 1.0 / model_count),
        grid_spec=pltpu.PrefetchScalarGridSpec(
            num_scalar_prefetch=1,
            grid=(2,),
            in_specs=[
                half_spec,
                pl.BlockSpec((half_rows, 1), lambda n, *_: (n, 0)),
                half_spec,
                half_spec,
                gain_spec,
            ]
            + [out_part] * parts,
            out_specs=[half_spec, half_spec, pl.BlockSpec((half_rows, query_width), lambda n, *_: (n, 0)), gain_spec],
            scratch_shapes=[pltpu.VMEM((model_width, query_width), bf16)],
        ),
        out_shape=(
            wide_shape,
            low_shape,
            jax.ShapeDtypeStruct((tok_count, query_width), bf16),
            jax.ShapeDtypeStruct((1, model_width), f32),
        ),
        compiler_params=params(),
        cost_estimate=cost(1),
        name="residual_back",
    )(me_array, residual, scale_mlp, cotangent, grad_mlp_sum, gain_mlp[None], *qo_weights)
    out_rows = token_total // parts
    dkv_spec = pl.BlockSpec((out_rows, 2 * heads * HD), lambda g, *_: (0, g))
    back = pl.pallas_call(
        functools.partial(attend_back_kernel, group, heads, parts, parts),
        grid_spec=pltpu.PrefetchScalarGridSpec(
            num_scalar_prefetch=3,
            grid=(head_steps,),
            in_specs=[head_spec]
            + [anywhere] * parts
            + [head_spec, turned_spec, lse_spec, head_spec]
            + [angle_spec, angle_spec, pl.BlockSpec((1, HD), lambda *_: (0, 0))],
            out_specs=[head_spec, pl.BlockSpec((8, HD), lambda g, *_: (g, 0))] + [dkv_spec] * parts,
            scratch_shapes=[
                pltpu.VMEM((token_total, 2 * kv_width), bf16),
                pltpu.VMEM((token_total, 2 * heads * HD), f32),
                pltpu.SemaphoreType.DMA((parts,)),
            ],
        ),
        out_shape=[
            jax.ShapeDtypeStruct((tok_count, query_width), bf16),
            jax.ShapeDtypeStruct((8 * head_steps, HD), f32),
        ]
        + [jax.ShapeDtypeStruct((out_rows, 2 * kv_width), bf16)] * parts,
        compiler_params=params(),
        cost_estimate=cost(1),
        name="attend_back",
    )(
        own_spans,
        inverse,
        starts,
        queries,
        *kv_parts,
        grad_att_low,
        attended,
        lse,
        lin_q,
        cosine,
        sine,
        head_gains[:1],
    )
    grad_query_low, query_gain_grad = back[:2]
    query_gain_grad = jnp.sum(query_gain_grad, axis=0) / 8.0
    if in_pairs:
        came = [swap(back[2 + k], "dp", 1) for k in range(1, parts, 2)]
        halves = [add_pair(back[2 + 2 * k], came[k]) for k in range(parts // 2)]
        halves, mlp_grads = lax.optimization_barrier((halves, mlp_grads))
        terms = [halves[0]] + [swap(halves[k], "dp", 2 * k) for k in range(1, parts // 2)]
    else:
        terms = [lax.psum_scatter(back[2], "dp", scatter_dimension=0, tiled=True)]

    [dw_query] = weight_grad(me_array, normed_turned, [grad_query_low], parts, row_count, True)
    [dw_out] = weight_grad(me_array, grad_res_low, [attended_low], parts, row_count)

    def scattered(made):
        if in_pairs:
            return sum(term.astype(f32) for term in scatter_small(*made)).astype(bf16)
        whole = made[0].reshape(model_width, -1)
        return lax.psum_scatter(whole, "dp", scatter_dimension=0, tiled=True)

    first_spec = pl.BlockSpec((tok_count // 8, model_width), lambda n: (0, 0))
    block_output = pl.pallas_call(
        output_first_kernel,
        grid=(1,),
        in_specs=[first_spec, first_spec],
        out_specs=first_spec,
        out_shape=low_shape,
        compiler_params=params(),
        cost_estimate=cost(6),
        name="output_first",
    )(residual, mlp_sum)
    terms, block_output, dw_query, dw_out = lax.optimization_barrier((terms, block_output, dw_query, dw_out))
    query_grads, out_grads = scattered(dw_query), scattered(dw_out)
    grad_kv_low, key_gain_grad, attn_gain_grad, grad_norm_part = pl.pallas_call(
        functools.partial(key_back_kernel, parts, len(terms), kv_heads),
        grid_spec=pltpu.PrefetchScalarGridSpec(
            num_scalar_prefetch=1,
            grid=(1,),
            in_specs=[pl.BlockSpec((tok_count, 2 * kv_width), lambda *_: (0, 0))] * len(terms)
            + [pl.BlockSpec((tok_count, kv_width), lambda *_: (0, 0))]
            + [angle_spec, angle_spec, pl.BlockSpec((1, HD), lambda *_: (0, 0))]
            + [q_all, rows_all, scale_spec]
            + [q_part] * parts
            + [pl.BlockSpec((model_width // parts, 2 * kv_width), lambda *_: (0, 0))] * parts,
            out_specs=[
                pl.BlockSpec((tok_count, 2 * kv_width), lambda *_: (0, 0)),
                pl.BlockSpec((8, HD), lambda *_: (0, 0)),
                gain_spec,
                rows_all,
            ],
        ),
        out_shape=[
            jax.ShapeDtypeStruct((tok_count, 2 * kv_width), bf16),
            jax.ShapeDtypeStruct((8, HD), f32),
            jax.ShapeDtypeStruct((1, model_width), f32),
            low_shape,
        ],
        compiler_params=params(),
        cost_estimate=cost(1),
        name="key_back",
    )(
        me_array,
        *terms,
        lin_k,
        cosine,
        sine,
        head_gains[1:],
        grad_query_low,
        block_input,
        scale_in,
        *qo_weights,
        *kv_weights,
    )
    [dw_kv] = weight_grad(me_array, normed_turned, [grad_kv_low], parts, row_count, True)

    grad_norm_share = lax.psum_scatter(grad_norm_part, "mp", scatter_dimension=0, tiled=True)
    kv_grads = scattered(dw_kv)
    mlp_sum, block_output, keys_done = lax.optimization_barrier((mlp_sum, block_output, grad_kv_low))
    rest_spec = pl.BlockSpec((tok_count // 8, model_width), lambda n: (n + 1, 0))
    block_output = pl.pallas_call(
        output_rest_kernel,
        grid=(7,),
        in_specs=[rest_spec, rest_spec, anywhere],
        out_specs=rest_spec,
        out_shape=low_shape,
        input_output_aliases={2: 0},
        compiler_params=params(),
        cost_estimate=cost(5),
        name="output_rest",
    )(residual, mlp_sum, block_output)
    query_grads, kv_grads, out_grads, grad_norm_share, block_output = lax.optimization_barrier(
        (query_grads, kv_grads, out_grads, grad_norm_share, block_output)
    )
    weight_grads = [query_grads, kv_grads, out_grads, mlp_grads]
    square = sum(jnp.sum(jnp.square(grad.astype(f32))) for grad in weight_grads)
    grad_norm_sum = lax.all_gather(grad_norm_share, "mp", axis=0, tiled=True)
    local = [attn_gain_grad[0], mlp_gain_grad[0], query_gain_grad, key_gain_grad[0]]
    totals = sum_all(jnp.concatenate([jnp.broadcast_to(square, (HD,))] + local))
    square_total, gain_grads = totals[0], totals[HD:]
    grad_norm = jnp.sqrt(square_total + jnp.sum(gain_grads * gain_grads))
    factor = 1.0 / jnp.maximum(grad_norm, 1.0)
    new_weights, new_momentum, new_ema = update_weights(factor[None], weights, momentum, ema_weights, weight_grads)
    grad_input = pl.pallas_call(
        input_back_kernel,
        grid=(2,),
        in_specs=[
            half_spec,
            half_spec,
            pl.BlockSpec((half_rows, 1), lambda n: (n, 0)),
            half_spec,
            gain_spec,
        ],
        out_specs=half_spec,
        out_shape=wide_shape,
        compiler_params=params(),
        cost_estimate=cost(8),
        name="input_back",
    )(grad_residual, block_input, scale_in, grad_norm_sum, gain_attn[None])
    new_gains, new_gain_momentum, new_gain_ema = update(gains, gain_momentum, gain_ema, gain_grads, factor, gain_rate)
    return (
        block_output,
        grad_input,
        grad_norm,
        new_weights,
        new_momentum,
        new_ema,
        new_gains,
        new_gain_momentum,
        new_gain_ema,
    )


def solution(mesh):
    return jax.shard_map(
        per_device,
        mesh=mesh,
        in_specs=(
            P("dp", None),
            P("dp", None),
            P(),
            P(),
            P("dp", "mp"),
            P("dp", "mp"),
            P("dp", "mp"),
            P(),
            P(),
            P(),
        ),
        out_specs=(
            P("dp", None),
            P("dp", None),
            P(),
            P("dp", "mp"),
            P("dp", "mp"),
            P("dp", "mp"),
            P(),
            P(),
            P(),
        ),
        check_vma=False,
    )
```

```python
import functools

import jax
import jax.numpy as jnp
from jax import lax
from jax.experimental import pallas as pl
from jax.experimental.pallas import tpu as pltpu
from jax.sharding import PartitionSpec as P

HEADS = 16
KV = 8
HD = 128
FF = 6144
SPAN = 128
CHUNK = 4
TILE = 256
WIDE = 512
VMEM_LIMIT = 60 * 1024 * 1024

eps_norm = 1e-06
rope_base = 1000000.0
learn_rate = 100.0
gain_rate = 4000.0
momentum_decay = 0.5
average_decay = 0.5
score_scale = HD ** (-0.5)
far = -1e30

bf16 = jnp.bfloat16
f32 = jnp.float32
plain_dims = (((1,), (0,)), ((), ()))
last_dims = (((1,), (1,)), ((), ()))
first_dims = (((0,), (0,)), ((), ()))


def dot(a, b, dims=plain_dims):
    return lax.dot_general(a, b, dims, preferred_element_type=f32)


def cost(micros):
    return pl.CostEstimate(flops=int(micros * 1.0e9), bytes_accessed=int(micros * 3.4e6), transcendentals=0)


def params(**more):
    return pltpu.CompilerParams(vmem_limit_bytes=VMEM_LIMIT, **more)


def swap(array, axis, distance):
    count = lax.axis_size(axis)
    return lax.ppermute(array, axis, [(i, i ^ distance) for i in range(count)])


def gather_chips(own):
    return [own] + [swap(own, "dp", k) for k in (2, 4, 6)]


def gather_cores(outer):
    inner = [swap(block, "dp", 1) for block in outer]
    return [block for pair in zip(outer, inner) for block in pair]


def scatter_small(even, odd):
    came = swap(odd, "dp", 1)
    half = (even.astype(f32) + came.astype(f32)).astype(bf16)
    return [half[0]] + [swap(half[k], "dp", 2 * k) for k in (1, 2, 3)]


def add_pair(a, b):
    return (a.astype(f32) + b.astype(f32)).astype(bf16)


def sum_all(value):
    for axis in ("dp", "mp"):
        distance = 1
        while distance < lax.axis_size(axis):
            value = value + swap(value, axis, distance)
            distance *= 2
    return value


def place_of(me_ref, k, parts):
    return me_ref[0] ^ k if parts > 1 else 0


def in_order(me_ref, part_refs, whole_ref):
    parts = len(part_refs)
    rows = part_refs[0].shape[0]
    for k, ref in enumerate(part_refs):
        at = pl.multiple_of(place_of(me_ref, k, parts) * rows, rows)
        whole_ref[pl.ds(at, rows), :] = ref[...]


def turned(normed, cosine, sine):
    return normed * cosine + pltpu.roll(normed, HD // 2, 1) * sine


def turned_back(gradient, cosine, sine):
    return gradient * cosine + pltpu.roll(gradient * sine, HD // 2, 1)


def unit_scale(values):
    return lax.rsqrt(jnp.mean(values * values, axis=-1, keepdims=True) + eps_norm)


def norm_back(unit, scale, gain, gradient):
    e = gradient * gain
    return scale * (e - unit * jnp.mean(e * unit, axis=-1, keepdims=True))


def project_kernel(parts, q_tiles, me_ref, h_ref, *refs):
    cos_ref, sin_ref, gain_ref, q_ref, kv_ref, lin_ref, w_ref = refs[parts:]
    tile = pl.program_id(0)
    in_order(me_ref, refs[:parts], w_ref)
    total = dot(h_ref[...], w_ref[...])
    per_tile = TILE // HD

    def normed_to(out_ref, gain):
        for part in range(per_tile):
            at = slice(part * HD, (part + 1) * HD)
            values = total[:, at]
            lin_ref[:, at] = values
            normed = values * unit_scale(values) * gain
            out_ref[:, at] = turned(normed, cos_ref[...], sin_ref[...]).astype(bf16)

    @pl.when(tile < q_tiles)
    def _():
        normed_to(q_ref, gain_ref[0:1])

    @pl.when(tile == q_tiles)
    def _():
        normed_to(kv_ref, gain_ref[1:2])

    @pl.when(tile > q_tiles)
    def _():
        kv_ref[...] = total.astype(bf16)


def span_limits(own_ref, starts_ref, i, group):
    span = own_ref[i]
    first = span * SPAN
    lane = lax.broadcasted_iota(jnp.int32, (1, group * SPAN), 1)
    places = first + (lane & (SPAN - 1))
    low = jnp.int32(0)
    begin = jnp.zeros((1, group * SPAN), jnp.int32)
    for d in range(starts_ref.shape[0]):
        start = starts_ref[d]
        low = jnp.maximum(low, jnp.where(start <= first, start, 0))
        begin = jnp.maximum(begin, jnp.where(start <= places, start, 0))
    return span, low // SPAN, places, begin


def key_rows(inverse_ref, newest, b):
    return pl.multiple_of(inverse_ref[jnp.maximum(newest - b, 0)] * SPAN, SPAN)


def allowed_keys(newest, places, begin):
    row = lax.broadcasted_iota(jnp.int32, (CHUNK * SPAN, 1), 0)
    key = newest * SPAN + (row & (SPAN - 1)) - (row & ~(SPAN - 1))
    return (key <= places) & (key >= begin)


def stacked(ref, i, head, group):
    rows = pl.ds(i * SPAN, SPAN)
    return jnp.concatenate([ref[rows, h * HD : (h + 1) * HD] for h in range(head * group, (head + 1) * group)], axis=0)


def head_columns(first, heads, kv_heads):
    keys = [pl.ds(pl.multiple_of((first + h) * HD, HD), HD) for h in range(heads)]
    values = [pl.ds(pl.multiple_of((first + h + kv_heads) * HD, HD), HD) for h in range(heads)]
    return keys, values


def load_parts(part_refs, target_ref, sem_ref, first):
    rows = part_refs[0].shape[0]
    return [
        pltpu.make_async_copy(ref, target_ref.at[pl.ds(k * rows, rows)], sem_ref.at[first + k])
        for k, ref in enumerate(part_refs)
    ]


def attend_kernel(group, heads, parts, own_ref, inverse_ref, starts_ref, q_ref, *refs):
    kv_parts = refs[:parts]
    turned_ref, low_ref, lse_ref, kv_ref, sem_ref = refs[parts:]
    g = pl.program_id(0)
    kv_heads = pl.num_programs(0) * heads
    kv_copies = load_parts(kv_parts, kv_ref, sem_ref, 0)

    @pl.when(g == 0)
    def _():
        for copy in kv_copies:
            copy.start()
        for copy in kv_copies:
            copy.wait()

    key_at, value_at = head_columns(g * heads, heads, kv_heads)
    wide = group * SPAN
    for i in range(own_ref.shape[0]):
        span, low, places, begin = span_limits(own_ref, starts_ref, i, group)
        queries = [stacked(q_ref, i, h, group) for h in range(heads)]
        count = (span - low) // CHUNK + 1

        def step(c, carry):
            newest = span - c * CHUNK
            at = [key_rows(inverse_ref, newest, b) for b in range(CHUNK)]
            allowed = allowed_keys(newest, places, begin)
            made = []
            for h, (top, weight, total) in enumerate(carry):
                keys = jnp.concatenate([kv_ref[pl.ds(a, SPAN), key_at[h]] for a in at], axis=0)
                values = jnp.concatenate([kv_ref[pl.ds(a, SPAN), value_at[h]] for a in at], axis=0)
                scores = jnp.where(allowed, dot(keys, queries[h], last_dims), far)
                new_top = jnp.maximum(top, jnp.max(scores, axis=0, keepdims=True))
                probs = jnp.exp((scores - new_top) * score_scale)
                shrink = jnp.exp((top - new_top) * score_scale)
                weight = weight * shrink + jnp.sum(probs, axis=0, keepdims=True)
                total = total * shrink + dot(values, probs.astype(bf16), first_dims)
                made.append((new_top, weight, total))
            return tuple(made)

        start = (jnp.full((1, wide), far, f32), jnp.zeros((1, wide), f32), jnp.zeros((HD, wide), f32))
        made = lax.fori_loop(0, count, step, (start,) * heads)
        for h, (top, weight, total) in enumerate(made):
            output = total / weight
            place = i * heads + h
            turned_ref[place] = output
            lse_ref[place] = jnp.broadcast_to(top * score_scale + jnp.log(weight), (8, wide))
            back = output.T.astype(bf16)
            for k in range(group):
                column = pl.multiple_of(((g * heads + h) * group + k) * HD, HD)
                low_ref[pl.ds(i * SPAN, SPAN), pl.ds(column, HD)] = back[k * SPAN : (k + 1) * SPAN]


def project_out_kernel(parts, me_ref, low_ref, *refs):
    out_parts = refs[:parts]
    o_ref = refs[parts]
    width = out_parts[0].shape[0]
    block = min(width, TILE)
    for k, w_ref in enumerate(out_parts):
        first = place_of(me_ref, k, parts) * width
        for b in range(width // block):
            at = pl.multiple_of(first + b * block, block)
            term = dot(low_ref[...], w_ref[b * block : (b + 1) * block], last_dims)
            o_ref[:, pl.ds(at, block)] = term.astype(bf16)


def plain_kernel(a_ref, w_ref, o_ref):
    o_ref[...] = dot(a_ref[...], w_ref[...]).astype(bf16)


def mlp_kernel(x_ref, s_ref, gain_ref, wg_ref, wu_ref, da_ref, y_ref, h_ref, scale_ref, dg_ref, du_ref, a_ref):
    @pl.when(pl.program_id(0) == 0)
    def _():
        def rows_of(r, unused):
            at = pl.ds(pl.multiple_of(r * 64, 64), 64)
            y = x_ref[at, :].astype(f32) + s_ref[at, :].astype(f32)
            y_ref[at, :] = y
            scale = unit_scale(y)
            scale_ref[at, :] = scale
            h_ref[at, :] = (y * scale * gain_ref[...]).astype(bf16)
            return unused

        lax.fori_loop(0, x_ref.shape[0] // 64, rows_of, 0, unroll=2)

    hidden = h_ref[...]
    gate = dot(hidden, wg_ref[...])
    up = dot(hidden, wu_ref[...])
    grad = da_ref[...].astype(f32)
    sig = 1.0 / (1.0 + jnp.exp(-gate))
    silu = gate * sig
    a_ref[...] = (silu * up).astype(bf16)
    dg_ref[...] = (grad * up * (sig + silu * (1.0 - sig))).astype(bf16)
    du_ref[...] = (grad * silu).astype(bf16)


def mlp_back_kernel(dg_ref, du_ref, wg_ref, wu_ref, dh_ref):
    dh_ref[...] = (dot(dg_ref[...], wg_ref[...], last_dims) + dot(du_ref[...], wu_ref[...], last_dims)).astype(bf16)


def rows_by_rows_kernel(a_ref, w_ref, o_ref):
    o_ref[...] = dot(a_ref[...], w_ref[...], last_dims).astype(bf16)


def residual_back_kernel(parts, share, me_ref, y_ref, scale_ref, c_ref, s_ref, gain_ref, *refs):
    dy_ref, low_ref, do_ref, dgain_ref, w_ref = refs[parts:]

    @pl.when(pl.program_id(0) == 0)
    def _():
        dgain_ref[...] = jnp.zeros_like(dgain_ref)
        in_order(me_ref, refs[:parts], w_ref)

    def rows_of(r, dgain):
        at = pl.ds(pl.multiple_of(r * 32, 32), 32)
        scale = scale_ref[at, :]
        unit = y_ref[at, :] * scale
        grad = s_ref[at, :].astype(f32)
        dy = c_ref[at, :].astype(f32) + norm_back(unit, scale, gain_ref[...], grad)
        dy_ref[at, :] = dy
        low_ref[at, :] = dy.astype(bf16)
        return dgain + jnp.sum(grad * unit, axis=0, keepdims=True)

    zeros = jnp.zeros(dgain_ref.shape, f32)
    dgain_ref[...] += share * lax.fori_loop(0, y_ref.shape[0] // 32, rows_of, zeros, unroll=2)
    do_ref[...] = dot(low_ref[...], w_ref[...]).astype(bf16)


def attend_back_kernel(group, heads, parts, outs, own_ref, inverse_ref, starts_ref, q_ref, *refs):
    kv_parts = refs[:parts]
    do_ref, turned_ref, lse_ref, lin_ref, cos_ref, sin_ref, gain_ref = refs[parts : parts + 7]
    dq_ref, dgain_ref = refs[parts + 7 : parts + 9]
    dkv_refs = refs[parts + 9 : parts + 9 + outs]
    kv_ref, acc_ref, sem_ref = refs[parts + 9 + outs :]
    g = pl.program_id(0)
    kv_heads = pl.num_programs(0) * heads
    copies = load_parts(kv_parts, kv_ref, sem_ref, 0)

    @pl.when(g == 0)
    def _():
        for copy in copies:
            copy.start()

    acc_ref[...] = jnp.zeros_like(acc_ref)

    @pl.when(g == 0)
    def _():
        for copy in copies:
            copy.wait()

    key_at, value_at = head_columns(g * heads, heads, kv_heads)
    wide = group * SPAN
    dgain = jnp.zeros((1, HD), f32)
    for i in range(own_ref.shape[0]):
        span, low, places, begin = span_limits(own_ref, starts_ref, i, group)
        queries = [stacked(q_ref, i, h, group) for h in range(heads)]
        grads = [stacked(do_ref, i, h, group) for h in range(heads)]
        deltas = [
            jnp.sum(grads[h].astype(f32).T * turned_ref[i * heads + h], axis=0, keepdims=True) for h in range(heads)
        ]
        lses = [lse_ref[i * heads + h, :1] for h in range(heads)]
        count = (span - low) // CHUNK + 1

        def step(c, carry):
            newest = span - c * CHUNK
            at = [key_rows(inverse_ref, newest, b) for b in range(CHUNK)]
            allowed = allowed_keys(newest, places, begin)
            made = []
            for h, grad_query in enumerate(carry):
                keys = jnp.concatenate([kv_ref[pl.ds(a, SPAN), key_at[h]] for a in at], axis=0)
                values = jnp.concatenate([kv_ref[pl.ds(a, SPAN), value_at[h]] for a in at], axis=0)
                scores = dot(keys, queries[h], last_dims) * score_scale
                probs = jnp.exp(jnp.where(allowed, scores - lses[h], far))
                grad_probs = dot(values, grads[h], last_dims)
                grad_scores = (probs * (grad_probs - deltas[h])).astype(bf16)
                grad_values = dot(probs.astype(bf16), grads[h])
                grad_keys = dot(grad_scores, queries[h]) * score_scale
                left = 2 * h * HD
                for b, a in enumerate(at):
                    rows = slice(b * SPAN, (b + 1) * SPAN)
                    acc_ref[pl.ds(a, SPAN), left : left + HD] += grad_keys[rows]
                    acc_ref[pl.ds(a, SPAN), left + HD : left + 2 * HD] += grad_values[rows]
                made.append(grad_query + dot(keys, grad_scores, first_dims))
            return tuple(made)

        made = lax.fori_loop(0, count, step, (jnp.zeros((HD, wide), f32),) * heads)
        place = pl.ds(i * SPAN, SPAN)
        for h, grad_query in enumerate(made):
            grad_query = (grad_query * score_scale).T
            for k in range(group):
                at = slice((h * group + k) * HD, (h * group + k + 1) * HD)
                back = turned_back(grad_query[k * SPAN : (k + 1) * SPAN], cos_ref[place, :], sin_ref[place, :])
                lin = lin_ref[place, at]
                scale = unit_scale(lin)
                unit = lin * scale
                dgain = dgain + jnp.sum(back * unit, axis=0, keepdims=True)
                dq_ref[place, at] = norm_back(unit, scale, gain_ref[...], back).astype(bf16)
    dgain_ref[...] = jnp.broadcast_to(dgain, dgain_ref.shape)

    rows = acc_ref.shape[0] // parts
    for k in range(parts):
        dkv_refs[k % outs][pl.ds((k // outs) * rows, rows), :] = acc_ref[pl.ds(k * rows, rows), :].astype(bf16)


def key_back_kernel(parts, terms, kv_heads, me_ref, *refs):
    term_refs = refs[:terms]
    lin_ref, cos_ref, sin_ref, gain_ref, dq_ref, x_ref, scale_ref = refs[terms : terms + 7]
    w_refs = refs[terms + 7 : terms + 7 + parts]
    dkv_ref, dgain_k_ref, dgain_ref, dh_ref = refs[terms + 7 + parts :]
    dgain = jnp.zeros((1, HD), f32)

    def total(begin):
        value = None
        for ref in term_refs:
            term = ref[:, begin : begin + HD].astype(f32)
            value = term if value is None else value + term
        return value

    for g in range(kv_heads):
        at = slice(g * HD, (g + 1) * HD)
        back = turned_back(total(2 * g * HD), cos_ref[...], sin_ref[...])
        lin = lin_ref[:, at]
        scale = unit_scale(lin)
        unit = lin * scale
        dgain = dgain + jnp.sum(back * unit, axis=0, keepdims=True)
        dkv_ref[:, at] = norm_back(unit, scale, gain_ref[...], back).astype(bf16)
        dkv_ref[:, (kv_heads + g) * HD : (kv_heads + g + 1) * HD] = total((2 * g + 1) * HD).astype(bf16)
    dgain_k_ref[...] = jnp.broadcast_to(dgain, dgain_k_ref.shape)

    scale = scale_ref[...]
    width = w_refs[0].shape[0]
    block = min(width, TILE)
    q_width = dq_ref.shape[1]
    for k, w_ref in enumerate(w_refs):
        first = place_of(me_ref, k, parts) * width
        for b in range(width // block):
            here = pl.ds(pl.multiple_of(first + b * block, block), block)
            rows = slice(b * block, (b + 1) * block)
            term = dot(dq_ref[...], w_ref[rows, :q_width], last_dims)
            term = term + dot(dkv_ref[...], w_ref[rows, q_width:], last_dims)
            dh_ref[:, here] = term.astype(bf16)
            unit = x_ref[:, here].astype(f32) * scale
            dgain_ref[:, here] = jnp.sum(term * unit, axis=0, keepdims=True)


def input_back_kernel(dy_ref, x_ref, scale_ref, s_ref, gain_ref, o_ref):
    def rows_of(r, unused):
        at = pl.ds(pl.multiple_of(r * 16, 16), 16)
        scale = scale_ref[at, :]
        back = norm_back(x_ref[at, :].astype(f32) * scale, scale, gain_ref[...], s_ref[at, :].astype(f32))
        o_ref[at, :] = dy_ref[at, :] + back
        return unused

    lax.fori_loop(0, x_ref.shape[0] // 16, rows_of, 0, unroll=4)


def transpose_kernel(me_ref, x_ref, o_ref):
    o_ref[...] = x_ref[...].T


def transposed(me, lhs, parts, rows):
    tokens, depth = lhs.shape
    rows = rows if parts > 1 else TILE
    return pl.pallas_call(
        transpose_kernel,
        grid_spec=pltpu.PrefetchScalarGridSpec(
            num_scalar_prefetch=1,
            grid=(depth // rows,),
            in_specs=[pl.BlockSpec((tokens, rows), weight_source(parts, depth // rows))],
            out_specs=pl.BlockSpec((rows, tokens), lambda p, _: (p, 0)),
        ),
        out_shape=jax.ShapeDtypeStruct((depth, tokens), bf16),
        compiler_params=params(),
        cost_estimate=cost(5),
        name="transposed",
    )(me, lhs)


def weight_source(parts, steps):
    half = steps // 2

    def source(p, me_ref):
        return (0, me_ref[0] ^ (2 * (p % half) + p // half)) if parts > 1 else (0, p)

    return source


def weight_grad_kernel(outs, count, me_ref, lhs_ref, *refs):
    rhs_refs = refs[:count]
    out_refs = refs[count:]
    step = pl.program_id(0)
    half = pl.num_programs(0) // outs
    for o in range(outs):

        @pl.when((step >= o * half) & (step < (o + 1) * half))
        def _():
            for rhs_ref, out_ref in zip(rhs_refs, out_refs[o * count : (o + 1) * count]):
                out_ref[0] = dot(lhs_ref[...], rhs_ref[...], first_dims).astype(bf16)


def mlp_weight_grad_kernel(h_ref, c_ref, dg_ref, du_ref, a_ref, o_ref):
    width = a_ref.shape[1]
    for k, (lhs_ref, rhs_ref) in enumerate(((h_ref, dg_ref), (h_ref, du_ref), (c_ref, a_ref))):
        o_ref[:, k * width : (k + 1) * width] = dot(lhs_ref[...], rhs_ref[...], first_dims).astype(bf16)


def weight_grad_turned_kernel(outs, lhs_ref, rhs_ref, *out_refs):
    for o, out_ref in enumerate(out_refs):

        @pl.when(pl.program_id(0) == o)
        def _():
            out_ref[...] = dot(lhs_ref[...], rhs_ref[...]).astype(bf16)


def weight_grad(me, lhs, rhs, parts, rows, is_transposed=False):
    tokens = rhs[0].shape[0]
    depth = lhs.size // tokens
    outs = 2 if parts > 1 else 1
    rows = rows if parts > 1 else TILE
    columns = sum(r.shape[1] for r in rhs)
    if is_transposed:
        half = depth // rows // outs
        made = pl.pallas_call(
            functools.partial(weight_grad_turned_kernel, outs),
            grid=(outs,),
            in_specs=[pl.BlockSpec((depth // outs, tokens), lambda p: (p, 0)), pl.BlockSpec(rhs[0].shape, lambda p: (0, 0))],
            out_specs=[pl.BlockSpec((depth // outs, columns), lambda p: (0, 0))] * outs,
            out_shape=[jax.ShapeDtypeStruct((depth // outs, columns), bf16)] * outs,
            compiler_params=params(),
            cost_estimate=cost(1),
            name="weight_grad_turned",
        )(lhs, rhs[0])
        return [[m.reshape(half, rows, columns) for m in made]]
    steps = depth // rows
    half = steps // outs

    def out_spec(o, width):
        return pl.BlockSpec((1, rows, width), lambda p, _: (jnp.clip(p - o * half, 0, half - 1), 0, 0))

    made = pl.pallas_call(
        functools.partial(weight_grad_kernel, outs, len(rhs)),
        grid_spec=pltpu.PrefetchScalarGridSpec(
            num_scalar_prefetch=1,
            grid=(steps,),
            in_specs=[pl.BlockSpec((tokens, rows), weight_source(parts, steps))]
            + [pl.BlockSpec(r.shape, lambda p, _: (0, 0)) for r in rhs],
            out_specs=[out_spec(o, r.shape[1]) for o in range(outs) for r in rhs],
        ),
        out_shape=[jax.ShapeDtypeStruct((half, rows, r.shape[1]), bf16) for o in range(outs) for r in rhs],
        compiler_params=params(),
        cost_estimate=cost(1),
        name="weight_grad",
    )(me, lhs, *rhs)
    return [made[k :: len(rhs)] for k in range(len(rhs))]


def update_kernel(factor_ref, w_ref, m_ref, e_ref, *refs):
    new_w_ref, new_m_ref, new_e_ref = refs[-3:]
    begin = 0
    for g_ref in refs[:-3]:
        at = slice(begin, begin + g_ref.shape[1])
        made = update(w_ref[:, at], m_ref[:, at], e_ref[:, at], g_ref[...].astype(f32), factor_ref[0], learn_rate)
        new_w_ref[:, at], new_m_ref[:, at], new_e_ref[:, at] = made
        begin += g_ref.shape[1]


def update_weights(factor, weights, momentum, average, pieces):
    rows, columns = weights.shape
    step = 64
    spec = pl.BlockSpec((step, columns), lambda n, _: (n, 0))
    shape = jax.ShapeDtypeStruct(weights.shape, f32)
    return pl.pallas_call(
        update_kernel,
        grid_spec=pltpu.PrefetchScalarGridSpec(
            num_scalar_prefetch=1,
            grid=(rows // step,),
            in_specs=[spec, spec, spec]
            + [pl.BlockSpec((step, piece.shape[1]), lambda n, _: (n, 0)) for piece in pieces],
            out_specs=[spec, spec, spec],
        ),
        out_shape=(shape, shape, shape),
        compiler_params=params(),
        cost_estimate=cost(1),
        name="update",
    )(factor, weights, momentum, average, *pieces)


def update(value, state, average, gradient, factor, step_rate):
    clipped = gradient * factor
    state_new = momentum_decay * state + clipped
    value_new = value - step_rate * (clipped + momentum_decay * state_new)
    average_new = average_decay * average + (1.0 - average_decay) * value_new
    return (value_new, state_new, average_new)


def per_device(
    block_input,
    cotangent,
    doc_lengths,
    span_order,
    weights,
    momentum,
    ema_weights,
    gains,
    gain_momentum,
    gain_ema,
):
    tok_count, model_width = block_input.shape
    data_count = lax.axis_size("dp")
    model_count = lax.axis_size("mp")
    me = lax.axis_index("dp").astype(jnp.int32)
    me_array = me[None]
    row_count = weights.shape[0]
    token_total = tok_count * data_count
    span_total = token_total // SPAN
    span_own = tok_count // SPAN
    seq_len = token_total // doc_lengths.shape[0]
    doc_total = doc_lengths.shape[0] * doc_lengths.shape[1]
    q_heads = HEADS // model_count
    kv_heads = KV // model_count
    group = q_heads // kv_heads
    query_width = q_heads * HD
    kv_width = kv_heads * HD
    ff_width = FF // model_count
    qkv_cols = query_width + 2 * kv_width
    out_end = qkv_cols + query_width
    in_pairs = data_count == 8
    parts = data_count if in_pairs else 1
    outs = 2 if in_pairs else 1
    gain_attn = gains[:model_width]
    gain_mlp = gains[model_width : 2 * model_width]
    head_gains = gains[2 * model_width :].reshape(2, HD)

    qkv_own = weights[:, :qkv_cols].astype(bf16)
    if in_pairs:
        qkv_outer = gather_chips(qkv_own)
        later, qkv_own = lax.optimization_barrier((weights, qkv_own))
        out_outer = gather_chips(later[:, qkv_cols:out_end].astype(bf16))
    else:
        later = weights
        qkv_parts = [lax.all_gather(qkv_own, "dp", axis=0, tiled=True)]
        out_own = weights[:, qkv_cols:out_end].astype(bf16)
        out_parts = [lax.all_gather(out_own, "dp", axis=0, tiled=True)]

    doc_ids = jnp.arange(doc_lengths.shape[1], dtype=jnp.int32)
    earlier = doc_ids[None, :] < doc_ids[:, None]
    starts = jnp.sum(jnp.where(earlier[None], doc_lengths[:, None, :], 0), axis=2)
    starts = starts + seq_len * jnp.arange(doc_lengths.shape[0], dtype=jnp.int32)[:, None]
    starts = starts.reshape(doc_total)
    span_ids = jnp.arange(span_total, dtype=jnp.int32)
    inverse = jnp.sum(jnp.where(span_order[None, :] == span_ids[:, None], span_ids[None, :], 0), axis=1)
    if in_pairs:
        inverse = ((inverse // span_own) ^ me) * span_own + inverse % span_own
    own_spans = lax.dynamic_slice(span_order, (me * span_own,), (span_own,))
    home = (own_spans[:, None] * SPAN + jnp.arange(SPAN, dtype=jnp.int32)[None, :]).reshape(tok_count)
    doc_start = jnp.max(jnp.where(starts[None, :] <= home[:, None], starts[None, :], 0), axis=1)
    freqs = rope_base ** (-(2.0 * (jnp.arange(HD, dtype=jnp.int32) % (HD // 2)).astype(f32)) / HD)
    angles = (home - doc_start).astype(f32)[:, None] * freqs[None, :]
    cosine = jnp.cos(angles)
    sine = jnp.sin(angles) * jnp.where(jnp.arange(HD) < HD // 2, -1.0, 1.0)[None, :]

    inputs = block_input.astype(f32)
    scale_in = unit_scale(inputs)
    normed_low = (inputs * scale_in * gain_attn).astype(bf16)

    normed_turned = transposed(me_array, normed_low, parts, row_count)
    if in_pairs:
        normed_turned, qkv_outer[1] = lax.optimization_barrier((normed_turned, qkv_outer[1]))
        qkv_parts = gather_cores(qkv_outer)

    q_tiles = query_width // TILE
    rows_all = pl.BlockSpec((tok_count, model_width), lambda *_: (0, 0))
    angle_spec = pl.BlockSpec((tok_count, HD), lambda *_: (0, 0))
    part_tile = pl.BlockSpec((model_width // parts, TILE), lambda n, *_: (0, n))
    queries, keys_values, lin = pl.pallas_call(
        functools.partial(project_kernel, parts, q_tiles),
        grid_spec=pltpu.PrefetchScalarGridSpec(
            num_scalar_prefetch=1,
            grid=(qkv_cols // TILE,),
            in_specs=[rows_all]
            + [part_tile] * parts
            + [angle_spec, angle_spec, pl.BlockSpec((2, HD), lambda *_: (0, 0))],
            out_specs=[
                pl.BlockSpec((tok_count, TILE), lambda n, *_: (0, jnp.minimum(n, q_tiles - 1))),
                pl.BlockSpec((tok_count, TILE), lambda n, *_: (0, jnp.maximum(n - q_tiles, 0))),
                pl.BlockSpec((tok_count, TILE), lambda n, *_: (0, jnp.minimum(n, q_tiles))),
            ],
            scratch_shapes=[pltpu.VMEM((model_width, TILE), bf16)],
        ),
        out_shape=(
            jax.ShapeDtypeStruct((tok_count, query_width), bf16),
            jax.ShapeDtypeStruct((tok_count, 2 * kv_width), bf16),
            jax.ShapeDtypeStruct((tok_count, query_width + kv_width), f32),
        ),
        compiler_params=params(),
        cost_estimate=cost(6),
        name="project",
    )(me_array, normed_low, *qkv_parts, cosine, sine, head_gains)

    mlp_own = later[:, out_end:].astype(bf16)
    if in_pairs:
        keys_values, out_outer = lax.optimization_barrier((keys_values, out_outer))
        kv_parts = gather_cores(gather_chips(keys_values))
        out_parts = gather_cores(out_outer)
        mlp_own, out_parts, kv_parts = lax.optimization_barrier((mlp_own, out_parts, kv_parts))
    else:
        kv_parts = [lax.all_gather(keys_values, "dp", axis=0, tiled=True)]
    mlp_weights = lax.all_gather(mlp_own, "dp", axis=0, tiled=True)

    heads = kv_heads if in_pairs else 1
    head_steps = kv_heads // heads
    wide = group * SPAN
    anywhere = pl.BlockSpec(memory_space=pl.ANY)
    head_spec = pl.BlockSpec((tok_count, heads * group * HD), lambda g, *_: (0, g))
    q_all = pl.BlockSpec((tok_count, query_width), lambda *_: (0, 0))
    turned_spec = pl.BlockSpec((span_own * heads, HD, wide), lambda g, *_: (g, 0, 0))
    lse_spec = pl.BlockSpec((span_own * heads, 8, wide), lambda g, *_: (g, 0, 0))
    attended, attended_low, lse = pl.pallas_call(
        functools.partial(attend_kernel, group, heads, parts),
        grid_spec=pltpu.PrefetchScalarGridSpec(
            num_scalar_prefetch=3,
            grid=(head_steps,),
            in_specs=[head_spec] + [anywhere] * parts,
            out_specs=[turned_spec, q_all, lse_spec],
            scratch_shapes=[
                pltpu.VMEM((token_total, 2 * kv_width), bf16),
                pltpu.SemaphoreType.DMA((parts,)),
            ],
        ),
        out_shape=(
            jax.ShapeDtypeStruct((span_own * kv_heads, HD, wide), f32),
            jax.ShapeDtypeStruct((tok_count, query_width), bf16),
            jax.ShapeDtypeStruct((span_own * kv_heads, 8, wide), f32),
        ),
        compiler_params=params(),
        cost_estimate=cost(16),
        name="attend",
    )(own_spans, inverse, starts, queries, *kv_parts)
    part_all = pl.BlockSpec((model_width // parts, query_width), lambda *_: (0, 0))
    attn_part = pl.pallas_call(
        functools.partial(project_out_kernel, parts),
        grid_spec=pltpu.PrefetchScalarGridSpec(
            num_scalar_prefetch=1,
            grid=(1,),
            in_specs=[q_all] + [part_all] * parts,
            out_specs=rows_all,
        ),
        out_shape=jax.ShapeDtypeStruct((tok_count, model_width), bf16),
        compiler_params=params(),
        cost_estimate=cost(4),
        name="project_out",
    )(me_array, attended_low, *out_parts)

    attn_sum = lax.psum(attn_part, "mp")

    tiles = ff_width // TILE
    gain_spec = pl.BlockSpec((1, model_width), lambda *_: (0, 0))
    tile_spec = pl.BlockSpec((tok_count, TILE), lambda n: (0, n))
    hidden_shape = jax.ShapeDtypeStruct((tok_count, ff_width), bf16)
    low_shape = jax.ShapeDtypeStruct((tok_count, model_width), bf16)
    wide_shape = jax.ShapeDtypeStruct((tok_count, model_width), f32)
    scale_spec = pl.BlockSpec((tok_count, 1), lambda *_: (0, 0))
    scale_shape = jax.ShapeDtypeStruct((tok_count, 1), f32)
    grad_hidden = pl.pallas_call(
        plain_kernel,
        grid=(tiles,),
        in_specs=[rows_all, pl.BlockSpec((model_width, TILE), lambda n: (0, n + 2 * tiles))],
        out_specs=tile_spec,
        out_shape=hidden_shape,
        compiler_params=params(),
        cost_estimate=cost(30),
        name="grad_hidden",
    )(cotangent, mlp_weights)
    residual, mlp_low, scale_mlp, grad_gate, grad_up, hidden_low = pl.pallas_call(
        mlp_kernel,
        grid=(tiles,),
        in_specs=[
            rows_all,
            rows_all,
            gain_spec,
            pl.BlockSpec((model_width, TILE), lambda n: (0, n)),
            pl.BlockSpec((model_width, TILE), lambda n: (0, n + tiles)),
            tile_spec,
        ],
        out_specs=[rows_all, rows_all, scale_spec, tile_spec, tile_spec, tile_spec],
        out_shape=(wide_shape, low_shape, scale_shape, hidden_shape, hidden_shape, hidden_shape),
        compiler_params=params(),
        cost_estimate=cost(18),
        name="mlp",
    )(block_input, attn_sum, gain_mlp[None], mlp_weights, mlp_weights, grad_hidden)

    hidden_all = pl.BlockSpec((tok_count, ff_width), lambda n: (0, 0))
    out_tile = pl.BlockSpec((tok_count, 512), lambda n: (0, n))
    grad_mlp_part = pl.pallas_call(
        mlp_back_kernel,
        grid=(model_width // WIDE,),
        in_specs=[
            hidden_all,
            hidden_all,
            pl.BlockSpec((WIDE, ff_width), lambda n: (n, 0)),
            pl.BlockSpec((WIDE, ff_width), lambda n: (n, 1)),
        ],
        out_specs=out_tile,
        out_shape=low_shape,
        compiler_params=params(),
        cost_estimate=cost(11),
        name="mlp_back",
    )(grad_gate, grad_up, mlp_weights, mlp_weights)
    grad_mlp_part, mlp_low, hidden_low = lax.optimization_barrier((grad_mlp_part, mlp_low, hidden_low))
    grad_mlp_sum = lax.psum(grad_mlp_part, "mp")

    row_tile = pl.BlockSpec((tok_count, TILE), lambda n: (0, n))
    dw_mlp = pl.pallas_call(
        mlp_weight_grad_kernel,
        grid=(model_width // TILE,),
        in_specs=[row_tile, row_tile, hidden_all, hidden_all, hidden_all],
        out_specs=pl.BlockSpec((TILE, 3 * ff_width), lambda n: (n, 0)),
        out_shape=jax.ShapeDtypeStruct((model_width, 3 * ff_width), bf16),
        compiler_params=params(),
        cost_estimate=cost(1),
        name="mlp_weight_grad",
    )(mlp_low, cotangent, grad_gate, grad_up, hidden_low)
    mlp_part = pl.pallas_call(
        rows_by_rows_kernel,
        grid=(model_width // 512,),
        in_specs=[hidden_all, pl.BlockSpec((512, ff_width), lambda n: (n, 2))],
        out_specs=out_tile,
        out_shape=low_shape,
        compiler_params=params(),
        cost_estimate=cost(1),
        name="mlp_out",
    )(hidden_low, mlp_weights)
    mlp_grads = lax.psum_scatter(dw_mlp, "dp", scatter_dimension=0, tiled=True)
    grad_mlp_sum, mlp_part, dw_mlp = lax.optimization_barrier((grad_mlp_sum, mlp_part, dw_mlp))
    mlp_sum = lax.psum(mlp_part, "mp")

    half_rows = tok_count // 2
    half_spec = pl.BlockSpec((half_rows, model_width), lambda n, *_: (n, 0))
    grad_residual, grad_res_low, grad_att_low, mlp_gain_grad = pl.pallas_call(
        functools.partial(residual_back_kernel, parts, 1.0 / model_count),
        grid_spec=pltpu.PrefetchScalarGridSpec(
            num_scalar_prefetch=1,
            grid=(2,),
            in_specs=[
                half_spec,
                pl.BlockSpec((half_rows, 1), lambda n, *_: (n, 0)),
                half_spec,
                half_spec,
                gain_spec,
            ]
            + [pl.BlockSpec((model_width // parts, query_width), lambda *_: (0, 0))] * parts,
            out_specs=[half_spec, half_spec, pl.BlockSpec((half_rows, query_width), lambda n, *_: (n, 0)), gain_spec],
            scratch_shapes=[pltpu.VMEM((model_width, query_width), bf16)],
        ),
        out_shape=(
            wide_shape,
            low_shape,
            jax.ShapeDtypeStruct((tok_count, query_width), bf16),
            jax.ShapeDtypeStruct((1, model_width), f32),
        ),
        compiler_params=params(),
        cost_estimate=cost(1),
        name="residual_back",
    )(me_array, residual, scale_mlp, cotangent, grad_mlp_sum, gain_mlp[None], *out_parts)
    out_rows = token_total // parts
    dkv_spec = pl.BlockSpec((out_rows, 2 * heads * HD), lambda g, *_: (0, g))
    back = pl.pallas_call(
        functools.partial(attend_back_kernel, group, heads, parts, parts),
        grid_spec=pltpu.PrefetchScalarGridSpec(
            num_scalar_prefetch=3,
            grid=(head_steps,),
            in_specs=[head_spec]
            + [anywhere] * parts
            + [head_spec, turned_spec, lse_spec, head_spec]
            + [angle_spec, angle_spec, pl.BlockSpec((1, HD), lambda *_: (0, 0))],
            out_specs=[head_spec, pl.BlockSpec((8, HD), lambda g, *_: (g, 0))] + [dkv_spec] * parts,
            scratch_shapes=[
                pltpu.VMEM((token_total, 2 * kv_width), bf16),
                pltpu.VMEM((token_total, 2 * heads * HD), f32),
                pltpu.SemaphoreType.DMA((parts,)),
            ],
        ),
        out_shape=[
            jax.ShapeDtypeStruct((tok_count, query_width), bf16),
            jax.ShapeDtypeStruct((8 * head_steps, HD), f32),
        ]
        + [jax.ShapeDtypeStruct((out_rows, 2 * kv_width), bf16)] * parts,
        compiler_params=params(),
        cost_estimate=cost(1),
        name="attend_back",
    )(
        own_spans,
        inverse,
        starts,
        queries,
        *kv_parts,
        grad_att_low,
        attended,
        lse,
        lin,
        cosine,
        sine,
        head_gains[:1],
    )
    grad_query_low, query_gain_grad = back[:2]
    query_gain_grad = jnp.sum(query_gain_grad, axis=0) / 8.0
    if in_pairs:
        came = [swap(back[2 + k], "dp", 1) for k in range(1, parts, 2)]
        halves = [add_pair(back[2 + 2 * k], came[k]) for k in range(parts // 2)]
        halves, mlp_grads = lax.optimization_barrier((halves, mlp_grads))
        terms = [halves[0]] + [swap(halves[k], "dp", 2 * k) for k in range(1, parts // 2)]
    else:
        terms = [lax.psum_scatter(back[2], "dp", scatter_dimension=0, tiled=True)]

    [dw_query] = weight_grad(me_array, normed_turned, [grad_query_low], parts, row_count, True)
    [dw_out] = weight_grad(me_array, grad_res_low, [attended_low], parts, row_count)

    def scattered(made):
        if in_pairs:
            return sum(term.astype(f32) for term in scatter_small(*made)).astype(bf16)
        whole = made[0].reshape(model_width, -1)
        return lax.psum_scatter(whole, "dp", scatter_dimension=0, tiled=True)

    block_output = (residual + mlp_sum.astype(f32)).astype(bf16)
    terms, block_output, dw_query, dw_out = lax.optimization_barrier((terms, block_output, dw_query, dw_out))
    query_grads, out_grads = scattered(dw_query), scattered(dw_out)
    grad_kv_low, key_gain_grad, attn_gain_grad, grad_norm_part = pl.pallas_call(
        functools.partial(key_back_kernel, parts, len(terms), kv_heads),
        grid_spec=pltpu.PrefetchScalarGridSpec(
            num_scalar_prefetch=1,
            grid=(1,),
            in_specs=[pl.BlockSpec((tok_count, 2 * kv_width), lambda *_: (0, 0))] * len(terms)
            + [pl.BlockSpec((tok_count, kv_width), lambda *_: (0, query_width // kv_width))]
            + [angle_spec, angle_spec, pl.BlockSpec((1, HD), lambda *_: (0, 0))]
            + [q_all, rows_all, scale_spec]
            + [pl.BlockSpec((model_width // parts, qkv_cols), lambda *_: (0, 0))] * parts,
            out_specs=[
                pl.BlockSpec((tok_count, 2 * kv_width), lambda *_: (0, 0)),
                pl.BlockSpec((8, HD), lambda *_: (0, 0)),
                gain_spec,
                rows_all,
            ],
        ),
        out_shape=[
            jax.ShapeDtypeStruct((tok_count, 2 * kv_width), bf16),
            jax.ShapeDtypeStruct((8, HD), f32),
            jax.ShapeDtypeStruct((1, model_width), f32),
            low_shape,
        ],
        compiler_params=params(),
        cost_estimate=cost(1),
        name="key_back",
    )(me_array, *terms, lin, cosine, sine, head_gains[1:], grad_query_low, block_input, scale_in, *qkv_parts)
    [dw_kv] = weight_grad(me_array, normed_turned, [grad_kv_low], parts, row_count, True)

    grad_norm_share = lax.psum_scatter(grad_norm_part, "mp", scatter_dimension=0, tiled=True)
    weight_grads = [query_grads, scattered(dw_kv), out_grads, mlp_grads]
    square = sum(jnp.sum(jnp.square(grad.astype(f32))) for grad in weight_grads)
    square, grad_norm_share = lax.optimization_barrier((square, grad_norm_share))
    grad_norm_sum = lax.all_gather(grad_norm_share, "mp", axis=0, tiled=True)
    local = [attn_gain_grad[0], mlp_gain_grad[0], query_gain_grad, key_gain_grad[0]]
    totals = sum_all(jnp.concatenate([jnp.broadcast_to(square, (HD,))] + local))
    square_total, gain_grads = totals[0], totals[HD:]
    grad_norm = jnp.sqrt(square_total + jnp.sum(gain_grads * gain_grads))
    factor = 1.0 / jnp.maximum(grad_norm, 1.0)
    new_weights, new_momentum, new_ema = update_weights(factor[None], weights, momentum, ema_weights, weight_grads)
    grad_input = pl.pallas_call(
        input_back_kernel,
        grid=(2,),
        in_specs=[
            half_spec,
            half_spec,
            pl.BlockSpec((half_rows, 1), lambda n: (n, 0)),
            half_spec,
            gain_spec,
        ],
        out_specs=half_spec,
        out_shape=wide_shape,
        compiler_params=params(),
        cost_estimate=cost(8),
        name="input_back",
    )(grad_residual, block_input, scale_in, grad_norm_sum, gain_attn[None])
    new_gains, new_gain_momentum, new_gain_ema = update(gains, gain_momentum, gain_ema, gain_grads, factor, gain_rate)
    return (
        block_output,
        grad_input,
        grad_norm,
        new_weights,
        new_momentum,
        new_ema,
        new_gains,
        new_gain_momentum,
        new_gain_ema,
    )


def solution(mesh):
    return jax.shard_map(
        per_device,
        mesh=mesh,
        in_specs=(
            P("dp", None),
            P("dp", None),
            P(),
            P(),
            P("dp", "mp"),
            P("dp", "mp"),
            P("dp", "mp"),
            P(),
            P(),
            P(),
        ),
        out_specs=(
            P("dp", None),
            P("dp", None),
            P(),
            P("dp", "mp"),
            P("dp", "mp"),
            P("dp", "mp"),
            P(),
            P(),
            P(),
        ),
        check_vma=False,
    )
```

```python
import functools

import jax
import jax.numpy as jnp
from jax import lax
from jax.experimental import pallas as pl
from jax.experimental.pallas import tpu as pltpu
from jax.sharding import PartitionSpec as P

HEADS = 16
KV = 8
HD = 128
FF = 6144
SPAN = 128
CHUNK = 4
TILE = 256
WIDE = 512
VMEM_LIMIT = 60 * 1024 * 1024

eps_norm = 1e-06
rope_base = 1000000.0
learn_rate = 100.0
gain_rate = 4000.0
momentum_decay = 0.5
average_decay = 0.5
score_scale = HD ** (-0.5)
far = -1e30

bf16 = jnp.bfloat16
f32 = jnp.float32
plain_dims = (((1,), (0,)), ((), ()))
last_dims = (((1,), (1,)), ((), ()))
first_dims = (((0,), (0,)), ((), ()))


def dot(a, b, dims=plain_dims):
    return lax.dot_general(a, b, dims, preferred_element_type=f32)


def cost(micros):
    return pl.CostEstimate(flops=int(micros * 1.0e9), bytes_accessed=int(micros * 3.4e6), transcendentals=0)


def params(**more):
    return pltpu.CompilerParams(vmem_limit_bytes=VMEM_LIMIT, **more)


def swap(array, axis, distance):
    count = lax.axis_size(axis)
    return lax.ppermute(array, axis, [(i, i ^ distance) for i in range(count)])


def gather_chips(own):
    return [own] + [swap(own, "dp", k) for k in (2, 4, 6)]


def gather_cores(outer):
    inner = [swap(block, "dp", 1) for block in outer]
    return [block for pair in zip(outer, inner) for block in pair]


def scatter_small(even, odd):
    came = swap(odd, "dp", 1)
    half = (even.astype(f32) + came.astype(f32)).astype(bf16)
    return [half[0]] + [swap(half[k], "dp", 2 * k) for k in (1, 2, 3)]


def add_pair(a, b):
    return (a.astype(f32) + b.astype(f32)).astype(bf16)


def sum_all(value):
    for axis in ("dp", "mp"):
        distance = 1
        while distance < lax.axis_size(axis):
            value = value + swap(value, axis, distance)
            distance *= 2
    return value


def place_of(me_ref, k, parts):
    return me_ref[0] ^ k if parts > 1 else 0


def in_order(me_ref, part_refs, whole_ref):
    parts = len(part_refs)
    rows = part_refs[0].shape[0]
    for k, ref in enumerate(part_refs):
        at = pl.multiple_of(place_of(me_ref, k, parts) * rows, rows)
        whole_ref[pl.ds(at, rows), :] = ref[...]


def turned(normed, cosine, sine):
    return normed * cosine + pltpu.roll(normed, HD // 2, 1) * sine


def turned_back(gradient, cosine, sine):
    return gradient * cosine + pltpu.roll(gradient * sine, HD // 2, 1)


def unit_scale(values):
    return lax.rsqrt(jnp.mean(values * values, axis=-1, keepdims=True) + eps_norm)


def norm_back(unit, scale, gain, gradient):
    e = gradient * gain
    return scale * (e - unit * jnp.mean(e * unit, axis=-1, keepdims=True))


def project_kernel(parts, q_tiles, me_ref, h_ref, *refs):
    cos_ref, sin_ref, gain_ref, q_ref, kv_ref, lin_ref, w_ref = refs[parts:]
    tile = pl.program_id(0)
    in_order(me_ref, refs[:parts], w_ref)
    total = dot(h_ref[...], w_ref[...])
    per_tile = TILE // HD

    def normed_to(out_ref, gain):
        for part in range(per_tile):
            at = slice(part * HD, (part + 1) * HD)
            values = total[:, at]
            lin_ref[:, at] = values
            normed = values * unit_scale(values) * gain
            out_ref[:, at] = turned(normed, cos_ref[...], sin_ref[...]).astype(bf16)

    @pl.when(tile < q_tiles)
    def _():
        normed_to(q_ref, gain_ref[0:1])

    @pl.when(tile == q_tiles)
    def _():
        normed_to(kv_ref, gain_ref[1:2])

    @pl.when(tile > q_tiles)
    def _():
        kv_ref[...] = total.astype(bf16)


def span_limits(own_ref, starts_ref, i, group):
    span = own_ref[i]
    first = span * SPAN
    lane = lax.broadcasted_iota(jnp.int32, (1, group * SPAN), 1)
    places = first + (lane & (SPAN - 1))
    low = jnp.int32(0)
    begin = jnp.zeros((1, group * SPAN), jnp.int32)
    for d in range(starts_ref.shape[0]):
        start = starts_ref[d]
        low = jnp.maximum(low, jnp.where(start <= first, start, 0))
        begin = jnp.maximum(begin, jnp.where(start <= places, start, 0))
    return span, low // SPAN, places, begin


def key_rows(inverse_ref, newest, b):
    return pl.multiple_of(inverse_ref[jnp.maximum(newest - b, 0)] * SPAN, SPAN)


def allowed_keys(newest, places, begin):
    row = lax.broadcasted_iota(jnp.int32, (CHUNK * SPAN, 1), 0)
    key = newest * SPAN + (row & (SPAN - 1)) - (row & ~(SPAN - 1))
    return (key <= places) & (key >= begin)


def stacked(ref, i, head, group):
    rows = pl.ds(i * SPAN, SPAN)
    return jnp.concatenate([ref[rows, h * HD : (h + 1) * HD] for h in range(head * group, (head + 1) * group)], axis=0)


def head_columns(first, heads, kv_heads):
    keys = [pl.ds(pl.multiple_of((first + h) * HD, HD), HD) for h in range(heads)]
    values = [pl.ds(pl.multiple_of((first + h + kv_heads) * HD, HD), HD) for h in range(heads)]
    return keys, values


def load_parts(part_refs, target_ref, sem_ref, first):
    rows = part_refs[0].shape[0]
    return [
        pltpu.make_async_copy(ref, target_ref.at[pl.ds(k * rows, rows)], sem_ref.at[first + k])
        for k, ref in enumerate(part_refs)
    ]


def attend_kernel(group, heads, parts, own_ref, inverse_ref, starts_ref, q_ref, *refs):
    kv_parts = refs[:parts]
    turned_ref, low_ref, lse_ref, kv_ref, sem_ref = refs[parts:]
    g = pl.program_id(0)
    kv_heads = pl.num_programs(0) * heads
    kv_copies = load_parts(kv_parts, kv_ref, sem_ref, 0)

    @pl.when(g == 0)
    def _():
        for copy in kv_copies:
            copy.start()
        for copy in kv_copies:
            copy.wait()

    key_at, value_at = head_columns(g * heads, heads, kv_heads)
    wide = group * SPAN
    for i in range(own_ref.shape[0]):
        span, low, places, begin = span_limits(own_ref, starts_ref, i, group)
        queries = [stacked(q_ref, i, h, group) for h in range(heads)]
        count = (span - low) // CHUNK + 1

        def step(c, carry):
            newest = span - c * CHUNK
            at = [key_rows(inverse_ref, newest, b) for b in range(CHUNK)]
            allowed = allowed_keys(newest, places, begin)
            made = []
            for h, (top, weight, total) in enumerate(carry):
                keys = jnp.concatenate([kv_ref[pl.ds(a, SPAN), key_at[h]] for a in at], axis=0)
                values = jnp.concatenate([kv_ref[pl.ds(a, SPAN), value_at[h]] for a in at], axis=0)
                scores = jnp.where(allowed, dot(keys, queries[h], last_dims), far)
                new_top = jnp.maximum(top, jnp.max(scores, axis=0, keepdims=True))
                probs = jnp.exp((scores - new_top) * score_scale)
                shrink = jnp.exp((top - new_top) * score_scale)
                weight = weight * shrink + jnp.sum(probs, axis=0, keepdims=True)
                total = total * shrink + dot(values, probs.astype(bf16), first_dims)
                made.append((new_top, weight, total))
            return tuple(made)

        start = (jnp.full((1, wide), far, f32), jnp.zeros((1, wide), f32), jnp.zeros((HD, wide), f32))
        made = lax.fori_loop(0, count, step, (start,) * heads)
        for h, (top, weight, total) in enumerate(made):
            output = total / weight
            place = i * heads + h
            turned_ref[place] = output
            lse_ref[place] = jnp.broadcast_to(top * score_scale + jnp.log(weight), (8, wide))
            back = output.T.astype(bf16)
            for k in range(group):
                column = pl.multiple_of(((g * heads + h) * group + k) * HD, HD)
                low_ref[pl.ds(i * SPAN, SPAN), pl.ds(column, HD)] = back[k * SPAN : (k + 1) * SPAN]


def project_out_kernel(parts, me_ref, low_ref, *refs):
    out_parts = refs[:parts]
    o_ref = refs[parts]
    width = out_parts[0].shape[0]
    block = min(width, TILE)
    for k, w_ref in enumerate(out_parts):
        first = place_of(me_ref, k, parts) * width
        for b in range(width // block):
            at = pl.multiple_of(first + b * block, block)
            term = dot(low_ref[...], w_ref[b * block : (b + 1) * block], last_dims)
            o_ref[:, pl.ds(at, block)] = term.astype(bf16)


def output_first_kernel(y_ref, s_ref, o_ref):
    o_ref[...] = (y_ref[...] + s_ref[...].astype(f32)).astype(bf16)


def output_rest_kernel(y_ref, s_ref, made_ref, o_ref):
    o_ref[...] = (y_ref[...] + s_ref[...].astype(f32)).astype(bf16)


def plain_kernel(a_ref, w_ref, o_ref):
    o_ref[...] = dot(a_ref[...], w_ref[...]).astype(bf16)


def mlp_kernel(x_ref, s_ref, gain_ref, wg_ref, wu_ref, da_ref, y_ref, h_ref, scale_ref, dg_ref, du_ref, a_ref):
    @pl.when(pl.program_id(0) == 0)
    def _():
        def rows_of(r, unused):
            at = pl.ds(pl.multiple_of(r * 64, 64), 64)
            y = x_ref[at, :].astype(f32) + s_ref[at, :].astype(f32)
            y_ref[at, :] = y
            scale = unit_scale(y)
            scale_ref[at, :] = scale
            h_ref[at, :] = (y * scale * gain_ref[...]).astype(bf16)
            return unused

        lax.fori_loop(0, x_ref.shape[0] // 64, rows_of, 0, unroll=2)

    hidden = h_ref[...]
    gate = dot(hidden, wg_ref[...])
    up = dot(hidden, wu_ref[...])
    grad = da_ref[...].astype(f32)
    sig = 1.0 / (1.0 + jnp.exp(-gate))
    silu = gate * sig
    a_ref[...] = (silu * up).astype(bf16)
    dg_ref[...] = (grad * up * (sig + silu * (1.0 - sig))).astype(bf16)
    du_ref[...] = (grad * silu).astype(bf16)


def mlp_back_kernel(dg_ref, du_ref, wg_ref, wu_ref, dh_ref):
    dh_ref[...] = (dot(dg_ref[...], wg_ref[...], last_dims) + dot(du_ref[...], wu_ref[...], last_dims)).astype(bf16)


def rows_by_rows_kernel(a_ref, w_ref, o_ref):
    o_ref[...] = dot(a_ref[...], w_ref[...], last_dims).astype(bf16)


def residual_back_kernel(parts, share, me_ref, y_ref, scale_ref, c_ref, s_ref, gain_ref, *refs):
    dy_ref, low_ref, do_ref, dgain_ref, w_ref = refs[parts:]

    @pl.when(pl.program_id(0) == 0)
    def _():
        dgain_ref[...] = jnp.zeros_like(dgain_ref)
        in_order(me_ref, refs[:parts], w_ref)

    def rows_of(r, dgain):
        at = pl.ds(pl.multiple_of(r * 32, 32), 32)
        scale = scale_ref[at, :]
        unit = y_ref[at, :] * scale
        grad = s_ref[at, :].astype(f32)
        dy = c_ref[at, :].astype(f32) + norm_back(unit, scale, gain_ref[...], grad)
        dy_ref[at, :] = dy
        low_ref[at, :] = dy.astype(bf16)
        return dgain + jnp.sum(grad * unit, axis=0, keepdims=True)

    zeros = jnp.zeros(dgain_ref.shape, f32)
    dgain_ref[...] += share * lax.fori_loop(0, y_ref.shape[0] // 32, rows_of, zeros, unroll=2)
    do_ref[...] = dot(low_ref[...], w_ref[...]).astype(bf16)


def attend_back_kernel(group, heads, parts, outs, own_ref, inverse_ref, starts_ref, q_ref, *refs):
    kv_parts = refs[:parts]
    do_ref, turned_ref, lse_ref, lin_ref, cos_ref, sin_ref, gain_ref = refs[parts : parts + 7]
    dq_ref, dgain_ref = refs[parts + 7 : parts + 9]
    dkv_refs = refs[parts + 9 : parts + 9 + outs]
    kv_ref, acc_ref, sem_ref = refs[parts + 9 + outs :]
    g = pl.program_id(0)
    kv_heads = pl.num_programs(0) * heads
    copies = load_parts(kv_parts, kv_ref, sem_ref, 0)

    @pl.when(g == 0)
    def _():
        for copy in copies:
            copy.start()

    acc_ref[...] = jnp.zeros_like(acc_ref)

    @pl.when(g == 0)
    def _():
        for copy in copies:
            copy.wait()

    key_at, value_at = head_columns(g * heads, heads, kv_heads)
    wide = group * SPAN
    dgain = jnp.zeros((1, HD), f32)
    for i in range(own_ref.shape[0]):
        span, low, places, begin = span_limits(own_ref, starts_ref, i, group)
        queries = [stacked(q_ref, i, h, group) for h in range(heads)]
        grads = [stacked(do_ref, i, h, group) for h in range(heads)]
        deltas = [
            jnp.sum(grads[h].astype(f32).T * turned_ref[i * heads + h], axis=0, keepdims=True) for h in range(heads)
        ]
        lses = [lse_ref[i * heads + h, :1] for h in range(heads)]
        count = (span - low) // CHUNK + 1

        def step(c, carry):
            newest = span - c * CHUNK
            at = [key_rows(inverse_ref, newest, b) for b in range(CHUNK)]
            allowed = allowed_keys(newest, places, begin)
            made = []
            for h, grad_query in enumerate(carry):
                keys = jnp.concatenate([kv_ref[pl.ds(a, SPAN), key_at[h]] for a in at], axis=0)
                values = jnp.concatenate([kv_ref[pl.ds(a, SPAN), value_at[h]] for a in at], axis=0)
                scores = dot(keys, queries[h], last_dims) * score_scale
                probs = jnp.exp(jnp.where(allowed, scores - lses[h], far))
                grad_probs = dot(values, grads[h], last_dims)
                grad_scores = (probs * (grad_probs - deltas[h])).astype(bf16)
                grad_values = dot(probs.astype(bf16), grads[h])
                grad_keys = dot(grad_scores, queries[h]) * score_scale
                left = 2 * h * HD
                for b, a in enumerate(at):
                    rows = slice(b * SPAN, (b + 1) * SPAN)
                    acc_ref[pl.ds(a, SPAN), left : left + HD] += grad_keys[rows]
                    acc_ref[pl.ds(a, SPAN), left + HD : left + 2 * HD] += grad_values[rows]
                made.append(grad_query + dot(keys, grad_scores, first_dims))
            return tuple(made)

        made = lax.fori_loop(0, count, step, (jnp.zeros((HD, wide), f32),) * heads)
        place = pl.ds(i * SPAN, SPAN)
        for h, grad_query in enumerate(made):
            grad_query = (grad_query * score_scale).T
            for k in range(group):
                at = slice((h * group + k) * HD, (h * group + k + 1) * HD)
                back = turned_back(grad_query[k * SPAN : (k + 1) * SPAN], cos_ref[place, :], sin_ref[place, :])
                lin = lin_ref[place, at]
                scale = unit_scale(lin)
                unit = lin * scale
                dgain = dgain + jnp.sum(back * unit, axis=0, keepdims=True)
                dq_ref[place, at] = norm_back(unit, scale, gain_ref[...], back).astype(bf16)
    dgain_ref[...] = jnp.broadcast_to(dgain, dgain_ref.shape)

    rows = acc_ref.shape[0] // parts
    for k in range(parts):
        dkv_refs[k % outs][pl.ds((k // outs) * rows, rows), :] = acc_ref[pl.ds(k * rows, rows), :].astype(bf16)


def key_back_kernel(parts, terms, kv_heads, me_ref, *refs):
    term_refs = refs[:terms]
    lin_ref, cos_ref, sin_ref, gain_ref, dq_ref, x_ref, scale_ref = refs[terms : terms + 7]
    w_refs = refs[terms + 7 : terms + 7 + parts]
    dkv_ref, dgain_k_ref, dgain_ref, dh_ref = refs[terms + 7 + parts :]
    dgain = jnp.zeros((1, HD), f32)

    def total(begin):
        value = None
        for ref in term_refs:
            term = ref[:, begin : begin + HD].astype(f32)
            value = term if value is None else value + term
        return value

    for g in range(kv_heads):
        at = slice(g * HD, (g + 1) * HD)
        back = turned_back(total(2 * g * HD), cos_ref[...], sin_ref[...])
        lin = lin_ref[:, at]
        scale = unit_scale(lin)
        unit = lin * scale
        dgain = dgain + jnp.sum(back * unit, axis=0, keepdims=True)
        dkv_ref[:, at] = norm_back(unit, scale, gain_ref[...], back).astype(bf16)
        dkv_ref[:, (kv_heads + g) * HD : (kv_heads + g + 1) * HD] = total((2 * g + 1) * HD).astype(bf16)
    dgain_k_ref[...] = jnp.broadcast_to(dgain, dgain_k_ref.shape)

    scale = scale_ref[...]
    width = w_refs[0].shape[0]
    block = min(width, TILE)
    q_width = dq_ref.shape[1]
    for k, w_ref in enumerate(w_refs):
        first = place_of(me_ref, k, parts) * width
        for b in range(width // block):
            here = pl.ds(pl.multiple_of(first + b * block, block), block)
            rows = slice(b * block, (b + 1) * block)
            term = dot(dq_ref[...], w_ref[rows, :q_width], last_dims)
            term = term + dot(dkv_ref[...], w_ref[rows, q_width:], last_dims)
            dh_ref[:, here] = term.astype(bf16)
            unit = x_ref[:, here].astype(f32) * scale
            dgain_ref[:, here] = jnp.sum(term * unit, axis=0, keepdims=True)


def input_back_kernel(dy_ref, x_ref, scale_ref, s_ref, gain_ref, o_ref):
    def rows_of(r, unused):
        at = pl.ds(pl.multiple_of(r * 16, 16), 16)
        scale = scale_ref[at, :]
        back = norm_back(x_ref[at, :].astype(f32) * scale, scale, gain_ref[...], s_ref[at, :].astype(f32))
        o_ref[at, :] = dy_ref[at, :] + back
        return unused

    lax.fori_loop(0, x_ref.shape[0] // 16, rows_of, 0, unroll=4)


def transpose_kernel(me_ref, x_ref, o_ref):
    o_ref[...] = x_ref[...].T


def transposed(me, lhs, parts, rows):
    tokens, depth = lhs.shape
    rows = rows if parts > 1 else TILE
    return pl.pallas_call(
        transpose_kernel,
        grid_spec=pltpu.PrefetchScalarGridSpec(
            num_scalar_prefetch=1,
            grid=(depth // rows,),
            in_specs=[pl.BlockSpec((tokens, rows), weight_source(parts, depth // rows))],
            out_specs=pl.BlockSpec((rows, tokens), lambda p, _: (p, 0)),
        ),
        out_shape=jax.ShapeDtypeStruct((depth, tokens), bf16),
        compiler_params=params(),
        cost_estimate=cost(5),
        name="transposed",
    )(me, lhs)


def weight_source(parts, steps):
    half = steps // 2

    def source(p, me_ref):
        return (0, me_ref[0] ^ (2 * (p % half) + p // half)) if parts > 1 else (0, p)

    return source


def weight_grad_kernel(outs, count, me_ref, lhs_ref, *refs):
    rhs_refs = refs[:count]
    out_refs = refs[count:]
    step = pl.program_id(0)
    half = pl.num_programs(0) // outs
    for o in range(outs):

        @pl.when((step >= o * half) & (step < (o + 1) * half))
        def _():
            for rhs_ref, out_ref in zip(rhs_refs, out_refs[o * count : (o + 1) * count]):
                out_ref[0] = dot(lhs_ref[...], rhs_ref[...], first_dims).astype(bf16)


def mlp_weight_grad_kernel(h_ref, c_ref, dg_ref, du_ref, a_ref, o_ref):
    width = a_ref.shape[1]
    for k, (lhs_ref, rhs_ref) in enumerate(((h_ref, dg_ref), (h_ref, du_ref), (c_ref, a_ref))):
        o_ref[:, k * width : (k + 1) * width] = dot(lhs_ref[...], rhs_ref[...], first_dims).astype(bf16)


def weight_grad_turned_kernel(outs, lhs_ref, rhs_ref, *out_refs):
    for o, out_ref in enumerate(out_refs):

        @pl.when(pl.program_id(0) == o)
        def _():
            out_ref[...] = dot(lhs_ref[...], rhs_ref[...]).astype(bf16)


def weight_grad(me, lhs, rhs, parts, rows, is_transposed=False):
    tokens = rhs[0].shape[0]
    depth = lhs.size // tokens
    outs = 2 if parts > 1 else 1
    rows = rows if parts > 1 else TILE
    columns = sum(r.shape[1] for r in rhs)
    if is_transposed:
        half = depth // rows // outs
        made = pl.pallas_call(
            functools.partial(weight_grad_turned_kernel, outs),
            grid=(outs,),
            in_specs=[pl.BlockSpec((depth // outs, tokens), lambda p: (p, 0)), pl.BlockSpec(rhs[0].shape, lambda p: (0, 0))],
            out_specs=[pl.BlockSpec((depth // outs, columns), lambda p: (0, 0))] * outs,
            out_shape=[jax.ShapeDtypeStruct((depth // outs, columns), bf16)] * outs,
            compiler_params=params(),
            cost_estimate=cost(1),
            name="weight_grad_turned",
        )(lhs, rhs[0])
        return [[m.reshape(half, rows, columns) for m in made]]
    steps = depth // rows
    half = steps // outs

    def out_spec(o, width):
        return pl.BlockSpec((1, rows, width), lambda p, _: (jnp.clip(p - o * half, 0, half - 1), 0, 0))

    made = pl.pallas_call(
        functools.partial(weight_grad_kernel, outs, len(rhs)),
        grid_spec=pltpu.PrefetchScalarGridSpec(
            num_scalar_prefetch=1,
            grid=(steps,),
            in_specs=[pl.BlockSpec((tokens, rows), weight_source(parts, steps))]
            + [pl.BlockSpec(r.shape, lambda p, _: (0, 0)) for r in rhs],
            out_specs=[out_spec(o, r.shape[1]) for o in range(outs) for r in rhs],
        ),
        out_shape=[jax.ShapeDtypeStruct((half, rows, r.shape[1]), bf16) for o in range(outs) for r in rhs],
        compiler_params=params(),
        cost_estimate=cost(1),
        name="weight_grad",
    )(me, lhs, *rhs)
    return [made[k :: len(rhs)] for k in range(len(rhs))]


def update_kernel(factor_ref, w_ref, m_ref, e_ref, *refs):
    new_w_ref, new_m_ref, new_e_ref = refs[-3:]
    begin = 0
    for g_ref in refs[:-3]:
        at = slice(begin, begin + g_ref.shape[1])
        made = update(w_ref[:, at], m_ref[:, at], e_ref[:, at], g_ref[...].astype(f32), factor_ref[0], learn_rate)
        new_w_ref[:, at], new_m_ref[:, at], new_e_ref[:, at] = made
        begin += g_ref.shape[1]


def update_weights(factor, weights, momentum, average, pieces):
    rows, columns = weights.shape
    step = 64
    spec = pl.BlockSpec((step, columns), lambda n, _: (n, 0))
    shape = jax.ShapeDtypeStruct(weights.shape, f32)
    return pl.pallas_call(
        update_kernel,
        grid_spec=pltpu.PrefetchScalarGridSpec(
            num_scalar_prefetch=1,
            grid=(rows // step,),
            in_specs=[spec, spec, spec]
            + [pl.BlockSpec((step, piece.shape[1]), lambda n, _: (n, 0)) for piece in pieces],
            out_specs=[spec, spec, spec],
        ),
        out_shape=(shape, shape, shape),
        compiler_params=params(),
        cost_estimate=cost(1),
        name="update",
    )(factor, weights, momentum, average, *pieces)


def update(value, state, average, gradient, factor, step_rate):
    clipped = gradient * factor
    state_new = momentum_decay * state + clipped
    value_new = value - step_rate * (clipped + momentum_decay * state_new)
    average_new = average_decay * average + (1.0 - average_decay) * value_new
    return (value_new, state_new, average_new)


def per_device(
    block_input,
    cotangent,
    doc_lengths,
    span_order,
    weights,
    momentum,
    ema_weights,
    gains,
    gain_momentum,
    gain_ema,
):
    tok_count, model_width = block_input.shape
    data_count = lax.axis_size("dp")
    model_count = lax.axis_size("mp")
    me = lax.axis_index("dp").astype(jnp.int32)
    me_array = me[None]
    row_count = weights.shape[0]
    token_total = tok_count * data_count
    span_total = token_total // SPAN
    span_own = tok_count // SPAN
    seq_len = token_total // doc_lengths.shape[0]
    doc_total = doc_lengths.shape[0] * doc_lengths.shape[1]
    q_heads = HEADS // model_count
    kv_heads = KV // model_count
    group = q_heads // kv_heads
    query_width = q_heads * HD
    kv_width = kv_heads * HD
    ff_width = FF // model_count
    qkv_cols = query_width + 2 * kv_width
    out_end = qkv_cols + query_width
    in_pairs = data_count == 8
    parts = data_count if in_pairs else 1
    outs = 2 if in_pairs else 1
    gain_attn = gains[:model_width]
    gain_mlp = gains[model_width : 2 * model_width]
    head_gains = gains[2 * model_width :].reshape(2, HD)

    qkv_own = weights[:, :qkv_cols].astype(bf16)
    if in_pairs:
        qkv_outer = gather_chips(qkv_own)
        later, qkv_own = lax.optimization_barrier((weights, qkv_own))
        out_outer = gather_chips(later[:, qkv_cols:out_end].astype(bf16))
    else:
        later = weights
        qkv_parts = [lax.all_gather(qkv_own, "dp", axis=0, tiled=True)]
        out_own = weights[:, qkv_cols:out_end].astype(bf16)
        out_parts = [lax.all_gather(out_own, "dp", axis=0, tiled=True)]

    doc_ids = jnp.arange(doc_lengths.shape[1], dtype=jnp.int32)
    earlier = doc_ids[None, :] < doc_ids[:, None]
    starts = jnp.sum(jnp.where(earlier[None], doc_lengths[:, None, :], 0), axis=2)
    starts = starts + seq_len * jnp.arange(doc_lengths.shape[0], dtype=jnp.int32)[:, None]
    starts = starts.reshape(doc_total)
    span_ids = jnp.arange(span_total, dtype=jnp.int32)
    inverse = jnp.sum(jnp.where(span_order[None, :] == span_ids[:, None], span_ids[None, :], 0), axis=1)
    if in_pairs:
        inverse = ((inverse // span_own) ^ me) * span_own + inverse % span_own
    own_spans = lax.dynamic_slice(span_order, (me * span_own,), (span_own,))
    home = (own_spans[:, None] * SPAN + jnp.arange(SPAN, dtype=jnp.int32)[None, :]).reshape(tok_count)
    doc_start = jnp.max(jnp.where(starts[None, :] <= home[:, None], starts[None, :], 0), axis=1)
    freqs = rope_base ** (-(2.0 * (jnp.arange(HD, dtype=jnp.int32) % (HD // 2)).astype(f32)) / HD)
    angles = (home - doc_start).astype(f32)[:, None] * freqs[None, :]
    cosine = jnp.cos(angles)
    sine = jnp.sin(angles) * jnp.where(jnp.arange(HD) < HD // 2, -1.0, 1.0)[None, :]

    inputs = block_input.astype(f32)
    scale_in = unit_scale(inputs)
    normed_low = (inputs * scale_in * gain_attn).astype(bf16)

    normed_turned = transposed(me_array, normed_low, parts, row_count)
    if in_pairs:
        normed_turned, qkv_outer[1] = lax.optimization_barrier((normed_turned, qkv_outer[1]))
        qkv_parts = gather_cores(qkv_outer)

    q_tiles = query_width // TILE
    rows_all = pl.BlockSpec((tok_count, model_width), lambda *_: (0, 0))
    angle_spec = pl.BlockSpec((tok_count, HD), lambda *_: (0, 0))
    part_tile = pl.BlockSpec((model_width // parts, TILE), lambda n, *_: (0, n))
    queries, keys_values, lin = pl.pallas_call(
        functools.partial(project_kernel, parts, q_tiles),
        grid_spec=pltpu.PrefetchScalarGridSpec(
            num_scalar_prefetch=1,
            grid=(qkv_cols // TILE,),
            in_specs=[rows_all]
            + [part_tile] * parts
            + [angle_spec, angle_spec, pl.BlockSpec((2, HD), lambda *_: (0, 0))],
            out_specs=[
                pl.BlockSpec((tok_count, TILE), lambda n, *_: (0, jnp.minimum(n, q_tiles - 1))),
                pl.BlockSpec((tok_count, TILE), lambda n, *_: (0, jnp.maximum(n - q_tiles, 0))),
                pl.BlockSpec((tok_count, TILE), lambda n, *_: (0, jnp.minimum(n, q_tiles))),
            ],
            scratch_shapes=[pltpu.VMEM((model_width, TILE), bf16)],
        ),
        out_shape=(
            jax.ShapeDtypeStruct((tok_count, query_width), bf16),
            jax.ShapeDtypeStruct((tok_count, 2 * kv_width), bf16),
            jax.ShapeDtypeStruct((tok_count, query_width + kv_width), f32),
        ),
        compiler_params=params(),
        cost_estimate=cost(6),
        name="project",
    )(me_array, normed_low, *qkv_parts, cosine, sine, head_gains)

    mlp_own = later[:, out_end:].astype(bf16)
    if in_pairs:
        keys_values, out_outer = lax.optimization_barrier((keys_values, out_outer))
        kv_parts = gather_cores(gather_chips(keys_values))
        out_parts = gather_cores(out_outer)
        mlp_own, out_parts, kv_parts = lax.optimization_barrier((mlp_own, out_parts, kv_parts))
    else:
        kv_parts = [lax.all_gather(keys_values, "dp", axis=0, tiled=True)]
    mlp_weights = lax.all_gather(mlp_own, "dp", axis=0, tiled=True)

    heads = kv_heads if in_pairs else 1
    head_steps = kv_heads // heads
    wide = group * SPAN
    anywhere = pl.BlockSpec(memory_space=pl.ANY)
    head_spec = pl.BlockSpec((tok_count, heads * group * HD), lambda g, *_: (0, g))
    q_all = pl.BlockSpec((tok_count, query_width), lambda *_: (0, 0))
    turned_spec = pl.BlockSpec((span_own * heads, HD, wide), lambda g, *_: (g, 0, 0))
    lse_spec = pl.BlockSpec((span_own * heads, 8, wide), lambda g, *_: (g, 0, 0))
    attended, attended_low, lse = pl.pallas_call(
        functools.partial(attend_kernel, group, heads, parts),
        grid_spec=pltpu.PrefetchScalarGridSpec(
            num_scalar_prefetch=3,
            grid=(head_steps,),
            in_specs=[head_spec] + [anywhere] * parts,
            out_specs=[turned_spec, q_all, lse_spec],
            scratch_shapes=[
                pltpu.VMEM((token_total, 2 * kv_width), bf16),
                pltpu.SemaphoreType.DMA((parts,)),
            ],
        ),
        out_shape=(
            jax.ShapeDtypeStruct((span_own * kv_heads, HD, wide), f32),
            jax.ShapeDtypeStruct((tok_count, query_width), bf16),
            jax.ShapeDtypeStruct((span_own * kv_heads, 8, wide), f32),
        ),
        compiler_params=params(),
        cost_estimate=cost(16),
        name="attend",
    )(own_spans, inverse, starts, queries, *kv_parts)
    part_all = pl.BlockSpec((model_width // parts, query_width), lambda *_: (0, 0))
    attn_part = pl.pallas_call(
        functools.partial(project_out_kernel, parts),
        grid_spec=pltpu.PrefetchScalarGridSpec(
            num_scalar_prefetch=1,
            grid=(1,),
            in_specs=[q_all] + [part_all] * parts,
            out_specs=rows_all,
        ),
        out_shape=jax.ShapeDtypeStruct((tok_count, model_width), bf16),
        compiler_params=params(),
        cost_estimate=cost(4),
        name="project_out",
    )(me_array, attended_low, *out_parts)

    attn_sum = lax.psum(attn_part, "mp")

    tiles = ff_width // TILE
    gain_spec = pl.BlockSpec((1, model_width), lambda *_: (0, 0))
    tile_spec = pl.BlockSpec((tok_count, TILE), lambda n: (0, n))
    hidden_shape = jax.ShapeDtypeStruct((tok_count, ff_width), bf16)
    low_shape = jax.ShapeDtypeStruct((tok_count, model_width), bf16)
    wide_shape = jax.ShapeDtypeStruct((tok_count, model_width), f32)
    scale_spec = pl.BlockSpec((tok_count, 1), lambda *_: (0, 0))
    scale_shape = jax.ShapeDtypeStruct((tok_count, 1), f32)
    grad_hidden = pl.pallas_call(
        plain_kernel,
        grid=(tiles,),
        in_specs=[rows_all, pl.BlockSpec((model_width, TILE), lambda n: (0, n + 2 * tiles))],
        out_specs=tile_spec,
        out_shape=hidden_shape,
        compiler_params=params(),
        cost_estimate=cost(30),
        name="grad_hidden",
    )(cotangent, mlp_weights)
    residual, mlp_low, scale_mlp, grad_gate, grad_up, hidden_low = pl.pallas_call(
        mlp_kernel,
        grid=(tiles,),
        in_specs=[
            rows_all,
            rows_all,
            gain_spec,
            pl.BlockSpec((model_width, TILE), lambda n: (0, n)),
            pl.BlockSpec((model_width, TILE), lambda n: (0, n + tiles)),
            tile_spec,
        ],
        out_specs=[rows_all, rows_all, scale_spec, tile_spec, tile_spec, tile_spec],
        out_shape=(wide_shape, low_shape, scale_shape, hidden_shape, hidden_shape, hidden_shape),
        compiler_params=params(),
        cost_estimate=cost(18),
        name="mlp",
    )(block_input, attn_sum, gain_mlp[None], mlp_weights, mlp_weights, grad_hidden)

    hidden_all = pl.BlockSpec((tok_count, ff_width), lambda n: (0, 0))
    out_tile = pl.BlockSpec((tok_count, 512), lambda n: (0, n))
    grad_mlp_part = pl.pallas_call(
        mlp_back_kernel,
        grid=(model_width // WIDE,),
        in_specs=[
            hidden_all,
            hidden_all,
            pl.BlockSpec((WIDE, ff_width), lambda n: (n, 0)),
            pl.BlockSpec((WIDE, ff_width), lambda n: (n, 1)),
        ],
        out_specs=out_tile,
        out_shape=low_shape,
        compiler_params=params(),
        cost_estimate=cost(11),
        name="mlp_back",
    )(grad_gate, grad_up, mlp_weights, mlp_weights)
    grad_mlp_part, mlp_low, hidden_low = lax.optimization_barrier((grad_mlp_part, mlp_low, hidden_low))
    grad_mlp_sum = lax.psum(grad_mlp_part, "mp")

    row_tile = pl.BlockSpec((tok_count, TILE), lambda n: (0, n))
    dw_mlp = pl.pallas_call(
        mlp_weight_grad_kernel,
        grid=(model_width // TILE,),
        in_specs=[row_tile, row_tile, hidden_all, hidden_all, hidden_all],
        out_specs=pl.BlockSpec((TILE, 3 * ff_width), lambda n: (n, 0)),
        out_shape=jax.ShapeDtypeStruct((model_width, 3 * ff_width), bf16),
        compiler_params=params(),
        cost_estimate=cost(1),
        name="mlp_weight_grad",
    )(mlp_low, cotangent, grad_gate, grad_up, hidden_low)
    mlp_part = pl.pallas_call(
        rows_by_rows_kernel,
        grid=(model_width // 512,),
        in_specs=[hidden_all, pl.BlockSpec((512, ff_width), lambda n: (n, 2))],
        out_specs=out_tile,
        out_shape=low_shape,
        compiler_params=params(),
        cost_estimate=cost(1),
        name="mlp_out",
    )(hidden_low, mlp_weights)
    mlp_grads = lax.psum_scatter(dw_mlp, "dp", scatter_dimension=0, tiled=True)
    grad_mlp_sum, mlp_part, dw_mlp = lax.optimization_barrier((grad_mlp_sum, mlp_part, dw_mlp))
    mlp_sum = lax.psum(mlp_part, "mp")

    half_rows = tok_count // 2
    half_spec = pl.BlockSpec((half_rows, model_width), lambda n, *_: (n, 0))
    grad_residual, grad_res_low, grad_att_low, mlp_gain_grad = pl.pallas_call(
        functools.partial(residual_back_kernel, parts, 1.0 / model_count),
        grid_spec=pltpu.PrefetchScalarGridSpec(
            num_scalar_prefetch=1,
            grid=(2,),
            in_specs=[
                half_spec,
                pl.BlockSpec((half_rows, 1), lambda n, *_: (n, 0)),
                half_spec,
                half_spec,
                gain_spec,
            ]
            + [pl.BlockSpec((model_width // parts, query_width), lambda *_: (0, 0))] * parts,
            out_specs=[half_spec, half_spec, pl.BlockSpec((half_rows, query_width), lambda n, *_: (n, 0)), gain_spec],
            scratch_shapes=[pltpu.VMEM((model_width, query_width), bf16)],
        ),
        out_shape=(
            wide_shape,
            low_shape,
            jax.ShapeDtypeStruct((tok_count, query_width), bf16),
            jax.ShapeDtypeStruct((1, model_width), f32),
        ),
        compiler_params=params(),
        cost_estimate=cost(1),
        name="residual_back",
    )(me_array, residual, scale_mlp, cotangent, grad_mlp_sum, gain_mlp[None], *out_parts)
    out_rows = token_total // parts
    dkv_spec = pl.BlockSpec((out_rows, 2 * heads * HD), lambda g, *_: (0, g))
    back = pl.pallas_call(
        functools.partial(attend_back_kernel, group, heads, parts, parts),
        grid_spec=pltpu.PrefetchScalarGridSpec(
            num_scalar_prefetch=3,
            grid=(head_steps,),
            in_specs=[head_spec]
            + [anywhere] * parts
            + [head_spec, turned_spec, lse_spec, head_spec]
            + [angle_spec, angle_spec, pl.BlockSpec((1, HD), lambda *_: (0, 0))],
            out_specs=[head_spec, pl.BlockSpec((8, HD), lambda g, *_: (g, 0))] + [dkv_spec] * parts,
            scratch_shapes=[
                pltpu.VMEM((token_total, 2 * kv_width), bf16),
                pltpu.VMEM((token_total, 2 * heads * HD), f32),
                pltpu.SemaphoreType.DMA((parts,)),
            ],
        ),
        out_shape=[
            jax.ShapeDtypeStruct((tok_count, query_width), bf16),
            jax.ShapeDtypeStruct((8 * head_steps, HD), f32),
        ]
        + [jax.ShapeDtypeStruct((out_rows, 2 * kv_width), bf16)] * parts,
        compiler_params=params(),
        cost_estimate=cost(1),
        name="attend_back",
    )(
        own_spans,
        inverse,
        starts,
        queries,
        *kv_parts,
        grad_att_low,
        attended,
        lse,
        lin,
        cosine,
        sine,
        head_gains[:1],
    )
    grad_query_low, query_gain_grad = back[:2]
    query_gain_grad = jnp.sum(query_gain_grad, axis=0) / 8.0
    if in_pairs:
        came = [swap(back[2 + k], "dp", 1) for k in range(1, parts, 2)]
        halves = [add_pair(back[2 + 2 * k], came[k]) for k in range(parts // 2)]
        halves, mlp_grads = lax.optimization_barrier((halves, mlp_grads))
        terms = [halves[0]] + [swap(halves[k], "dp", 2 * k) for k in range(1, parts // 2)]
    else:
        terms = [lax.psum_scatter(back[2], "dp", scatter_dimension=0, tiled=True)]

    [dw_query] = weight_grad(me_array, normed_turned, [grad_query_low], parts, row_count, True)
    [dw_out] = weight_grad(me_array, grad_res_low, [attended_low], parts, row_count)

    def scattered(made):
        if in_pairs:
            return sum(term.astype(f32) for term in scatter_small(*made)).astype(bf16)
        whole = made[0].reshape(model_width, -1)
        return lax.psum_scatter(whole, "dp", scatter_dimension=0, tiled=True)

    first_spec = pl.BlockSpec((tok_count // 8, model_width), lambda n: (0, 0))
    block_output = pl.pallas_call(
        output_first_kernel,
        grid=(1,),
        in_specs=[first_spec, first_spec],
        out_specs=first_spec,
        out_shape=low_shape,
        compiler_params=params(),
        cost_estimate=cost(6),
        name="output_first",
    )(residual, mlp_sum)
    terms, block_output, dw_query, dw_out = lax.optimization_barrier((terms, block_output, dw_query, dw_out))
    query_grads, out_grads = scattered(dw_query), scattered(dw_out)
    grad_kv_low, key_gain_grad, attn_gain_grad, grad_norm_part = pl.pallas_call(
        functools.partial(key_back_kernel, parts, len(terms), kv_heads),
        grid_spec=pltpu.PrefetchScalarGridSpec(
            num_scalar_prefetch=1,
            grid=(1,),
            in_specs=[pl.BlockSpec((tok_count, 2 * kv_width), lambda *_: (0, 0))] * len(terms)
            + [pl.BlockSpec((tok_count, kv_width), lambda *_: (0, query_width // kv_width))]
            + [angle_spec, angle_spec, pl.BlockSpec((1, HD), lambda *_: (0, 0))]
            + [q_all, rows_all, scale_spec]
            + [pl.BlockSpec((model_width // parts, qkv_cols), lambda *_: (0, 0))] * parts,
            out_specs=[
                pl.BlockSpec((tok_count, 2 * kv_width), lambda *_: (0, 0)),
                pl.BlockSpec((8, HD), lambda *_: (0, 0)),
                gain_spec,
                rows_all,
            ],
        ),
        out_shape=[
            jax.ShapeDtypeStruct((tok_count, 2 * kv_width), bf16),
            jax.ShapeDtypeStruct((8, HD), f32),
            jax.ShapeDtypeStruct((1, model_width), f32),
            low_shape,
        ],
        compiler_params=params(),
        cost_estimate=cost(1),
        name="key_back",
    )(me_array, *terms, lin, cosine, sine, head_gains[1:], grad_query_low, block_input, scale_in, *qkv_parts)
    [dw_kv] = weight_grad(me_array, normed_turned, [grad_kv_low], parts, row_count, True)

    grad_norm_share = lax.psum_scatter(grad_norm_part, "mp", scatter_dimension=0, tiled=True)
    mlp_sum, block_output, keys_done = lax.optimization_barrier((mlp_sum, block_output, grad_kv_low))
    rest_spec = pl.BlockSpec((tok_count // 8, model_width), lambda n: (n + 1, 0))
    block_output = pl.pallas_call(
        output_rest_kernel,
        grid=(7,),
        in_specs=[rest_spec, rest_spec, anywhere],
        out_specs=rest_spec,
        out_shape=low_shape,
        input_output_aliases={2: 0},
        compiler_params=params(),
        cost_estimate=cost(5),
        name="output_rest",
    )(residual, mlp_sum, block_output)
    weight_grads = [query_grads, scattered(dw_kv), out_grads, mlp_grads]
    square = sum(jnp.sum(jnp.square(grad.astype(f32))) for grad in weight_grads)
    square, grad_norm_share, block_output = lax.optimization_barrier((square, grad_norm_share, block_output))
    grad_norm_sum = lax.all_gather(grad_norm_share, "mp", axis=0, tiled=True)
    local = [attn_gain_grad[0], mlp_gain_grad[0], query_gain_grad, key_gain_grad[0]]
    totals = sum_all(jnp.concatenate([jnp.broadcast_to(square, (HD,))] + local))
    square_total, gain_grads = totals[0], totals[HD:]
    grad_norm = jnp.sqrt(square_total + jnp.sum(gain_grads * gain_grads))
    factor = 1.0 / jnp.maximum(grad_norm, 1.0)
    new_weights, new_momentum, new_ema = update_weights(factor[None], weights, momentum, ema_weights, weight_grads)
    grad_input = pl.pallas_call(
        input_back_kernel,
        grid=(2,),
        in_specs=[
            half_spec,
            half_spec,
            pl.BlockSpec((half_rows, 1), lambda n: (n, 0)),
            half_spec,
            gain_spec,
        ],
        out_specs=half_spec,
        out_shape=wide_shape,
        compiler_params=params(),
        cost_estimate=cost(8),
        name="input_back",
    )(grad_residual, block_input, scale_in, grad_norm_sum, gain_attn[None])
    new_gains, new_gain_momentum, new_gain_ema = update(gains, gain_momentum, gain_ema, gain_grads, factor, gain_rate)
    return (
        block_output,
        grad_input,
        grad_norm,
        new_weights,
        new_momentum,
        new_ema,
        new_gains,
        new_gain_momentum,
        new_gain_ema,
    )


def solution(mesh):
    return jax.shard_map(
        per_device,
        mesh=mesh,
        in_specs=(
            P("dp", None),
            P("dp", None),
            P(),
            P(),
            P("dp", "mp"),
            P("dp", "mp"),
            P("dp", "mp"),
            P(),
            P(),
            P(),
        ),
        out_specs=(
            P("dp", None),
            P("dp", None),
            P(),
            P("dp", "mp"),
            P("dp", "mp"),
            P("dp", "mp"),
            P(),
            P(),
            P(),
        ),
        check_vma=False,
    )
```
